512 devices in a mesh: tests: 16 (over z, y_hi), grid: 32 (over x, y_lo, core).
Axes of the slice: x: 4, y: 8 (y_hi: 2, y_lo: 4; y = y_hi * 4 + y_lo), z: 8, core: 2. Of those that a mesh axis runs over, the one named last changes fastest.
Arguments:
- log_cond: float32 [64, 128, 128], P('grid'), may hold values from -0.7 to 0.7
- opening_increase: float32 [16, 64, 128, 128], P('tests', 'grid'), may hold values from -6 to 6
- heat_load: float32 [16, 64, 128, 128], P('tests', 'grid'), may hold values from -6 to 6
- measured: float32 [16, 128], P('tests', 'grid'), may hold values from -12 to 12
- duct_cells: int32 [8192, 8], P('grid'), may hold values from 0 to 32767
- duct_segment: int32 [8192, 1], P('grid'), may hold values from 0 to 127; in each aligned block of 256 rows (0 to 255, 256 to 511, ...) at most 4 rows name the same one
Outputs:
- theta_grad: float32 [64, 128, 128], P('grid', 'tests')
- seg_residual: float32 [16, 128], P('tests', 'grid')
The draws below stay inside these ranges and needn't reach their ends.
Inputs may be any that keep to these rules, and one draw needn't show every extreme that they name: `duct_cells`: row r is a flat index (first dimension slowest) into the 2 x 128 x 128 cells of slab r // 256. `duct_segment`: in each aligned block of 256 rows (the ducts of one slab) no segment is named more than 4 times, a bound that some block reaches.
All inputs are finite; a program needn't handle non-finite values.
Results may differ from the reference program's by a relative error of at most 0.000022.
Values sent between devices are 32-bit elements; how exact they have to be, the bound alone decides.
No kernel may reach another device: no remote copies, remote signals or barrier semaphores. Data moves between devices by JAX's collectives and lax.ppermute only.
A program may use at most 64 MiB of HBM per device.

```python
import math
import jax
import jax.numpy as jnp
import numpy as np
from jax import lax

CX = 2
NY = 128
NZ = 128
STEPS = 4
DUCT_DEV = 256
LIST = 8
TESTS = 16
NX = 64
SEGMENTS = 128
DUCTS = 8192
CAP = 4


def set_ends(result, own_key, smallest, largest):
    dims = result.shape
    spot = [jax.random.randint(jax.random.fold_in(own_key, axis), (), 0, dims[axis]) for axis in range(len(dims))]
    result = result.at[tuple(spot)].set(smallest)
    longest = dims.index(max(dims))
    spot[longest] = (spot[longest] + 1) % dims[longest]
    return result.at[tuple(spot)].set(largest)


def block_scale(own_key, dims, shards, low, high):
    level, own = 1.0, jax.random.fold_in(own_key, 6)
    for dim, shards_of in shards:
        draws = jnp.exp(jax.random.uniform(jax.random.fold_in(own, dim), (shards_of,), jnp.float32, low / len(shards), high / len(shards)))
        level = level * jnp.repeat(draws, dims[dim] // shards_of).reshape([-1 if axis == dim else 1 for axis in range(len(dims))])
    return level


def assign_block(key, own, number, rows, count, top, reach, skew):
    sequence = jax.random.permutation(key, count)
    crowded, usual = portions_of(count, rows * top, reach, skew, True), portions_of(count, rows * top, reach, skew, False)
    places = jnp.arange(count)

    def named(tallies, offset_by):
        used = int((tallies > 0).sum())
        fixed = max(1, used // 4)
        shifted = fixed + (places - fixed + offset_by * (used - fixed)) % max(1, count - fixed)
        return jnp.zeros((count,), jnp.int32).at[sequence[jnp.where(places < fixed, places, shifted)]].set(jnp.asarray(tallies, jnp.int32))

    tallies = jnp.where(number % 4 == 0, named(crowded, number // 4), named(usual, number - number // 4 - 1))
    mixed = jax.random.permutation(jax.random.fold_in(own, 3), count)
    source_of, taker = mixed[0:count // 2 * 2:2], mixed[1:count // 2 * 2:2]
    room = jnp.minimum(tallies[source_of] - 1, reach - tallies[taker]) // 2
    room = jnp.where((source_of == sequence[0]) | (taker == sequence[0]) | (tallies[taker] == 0), 0, jnp.maximum(room, 0))
    shifted = jax.random.randint(jax.random.fold_in(own, 4), (count // 2,), 0, 1 << 20) % (room + 1)
    tallies = tallies.at[source_of].add(-shifted).at[taker].add(shifted)
    items = jnp.searchsorted(jnp.cumsum(tallies), jnp.arange(rows * top), side="right").astype(jnp.int32)
    grid = items.reshape(top, rows).T
    grid = grid[jax.random.permutation(jax.random.fold_in(own, 1), rows)]
    offset_by = jax.random.randint(jax.random.fold_in(own, 2), (rows, 1), 0, top)
    return jnp.take_along_axis(grid, (jnp.arange(top)[None, :] + offset_by) % top, axis=1)


def portions_of(amount, total, reach, lean, full):
    loads = [(1 << 20) // math.isqrt(standing ** lean) + 1 for standing in range(1, amount + 1)]
    largest = reach if full else min(reach, max(-(-total // amount), total * loads[0] // sum(loads)))
    least = 1 if total - largest >= amount - 1 else 0
    counts, surplus = [largest] + [least] * (amount - 1), total - largest - least * (amount - 1)
    while surplus > 0:
        candidates = [i for i in range(1, amount) if counts[i] < largest] or [i for i in range(1, amount) if counts[i] < reach]
        whole, remaining = sum([loads[i] for i in candidates]), surplus
        for i in candidates:
            more = min(reach - counts[i], max(1, remaining * loads[i] // whole), surplus)
            counts[i] = counts[i] + more
            surplus = surplus - more
    return np.array(counts)


def gaussian(rng, shape, scale, most, cuts=(), kind=jnp.bfloat16):
    result = jax.random.normal(rng, shape, jnp.float32) * scale
    if len(cuts) > 0:
        result = block_scale(rng, shape, cuts, -0.22, 0.18) * result
    return jnp.clip(result, min=-most, max=most).astype(kind)


def setup_inputs(seed: int = 0) -> dict:
    keys = jax.random.split(jax.random.key(seed), 7)
    log_cond = jnp.clip(jax.random.uniform(keys[0], (NX, NY, NZ), jnp.float32, -0.7, 0.7) * block_scale(keys[0], (NX, NY, NZ), ((0, 32),), -0.4, 0.0), -0.7, 0.7)
    opening_increase = gaussian(keys[1], (TESTS, NX, NY, NZ), 1.0, 6.0, ((0, 16), (1, 32)), jnp.float32)
    heat_load = gaussian(keys[2], (TESTS, NX, NY, NZ), 1.0, 6.0, ((0, 16), (1, 32)), jnp.float32)
    measured = gaussian(keys[3], (TESTS, SEGMENTS), 3.0, 12.0, ((0, 16), (1, 32)), jnp.float32)
    duct_cells = set_ends(jax.random.randint(keys[4], (DUCTS, LIST), 0, CX * NY * NZ), jax.random.fold_in(keys[4], 1), 0, (CX * NY * NZ) - 1).astype(jnp.int32)
    duct_segment_keys = jax.random.split(jax.random.fold_in(keys[5], 1), DUCTS // DUCT_DEV)
    duct_segment_turns = jax.random.permutation(jax.random.fold_in(keys[5], 3), DUCTS // DUCT_DEV)
    duct_segment = jax.vmap(lambda own, number: assign_block(jax.random.fold_in(keys[5], 2), own, number, DUCT_DEV, SEGMENTS, 1, CAP, 2))(duct_segment_keys, duct_segment_turns).reshape((DUCTS, 1))
    return dict(log_cond=log_cond, opening_increase=opening_increase, heat_load=heat_load, measured=measured, duct_cells=duct_cells, duct_segment=duct_segment)


timelapse_width = 0.08
boundary_factor = 0.5
axis_weights = (1.0, 1.0, 1.0, 1.0, 0.5, 0.5)

def adjacent_entries(extended_profile):
    middle_entry = extended_profile[1:-1, 1:-1, 1:-1]
    remaining_entries = [extended_profile[2:, 1:-1, 1:-1], extended_profile[:-2, 1:-1, 1:-1], extended_profile[1:-1, 2:, 1:-1], extended_profile[1:-1, :-2, 1:-1], extended_profile[1:-1, 1:-1, 2:], extended_profile[1:-1, 1:-1, :-2]]
    return (middle_entry, remaining_entries)

def spreading_matrix(thermal_profile, thermal_permeance):
    middle_entry, remaining_entries = adjacent_entries(jnp.pad(thermal_profile, 1))
    unused, cond_others = adjacent_entries(jnp.pad(thermal_permeance, 1))
    accumulated_amount = jnp.zeros_like(thermal_profile)
    for weight, other, other_cond in zip(axis_weights, remaining_entries, cond_others):
        accumulated_amount = accumulated_amount + weight * 0.5 * (thermal_permeance + other_cond) * (other - middle_entry)
    return accumulated_amount

def test_loss(log_cond, opening_position, power_injection, target, whole_domain_nodes, segment_ids):
    thermal_permeance = jnp.exp(log_cond)
    thermal_profile = opening_position
    for sweep in range(STEPS):
        thermal_profile = thermal_profile + timelapse_width * (spreading_matrix(thermal_profile, thermal_permeance) + power_injection)
    interim_outcome = boundary_factor * lax.optimization_barrier(jnp.sum(thermal_profile.reshape(-1)[whole_domain_nodes], axis=1))
    totals = jax.ops.segment_sum(interim_outcome, segment_ids, num_segments=SEGMENTS)
    resid = totals - target
    return (0.5 * jnp.sum(resid * resid), resid)

def reference(log_cond, opening_increase, heat_load, measured, duct_cells, duct_segment):
    offsets = jnp.arange(DUCTS, dtype=jnp.int32) // DUCT_DEV * (CX * NY * NZ)
    whole_domain_nodes = (duct_cells + offsets[:, None]).astype(jnp.int32)
    segment_ids = duct_segment[:, 0]
    grad_fn = jax.grad(test_loss, argnums=0, has_aux=True)

    def one_test(carry, inputs):
        opening_position, power_injection, target = inputs
        grads, resid = grad_fn(log_cond, opening_position, power_injection, target, whole_domain_nodes, segment_ids)
        return (carry + grads, resid)
    accumulated_amount, resids = lax.scan(one_test, jnp.zeros_like(log_cond), (opening_increase, heat_load, measured))
    return (accumulated_amount, resids)
```

```python
import functools

import jax
import jax.numpy as jnp
from jax import lax
from jax.experimental import pallas as pl
from jax.experimental.pallas import tpu as pltpu
from jax.sharding import PartitionSpec as P

STEPS = 4
DT = 0.08
WX = 0.5 * DT
WZ = 0.25 * DT
NY = 128
NZ = 128
CELLS = 2 * NY
EXT = 10
PAD = 8
YP = NY + 2 * PAD
MID = slice(PAD, PAD + NY)
CH = 32
PACK = 3 * CELLS + 24
bf16 = jnp.bfloat16
f32 = jnp.float32


def position():
    g = lax.axis_index("grid")
    return g, lax.rem(g, 2), lax.div(g, 2), lax.axis_size("grid") // 2


def validity():
    _, core, chip, chips = position()
    low, high = (chip > 0).astype(f32), (chip < chips - 1).astype(f32)
    near = jnp.where(core == 0, low, high)
    far = jnp.where(core == 0, high, low)
    return near, far


def row_validity(i, near, far):
    return jnp.where(i < 4, near, jnp.where(i < 8, 1.0, far))


def lane_masks(rows):
    lane = lax.broadcasted_iota(jnp.int32, (rows, NZ), 1)
    return lane < NZ - 1, lane > 0


def ahead_z(values, keep):
    return jnp.where(keep, pltpu.roll(values, NZ - 1, 1), 0.0)


def behind_z(values, keep):
    return jnp.where(keep, pltpu.roll(values, 1, 1), 0.0)


def zero_pads(ref, lead):
    ref[lead, 0:PAD] = jnp.zeros((PAD, NZ), f32)
    ref[lead, PAD + NY : YP] = jnp.zeros((PAD, NZ), f32)


def coefficients(cond, kx, ky, kzp, kzm, keep):
    ahead_keep, behind_keep = lane_masks(CH)

    def row(i, carry):
        for y in range(0, NY, CH):
            here = pl.ds(PAD + y, CH)
            c = cond[i, here]
            cxp, cxm = cond[i + 1, here], cond[i - 1, here]
            cyp, cym = cond[i, pl.ds(PAD + y + 1, CH)], cond[i, pl.ds(PAD + y - 1, CH)]
            czp, czm = ahead_z(c, ahead_keep), behind_z(c, behind_keep)
            kx[i, pl.ds(y, CH)] = WX * (c + cxp)
            face_y = WX * (c + cyp)
            if y + CH == NY:
                edge = lax.broadcasted_iota(jnp.int32, (CH, NZ), 0) == CH - 1
                face_y = jnp.where(edge, 0.0, face_y)
            ky[i, here] = face_y
            kzp[i, pl.ds(y, CH)] = jnp.where(ahead_keep, WZ * (c + czp), 0.0)
            kzm[i, pl.ds(y, CH)] = jnp.where(behind_keep, WZ * (c + czm), 0.0)
            total = WX * (((cxp + cxm) + (cyp + cym)) + 4.0 * c) + WZ * ((czp + czm) + 2.0 * c)
            keep[i, pl.ds(y, CH)] = 1.0 - total
        ky[i, 0:PAD] = jnp.zeros((PAD, NZ), f32)
        return carry

    kx[0] = WX * (cond[0, MID] + cond[1, MID])
    lax.fori_loop(1, 9, row, 0)


def advance(src, dst, first, last, coefs, load, near, far):
    kx, ky, kzp, kzm, keep = coefs

    def row(i, carry):
        inside = row_validity(i, near, far)
        for y in range(0, NY, CH):
            here, flat = pl.ds(PAD + y, CH), pl.ds(y, CH)
            u = src[i, here]
            new = keep[i, flat] * u
            new += kx[i, flat] * src[i + 1, here]
            new += kx[i - 1, flat] * src[i - 1, here]
            new += ky[i, here] * src[i, pl.ds(PAD + y + 1, CH)]
            new += ky[i, pl.ds(PAD + y - 1, CH)] * src[i, pl.ds(PAD + y - 1, CH)]
            new += kzp[i, flat] * pltpu.roll(u, NZ - 1, 1)
            new += kzm[i, flat] * pltpu.roll(u, 1, 1)
            if load is not None:
                new += load[i, flat]
            dst[i, here] = new * inside
        return carry

    lax.fori_loop(first, last + 1, row, 0)


def parts_of(values, count):
    parts = []
    for _ in range(count):
        part = values.astype(bf16).astype(f32)
        parts.append(part)
        values = values - part
    return parts


def stacked_rows(parts):
    row = lax.broadcasted_iota(jnp.int32, (16, parts[0].shape[1]), 0)
    out = jnp.zeros(row.shape, f32)
    for number, part in enumerate(parts):
        out = jnp.where(row == number, part, out)
    return out.astype(bf16)


def hot(index, count):
    return lax.broadcasted_iota(jnp.int32, (count, index.shape[1]), 0) == index


def as_bf16(mask):
    return jnp.where(mask, 1.0, 0.0).astype(bf16)


def duct_lists(duct, base, core):
    cells = jnp.concatenate([duct[base : base + 8], duct[base + 8 : base + 16]], axis=1)
    cells = cells.astype(jnp.int32) ^ (core * CELLS // 2 * NZ)
    extra = duct[base + 16 : base + 24]
    segment = jnp.concatenate([extra[0:1], extra[1:2]], axis=1).astype(jnp.int32)
    return cells >> 7, cells & (NZ - 1), segment


def forward_kernel(
    near2, near1, own, far1, far2, measured, kept, sums, temp, load, cond, kx, ky, kzp, kzm, keep
):
    g, core, _, _ = position()
    near, far = validity()
    slabs = (near2, near1, own, far1, far2)
    for j, slab in enumerate(slabs):
        valid = (near, near, 1.0, 1.0, far)[j]
        for r in range(2):
            i = 2 * j + r
            start = pl.multiple_of((r ^ core) * NY, NY)
            temp[0, i, MID] = slab[pl.ds(start, NY)]
            load[i] = DT * slab[pl.ds(CELLS + start, NY)]
            cond[i, MID] = jnp.exp(slab[pl.ds(2 * CELLS + start, NY)]) * valid

    def pads(i, carry):
        zero_pads(cond, i)
        for k in range(STEPS):
            zero_pads(temp.at[k], i)
        return carry

    lax.fori_loop(0, EXT, pads, 0)
    coefficients(cond, kx, ky, kzp, kzm, keep)
    coefs = (kx, ky, kzp, kzm, keep)
    for k in range(STEPS):
        advance(temp.at[k], temp.at[k + 1], k + 1, 8 - k, coefs, load, near, far)

    def save(i, carry):
        for k in range(STEPS):
            kept[k, i] = temp[k, 3 + i]
        return carry

    lax.fori_loop(0, 4, save, 0)

    rows, lanes, segment = duct_lists(own, 3 * CELLS, core)
    across = jnp.concatenate([temp[STEPS, 4, MID].T, temp[STEPS, 5, MID].T], axis=1)
    stack = jnp.concatenate([part.astype(bf16) for part in parts_of(across, 3)], axis=0)
    picked = jnp.zeros((NZ, 256), f32)
    for c in range(8):
        at_row = as_bf16(hot(rows[c : c + 1], CELLS))
        found = jnp.dot(stack, at_row, preferred_element_type=f32)
        value = (found[2 * NZ :] + found[NZ : 2 * NZ]) + found[:NZ]
        picked = picked + jnp.where(hot(lanes[c : c + 1], NZ), value, 0.0)
    partial = 0.5 * jnp.sum(picked, axis=0, keepdims=True)
    by_segment = lax.dot_general(
        stacked_rows(parts_of(partial, 3)),
        as_bf16(hot(segment, 128)),
        (((1,), (1,)), ((), ())),
        preferred_element_type=f32,
    )
    total = jnp.sum(by_segment, axis=0, keepdims=True)
    lane = lax.broadcasted_iota(jnp.int32, (1, 128), 1)
    for n in range(measured.shape[1]):
        mine = lane == measured.shape[1] * g + n
        total = total - jnp.where(mine, measured[0:1, n : n + 1], 0.0)
    sums[...] = jnp.broadcast_to(total, sums.shape)


def backward_kernel(
    near2, near1, own, far1, far2, near2d, near1d, ownd, far1d, far2d, kept, sums,
    grad, seg, costate, cond, kx, ky, kzp, kzm, keep, acc,
):
    g, core, _, _ = position()
    near, far = validity()
    conds = (near2, near1, own, far1, far2)
    ducts = (near2d, near1d, ownd, far1d, far2d)
    resid = jnp.sum(sums[...], axis=0, keepdims=True)
    shift = lax.rem(128 - seg.shape[1] * g, 128)
    seg[...] = pltpu.roll(jnp.broadcast_to(resid, (8, 128)), shift, 1)[0:1, 0 : seg.shape[1]]
    stack = stacked_rows(parts_of(0.5 * resid, 3))
    for j in range(5):
        valid = (near, near, 1.0, 1.0, far)[j]
        for r in range(2):
            start = pl.multiple_of((r ^ core) * NY, NY)
            cond[2 * j + r, MID] = jnp.exp(conds[j][pl.ds(start, NY)]) * valid
        rows, lanes, segment = duct_lists(ducts[j], 0, core)
        source = jnp.dot(stack, as_bf16(hot(segment, 128)), preferred_element_type=f32)
        source = jnp.sum(source, axis=0, keepdims=True) * valid
        upper, lower = parts_of(source, 2)
        out = jnp.zeros((CELLS, 2 * NZ), f32)
        for c in range(8):
            at_row = as_bf16(hot(rows[c : c + 1], CELLS))
            at_lane = hot(lanes[c : c + 1], NZ)
            weight = jnp.concatenate(
                [jnp.where(at_lane, upper, 0.0).astype(bf16), jnp.where(at_lane, lower, 0.0).astype(bf16)],
                axis=0,
            )
            out = out + lax.dot_general(
                at_row, weight, (((1,), (1,)), ((), ())), preferred_element_type=f32
            )
        out = out[:, :NZ] + out[:, NZ:]
        costate[0, 2 * j, MID] = out[:NY]
        costate[0, 2 * j + 1, MID] = out[NY:]

    def pads(i, carry):
        zero_pads(cond, i)
        for k in range(STEPS):
            zero_pads(costate.at[k], i)
        return carry

    lax.fori_loop(0, EXT, pads, 0)
    coefficients(cond, kx, ky, kzp, kzm, keep)
    coefs = (kx, ky, kzp, kzm, keep)
    for k in range(STEPS - 1):
        advance(costate.at[k], costate.at[k + 1], k + 1, 8 - k, coefs, None, near, far)
    ahead_keep, behind_keep = lane_masks(CH)
    share = grad.shape[2]

    def sensitivity(i, carry):
        at = (i - 4) ^ core
        for y in range(0, NY, CH):
            here = pl.ds(PAD + y, CH)
            left, right = pl.ds(PAD + y - 1, CH), pl.ds(PAD + y + 1, CH)
            total = jnp.zeros((CH, NZ), f32)
            for k in range(STEPS):
                u, a = kept.at[k], costate.at[STEPS - 1 - k]
                p = i - 3
                uc, ac = u[p, here], a[i, here]
                total += (uc - u[p + 1, here]) * (ac - a[i + 1, here])
                total += (uc - u[p - 1, here]) * (ac - a[i - 1, here])
                total += (uc - u[p, right]) * (ac - a[i, right])
                total += (uc - u[p, left]) * (ac - a[i, left])
                side = (uc - ahead_z(uc, ahead_keep)) * (ac - ahead_z(ac, ahead_keep))
                side += (uc - behind_z(uc, behind_keep)) * (ac - behind_z(ac, behind_keep))
                total += 0.5 * side
            acc[pl.ds(y, CH)] = (-WX) * cond[i, here] * total
        for n in range(NY // share):
            grad[n, at] = acc[pl.ds(n * share, share)]
        return carry

    lax.fori_loop(4, 6, sensitivity, 0)


def field(*lead, pad=True):
    return pltpu.VMEM((*lead, YP if pad else NY, NZ), f32)


def local(log_cond, opening_increase, heat_load, measured, duct_cells, duct_segment):
    grid = lax.axis_size("grid")
    tests = lax.axis_size("tests")
    lists = duct_cells.reshape(2, 128, 8).transpose(0, 2, 1).reshape(16, 128).astype(f32)
    segment = duct_segment.reshape(2, 128).astype(f32)
    pack = jnp.concatenate(
        [
            opening_increase.reshape(CELLS, NZ),
            heat_load.reshape(CELLS, NZ),
            log_cond.reshape(CELLS, NZ),
            lists,
            segment,
            jnp.zeros((6, NZ), f32),
        ],
        axis=0,
    )
    to_far = [(s, s - 2) for s in range(2, grid, 2)] + [(s, s + 2) for s in range(1, grid - 2, 2)]
    to_near = [(s, s + 2) for s in range(0, grid - 2, 2)] + [(s, s - 2) for s in range(3, grid, 2)]
    swap = [(s, s ^ 1) for s in range(grid)]
    far2 = lax.ppermute(pack, "grid", to_far)
    far1 = lax.ppermute(pack, "grid", swap)
    near2 = lax.ppermute(pack, "grid", to_near)
    near1 = lax.ppermute(far2, "grid", swap)
    packs = (near2, near1, pack, far1, far2)
    vmem = pl.BlockSpec(memory_space=pltpu.VMEM)
    coefs = [field(EXT, pad=False), field(EXT), field(EXT, pad=False), field(EXT, pad=False), field(EXT, pad=False)]
    params = pltpu.CompilerParams(vmem_limit_bytes=40 * 1024 * 1024)
    kept, sums = pl.pallas_call(
        forward_kernel,
        out_shape=(
            jax.ShapeDtypeStruct((STEPS, 4, YP, NZ), f32),
            jax.ShapeDtypeStruct((grid, 128), f32),
        ),
        in_specs=[vmem] * 6,
        out_specs=(vmem, vmem),
        scratch_shapes=[field(STEPS + 1, EXT), field(EXT, pad=False), field(EXT), *coefs],
        compiler_params=params,
        name="forward",
    )(*packs, measured)
    sums = lax.all_to_all(sums, "grid", split_axis=0, concat_axis=0, tiled=True)
    cond_spec = pl.BlockSpec((CELLS, NZ), lambda i: (2, 0))
    duct_spec = pl.BlockSpec((24, NZ), lambda i: (3 * CELLS // 24, 0))
    whole4 = pl.BlockSpec((STEPS, 4, YP, NZ), lambda i: (0, 0, 0, 0))
    share = NY // tests
    grad, seg = pl.pallas_call(
        backward_kernel,
        grid=(1,),
        out_shape=(
            jax.ShapeDtypeStruct((tests, 2, share, NZ), f32),
            jax.ShapeDtypeStruct(measured.shape, f32),
        ),
        in_specs=[cond_spec] * 5 + [duct_spec] * 5 + [whole4, pl.BlockSpec((grid, 128), lambda i: (0, 0))],
        out_specs=(
            pl.BlockSpec((tests, 2, share, NZ), lambda i: (0, 0, 0, 0)),
            pl.BlockSpec(measured.shape, lambda i: (0, 0)),
        ),
        scratch_shapes=[field(STEPS, EXT), field(EXT), *coefs, pltpu.VMEM((NY, NZ), f32)],
        compiler_params=params,
        name="backward",
    )(*packs, *packs, kept, sums)
    grad = lax.all_to_all(grad, "tests", split_axis=0, concat_axis=0, tiled=True)
    return jnp.sum(grad, axis=0), seg


def solution(mesh):
    in_specs = (
        P("grid", None, None),
        P("tests", "grid", None, None),
        P("tests", "grid", None, None),
        P("tests", "grid"),
        P("grid", None),
        P("grid", None),
    )
    out_specs = (P("grid", "tests", None), P("tests", "grid"))
    return jax.shard_map(local, mesh=mesh, in_specs=in_specs, out_specs=out_specs, check_vma=False)
```

```python
import jax
import jax.numpy as jnp
from jax import lax
from jax.experimental import pallas as pl
from jax.experimental.pallas import tpu as pltpu
from jax.sharding import PartitionSpec as P

STEPS = 4
DT = 0.08
WX = 0.5 * DT
WZ = 0.25 * DT
NY = 128
NZ = 128
CELLS = 2 * NY
EXT = 10
PAD = 8
YP = NY + 2 * PAD
MID = slice(PAD, PAD + NY)
CH = 32
Q0 = 0
U0 = NY
C0 = U0 + CELLS
D0 = C0 + CELLS
Q1 = D0 + 24
PACK = Q1 + NY
bf16 = jnp.bfloat16
f32 = jnp.float32


def position():
    g = lax.axis_index("grid")
    return g, lax.rem(g, 2), lax.div(g, 2), lax.axis_size("grid") // 2


def validity():
    _, core, chip, chips = position()
    low, high = (chip > 0).astype(f32), (chip < chips - 1).astype(f32)
    near = jnp.where(core == 0, low, high)
    far = jnp.where(core == 0, high, low)
    return near, far


def row_validity(i, near, far):
    return jnp.where(i < 4, near, jnp.where(i < 8, 1.0, far))


def lane_masks(rows):
    lane = lax.broadcasted_iota(jnp.int32, (rows, NZ), 1)
    return lane < NZ - 1, lane > 0


def ahead_z(values, keep):
    return jnp.where(keep, pltpu.roll(values, NZ - 1, 1), 0.0)


def behind_z(values, keep):
    return jnp.where(keep, pltpu.roll(values, 1, 1), 0.0)


def zero_pads(ref, lead):
    ref[lead, 0:PAD] = jnp.zeros((PAD, NZ), f32)
    ref[lead, PAD + NY : YP] = jnp.zeros((PAD, NZ), f32)


def coefficients(cond, kx, ky, kzp, kzm, keep):
    ahead_keep, behind_keep = lane_masks(CH)

    def row(i, carry):
        for y in range(0, NY, CH):
            here = pl.ds(PAD + y, CH)
            c = cond[i, here]
            cxp, cxm = cond[i + 1, here], cond[i - 1, here]
            cyp, cym = cond[i, pl.ds(PAD + y + 1, CH)], cond[i, pl.ds(PAD + y - 1, CH)]
            czp, czm = ahead_z(c, ahead_keep), behind_z(c, behind_keep)
            kx[i, pl.ds(y, CH)] = WX * (c + cxp)
            face_y = WX * (c + cyp)
            if y + CH == NY:
                edge = lax.broadcasted_iota(jnp.int32, (CH, NZ), 0) == CH - 1
                face_y = jnp.where(edge, 0.0, face_y)
            ky[i, here] = face_y
            kzp[i, pl.ds(y, CH)] = jnp.where(ahead_keep, WZ * (c + czp), 0.0)
            kzm[i, pl.ds(y, CH)] = jnp.where(behind_keep, WZ * (c + czm), 0.0)
            total = WX * (((cxp + cxm) + (cyp + cym)) + 4.0 * c) + WZ * ((czp + czm) + 2.0 * c)
            keep[i, pl.ds(y, CH)] = 1.0 - total
        ky[i, 0:PAD] = jnp.zeros((PAD, NZ), f32)
        return carry

    kx[0] = WX * (cond[0, MID] + cond[1, MID])
    lax.fori_loop(1, 9, row, 0)


def advance(src, dst, first, last, coefs, load, near, far):
    kx, ky, kzp, kzm, keep = coefs

    def row(i, carry):
        inside = row_validity(i, near, far)
        for y in range(0, NY, CH):
            here, flat = pl.ds(PAD + y, CH), pl.ds(y, CH)
            u = src[i, here]
            new = keep[i, flat] * u
            new += kx[i, flat] * src[i + 1, here]
            new += kx[i - 1, flat] * src[i - 1, here]
            new += ky[i, here] * src[i, pl.ds(PAD + y + 1, CH)]
            new += ky[i, pl.ds(PAD + y - 1, CH)] * src[i, pl.ds(PAD + y - 1, CH)]
            new += kzp[i, flat] * pltpu.roll(u, NZ - 1, 1)
            new += kzm[i, flat] * pltpu.roll(u, 1, 1)
            if load is not None:
                new += load[i, flat]
            dst[i, here] = new * inside
        return carry

    lax.fori_loop(first, last + 1, row, 0)


def parts_of(values, count):
    parts = []
    for _ in range(count):
        part = values.astype(bf16).astype(f32)
        parts.append(part)
        values = values - part
    return parts


def stacked_rows(parts):
    row = lax.broadcasted_iota(jnp.int32, (16, parts[0].shape[1]), 0)
    out = jnp.zeros(row.shape, f32)
    for number, part in enumerate(parts):
        out = jnp.where(row == number, part, out)
    return out.astype(bf16)


def hot(index, count):
    return lax.broadcasted_iota(jnp.int32, (count, index.shape[1]), 0) == index


def as_bf16(mask):
    return jnp.where(mask, 1.0, 0.0).astype(bf16)


def duct_lists(duct, base, flip):
    cells = jnp.concatenate([duct[base : base + 8], duct[base + 8 : base + 16]], axis=1)
    cells = cells.astype(jnp.int32)
    if flip:
        cells = cells ^ (NY * NZ)
    extra = duct[base + 16 : base + 24]
    segment = jnp.concatenate([extra[0:1], extra[1:2]], axis=1).astype(jnp.int32)
    return cells >> 7, cells & (NZ - 1), segment


def pack_kernel(log_cond, opening, heat, cells, segment, measured, full, cells_v, segment_v, measured_v, sems):
    g, core, _, _ = position()
    copies = []

    def copy(src, dst):
        copies.append(pltpu.make_async_copy(src, dst, sems.at[len(copies)]))
        copies[-1].start()

    for r in range(2):
        at = r ^ core
        copy(opening.at[0, at], full.at[pl.ds(U0 + r * NY, NY)])
        copy(log_cond.at[at], full.at[pl.ds(C0 + r * NY, NY)])
        copy(heat.at[0, at], full.at[pl.ds(Q1 if r else Q0, NY)])
    copy(cells, cells_v)
    copy(segment, segment_v)
    copy(measured, measured_v)
    for each in copies:
        each.wait()
    flipped = (cells_v[...] ^ (core * NY * NZ)).astype(f32)
    lane = lax.broadcasted_iota(jnp.int32, (8, 128), 1)
    row = lax.broadcasted_iota(jnp.int32, (8, 128), 0)
    seg = segment_v[...].astype(f32)
    extra = jnp.where(row == 0, seg[:, :128], jnp.where(row == 1, seg[:, 128:], 0.0))
    for n in range(measured.shape[1]):
        mine = (row == 2) & (lane == measured.shape[1] * g + n)
        extra = jnp.where(mine, measured_v[0:1, n : n + 1], extra)
    full[D0 : D0 + 8] = flipped[:, :128]
    full[D0 + 8 : D0 + 16] = flipped[:, 128:]
    full[D0 + 16 : D0 + 24] = extra


def slab_rows(near2, near1, own, far1, far2):
    out = []
    for j, slab in enumerate((near2, near1, own, far1, far2)):
        for r in range(2):
            out.append((slab, 1 - r if j in (1, 3) else r))
    return out


def forward_kernel(
    near2, near1, own, far1, far2, temp, sums, cond, kx, ky, kzp, kzm, keep, load
):
    near, far = validity()
    for i, (slab, r) in enumerate(slab_rows(near2, near1, own, far1, far2)):
        valid = near if i < 4 else (far if i > 7 else 1.0)
        temp[0, i, MID] = slab[pl.ds(U0 + r * NY, NY)]
        cond[i, MID] = jnp.exp(slab[pl.ds(C0 + r * NY, NY)]) * valid
        if 1 <= i <= 8:
            load[i] = DT * slab[pl.ds(Q1 if r else Q0, NY)]

    def pads(i, carry):
        zero_pads(cond, i)
        for k in range(STEPS):
            zero_pads(temp.at[k], i)
        return carry

    lax.fori_loop(0, EXT, pads, 0)
    coefficients(cond, kx, ky, kzp, kzm, keep)
    coefs = (kx, ky, kzp, kzm, keep)
    for k in range(STEPS):
        advance(temp.at[k], temp.at[k + 1], k + 1, 8 - k, coefs, load, near, far)

    rows, lanes, segment = duct_lists(own, D0, False)
    across = jnp.concatenate([temp[STEPS, 4, MID].T, temp[STEPS, 5, MID].T], axis=1)
    stack = jnp.concatenate([part.astype(bf16) for part in parts_of(across, 3)], axis=0)
    picked = jnp.zeros((NZ, 256), f32)
    for c in range(8):
        at_row = as_bf16(hot(rows[c : c + 1], CELLS))
        found = jnp.dot(stack, at_row, preferred_element_type=f32)
        value = (found[2 * NZ :] + found[NZ : 2 * NZ]) + found[:NZ]
        picked = picked + jnp.where(hot(lanes[c : c + 1], NZ), value, 0.0)
    partial = 0.5 * jnp.sum(picked, axis=0, keepdims=True)
    by_segment = lax.dot_general(
        stacked_rows(parts_of(partial, 3)),
        as_bf16(hot(segment, 128)),
        (((1,), (1,)), ((), ())),
        preferred_element_type=f32,
    )
    total = jnp.sum(by_segment, axis=0, keepdims=True) - own[pl.ds(D0 + 16, 8)][2:3]
    sums[...] = jnp.broadcast_to(total, sums.shape)


def backward_kernel(
    near2, near1, own, far1, far2, temp, sums, cond, kx, ky, kzp, kzm, keep,
    grad, seg, costate, acc, at_rows, weights,
):
    g, core, _, _ = position()
    near, far = validity()
    resid = jnp.sum(sums[...], axis=0, keepdims=True)
    shift = lax.rem(128 - seg.shape[1] * g, 128)
    seg[...] = pltpu.roll(jnp.broadcast_to(resid, (8, 128)), shift, 1)[0:1, 0 : seg.shape[1]]
    stack = stacked_rows(parts_of(0.5 * resid, 3))
    for j, slab in enumerate((near2, near1, own, far1, far2)):
        valid = (near, near, 1.0, 1.0, far)[j]
        rows, lanes, segment = duct_lists(slab, D0, j in (1, 3))
        source = jnp.dot(stack, as_bf16(hot(segment, 128)), preferred_element_type=f32)
        source = jnp.sum(source, axis=0, keepdims=True) * valid
        upper, lower = parts_of(source, 2)
        for c in range(8):
            at = pl.ds(256 * c, 256)
            at_rows[j, :, at] = as_bf16(hot(rows[c : c + 1], CELLS))
            at_lane = hot(lanes[c : c + 1], NZ)
            weights[j, 0:NZ, at] = jnp.where(at_lane, upper, 0.0).astype(bf16)
            weights[j, NZ : 2 * NZ, at] = jnp.where(at_lane, lower, 0.0).astype(bf16)
        out = lax.dot_general(
            at_rows[j], weights[j], (((1,), (1,)), ((), ())), preferred_element_type=f32
        )
        out = out[:, :NZ] + out[:, NZ:]
        costate[0, 2 * j, MID] = out[:NY]
        costate[0, 2 * j + 1, MID] = out[NY:]

    def pads(i, carry):
        for k in range(STEPS):
            zero_pads(costate.at[k], i)
        return carry

    lax.fori_loop(0, EXT, pads, 0)
    coefs = (kx, ky, kzp, kzm, keep)
    for k in range(STEPS - 1):
        advance(costate.at[k], costate.at[k + 1], k + 1, 8 - k, coefs, None, near, far)
    ahead_keep, behind_keep = lane_masks(CH)
    share = grad.shape[2]

    def sensitivity(i, carry):
        at = (i - 4) ^ core
        for y in range(0, NY, CH):
            here = pl.ds(PAD + y, CH)
            left, right = pl.ds(PAD + y - 1, CH), pl.ds(PAD + y + 1, CH)
            total = jnp.zeros((CH, NZ), f32)
            for k in range(STEPS):
                u, a = temp.at[k], costate.at[STEPS - 1 - k]
                uc, ac = u[i, here], a[i, here]
                total += (uc - u[i + 1, here]) * (ac - a[i + 1, here])
                total += (uc - u[i - 1, here]) * (ac - a[i - 1, here])
                total += (uc - u[i, right]) * (ac - a[i, right])
                total += (uc - u[i, left]) * (ac - a[i, left])
                side = (uc - ahead_z(uc, ahead_keep)) * (ac - ahead_z(ac, ahead_keep))
                side += (uc - behind_z(uc, behind_keep)) * (ac - behind_z(ac, behind_keep))
                total += 0.5 * side
            acc[pl.ds(y, CH)] = (-WX) * cond[i, here] * total
        for n in range(NY // share):
            grad[n, at] = acc[pl.ds(n * share, share)]
        return carry

    lax.fori_loop(4, 6, sensitivity, 0)


def field(*lead, pad=True):
    return (*lead, YP if pad else NY, NZ)


def in_hbm(values):
    return pltpu.with_memory_space_constraint(values, pltpu.HBM)


def local(log_cond, opening_increase, heat_load, measured, duct_cells, duct_segment):
    grid = lax.axis_size("grid")
    tests = lax.axis_size("tests")
    vmem = pl.BlockSpec(memory_space=pltpu.VMEM)
    params = pltpu.CompilerParams(vmem_limit_bytes=24 * 1024 * 1024)
    pack = pl.pallas_call(
        pack_kernel,
        out_shape=pltpu.VMEM((PACK, NZ), f32),
        in_specs=[pl.BlockSpec(memory_space=pltpu.HBM)] * 6,
        out_specs=vmem,
        scratch_shapes=[
            pltpu.VMEM((8, 256), jnp.int32),
            pltpu.VMEM((1, 256), jnp.int32),
            pltpu.VMEM(measured.shape, f32),
            pltpu.SemaphoreType.DMA((9,)),
        ],
        compiler_params=params,
        name="pack",
    )(*map(in_hbm, (log_cond, opening_increase, heat_load, duct_cells.T, duct_segment.T, measured)))
    to_far = [(s, s - 2) for s in range(2, grid, 2)] + [(s, s + 2) for s in range(1, grid - 2, 2)]
    to_near = [(s, s + 2) for s in range(0, grid - 2, 2)] + [(s, s - 2) for s in range(3, grid, 2)]
    swap = [(s, s ^ 1) for s in range(grid)]
    far2 = lax.ppermute(pack, "grid", to_far)
    far1 = lax.ppermute(pack, "grid", swap)
    near2 = lax.ppermute(pack, "grid", to_near)
    near1 = lax.ppermute(far2, "grid", swap)
    packs = (near2, near1, pack, far1, far2)
    coefs = [field(EXT), field(EXT, pad=False), field(EXT), field(EXT, pad=False), field(EXT, pad=False), field(EXT, pad=False)]
    temp, sums, *coefs = pl.pallas_call(
        forward_kernel,
        out_shape=tuple(
            jax.ShapeDtypeStruct(shape, f32) for shape in (field(STEPS + 1, EXT), (grid, 128), *coefs)
        ),
        in_specs=[vmem] * 5,
        out_specs=(vmem,) * 8,
        scratch_shapes=[pltpu.VMEM(field(EXT, pad=False), f32)],
        compiler_params=params,
        name="forward",
    )(*packs)
    sums = lax.all_to_all(sums, "grid", split_axis=0, concat_axis=0, tiled=True)
    share = NY // tests
    grad, seg = pl.pallas_call(
        backward_kernel,
        out_shape=(
            jax.ShapeDtypeStruct((tests, 2, share, NZ), f32),
            jax.ShapeDtypeStruct(measured.shape, f32),
        ),
        in_specs=[vmem] * 13,
        out_specs=(vmem, vmem),
        scratch_shapes=[
            pltpu.VMEM(field(STEPS, EXT), f32),
            pltpu.VMEM((NY, NZ), f32),
            pltpu.VMEM((5, CELLS, 2048), bf16),
            pltpu.VMEM((5, CELLS, 2048), bf16),
        ],
        compiler_params=params,
        name="backward",
    )(*packs, temp, sums, *coefs)
    grad = lax.all_to_all(grad, "tests", split_axis=0, concat_axis=0, tiled=True)
    return jnp.sum(grad, axis=0), seg


def solution(mesh):
    in_specs = (
        P("grid", None, None),
        P("tests", "grid", None, None),
        P("tests", "grid", None, None),
        P("tests", "grid"),
        P("grid", None),
        P("grid", None),
    )
    out_specs = (P("grid", "tests", None), P("tests", "grid"))
    return jax.shard_map(local, mesh=mesh, in_specs=in_specs, out_specs=out_specs, check_vma=False)
```

```python
import jax
import jax.numpy as jnp
from jax import lax
from jax.experimental import pallas as pl
from jax.experimental.pallas import tpu as pltpu
from jax.sharding import PartitionSpec as P

STEPS = 4
DT = 0.08
WX = 0.5 * DT
WZ = 0.25 * DT
NY = 128
NZ = 128
CELLS = 2 * NY
EXT = 10
PAD = 8
YP = NY + 2 * PAD
MID = slice(PAD, PAD + NY)
CH = 32
Q0 = 0
U0 = NY
C0 = U0 + CELLS
D0 = C0 + CELLS
Q1 = D0 + 24
PACK = Q1 + NY
COST_ESTIMATE = 2_000_000_000
bf16 = jnp.bfloat16
f32 = jnp.float32


def position():
    g = lax.axis_index("grid")
    return g, lax.rem(g, 2), lax.div(g, 2), lax.axis_size("grid") // 2


def validity():
    _, core, chip, chips = position()
    low, high = (chip > 0).astype(f32), (chip < chips - 1).astype(f32)
    near = jnp.where(core == 0, low, high)
    far = jnp.where(core == 0, high, low)
    return near, far


def row_validity(i, near, far):
    return jnp.where(i < 4, near, jnp.where(i < 8, 1.0, far))


def lane_masks(rows):
    lane = lax.broadcasted_iota(jnp.int32, (rows, NZ), 1)
    return lane < NZ - 1, lane > 0


def ahead_z(values, keep):
    return jnp.where(keep, pltpu.roll(values, NZ - 1, 1), 0.0)


def behind_z(values, keep):
    return jnp.where(keep, pltpu.roll(values, 1, 1), 0.0)


def zero_pads(ref, lead):
    ref[lead, 0:PAD] = jnp.zeros((PAD, NZ), f32)
    ref[lead, PAD + NY : YP] = jnp.zeros((PAD, NZ), f32)


def coefficients(cond, kx, ky, kzp, kzm, keep):
    ahead_keep, behind_keep = lane_masks(CH)

    def row(i, carry):
        for y in range(0, NY, CH):
            here = pl.ds(PAD + y, CH)
            c = cond[i, here]
            cxp, cxm = cond[i + 1, here], cond[i - 1, here]
            cyp, cym = cond[i, pl.ds(PAD + y + 1, CH)], cond[i, pl.ds(PAD + y - 1, CH)]
            czp, czm = ahead_z(c, ahead_keep), behind_z(c, behind_keep)
            kx[i, pl.ds(y, CH)] = WX * (c + cxp)
            face_y = WX * (c + cyp)
            if y + CH == NY:
                edge = lax.broadcasted_iota(jnp.int32, (CH, NZ), 0) == CH - 1
                face_y = jnp.where(edge, 0.0, face_y)
            ky[i, here] = face_y
            kzp[i, pl.ds(y, CH)] = jnp.where(ahead_keep, WZ * (c + czp), 0.0)
            kzm[i, pl.ds(y, CH)] = jnp.where(behind_keep, WZ * (c + czm), 0.0)
            total = WX * (((cxp + cxm) + (cyp + cym)) + 4.0 * c) + WZ * ((czp + czm) + 2.0 * c)
            keep[i, pl.ds(y, CH)] = 1.0 - total
        ky[i, 0:PAD] = jnp.zeros((PAD, NZ), f32)
        return carry

    kx[0] = WX * (cond[0, MID] + cond[1, MID])
    lax.fori_loop(1, 9, row, 0)


def advance(src, dst, first, last, coefs, load, near, far):
    kx, ky, kzp, kzm, keep = coefs

    def row(i, carry):
        inside = row_validity(i, near, far)
        for y in range(0, NY, CH):
            here, flat = pl.ds(PAD + y, CH), pl.ds(y, CH)
            u = src[i, here]
            new = keep[i, flat] * u
            new += kx[i, flat] * src[i + 1, here]
            new += kx[i - 1, flat] * src[i - 1, here]
            new += ky[i, here] * src[i, pl.ds(PAD + y + 1, CH)]
            new += ky[i, pl.ds(PAD + y - 1, CH)] * src[i, pl.ds(PAD + y - 1, CH)]
            new += kzp[i, flat] * pltpu.roll(u, NZ - 1, 1)
            new += kzm[i, flat] * pltpu.roll(u, 1, 1)
            if load is not None:
                new += load[i, flat]
            dst[i, here] = new * inside
        return carry

    lax.fori_loop(first, last + 1, row, 0)


def parts_of(values, count):
    parts = []
    for _ in range(count):
        part = values.astype(bf16).astype(f32)
        parts.append(part)
        values = values - part
    return parts


def stacked_rows(parts):
    row = lax.broadcasted_iota(jnp.int32, (16, parts[0].shape[1]), 0)
    out = jnp.zeros(row.shape, f32)
    for number, part in enumerate(parts):
        out = jnp.where(row == number, part, out)
    return out.astype(bf16)


def hot(index, count):
    return lax.broadcasted_iota(jnp.int32, (count, index.shape[1]), 0) == index


def as_bf16(mask):
    return jnp.where(mask, 1.0, 0.0).astype(bf16)


def duct_lists(duct, base, flip):
    cells = jnp.concatenate([duct[base : base + 8], duct[base + 8 : base + 16]], axis=1)
    cells = cells.astype(jnp.int32)
    if flip:
        cells = cells ^ (NY * NZ)
    extra = duct[base + 16 : base + 24]
    segment = jnp.concatenate([extra[0:1], extra[1:2]], axis=1).astype(jnp.int32)
    return cells >> 7, cells & (NZ - 1), segment


def pack_kernel(log_cond, opening, heat, cells, segment, measured, full, near, cells_v, segment_v, measured_v, sems):
    g, core, _, _ = position()
    copies = []

    def copy(src, dst):
        copies.append(pltpu.make_async_copy(src, dst, sems.at[len(copies)]))
        copies[-1].start()

    for r in range(2):
        at = r ^ core
        for out, skip in ((full, 0), (near, NY)):
            copy(opening.at[0, at], out.at[pl.ds(U0 - skip + r * NY, NY)])
            copy(log_cond.at[at], out.at[pl.ds(C0 - skip + r * NY, NY)])
            if r == 1:
                copy(heat.at[0, at], out.at[pl.ds(Q1 - skip, NY)])
            elif skip == 0:
                copy(heat.at[0, at], out.at[pl.ds(Q0, NY)])
    copy(cells, cells_v)
    copy(segment, segment_v)
    copy(measured, measured_v)
    for each in copies:
        each.wait()
    flipped = (cells_v[...] ^ (core * NY * NZ)).astype(f32)
    lane = lax.broadcasted_iota(jnp.int32, (8, 128), 1)
    row = lax.broadcasted_iota(jnp.int32, (8, 128), 0)
    seg = segment_v[...].astype(f32)
    extra = jnp.where(row == 0, seg[:, :128], jnp.where(row == 1, seg[:, 128:], 0.0))
    for n in range(measured.shape[1]):
        mine = (row == 2) & (lane == measured.shape[1] * g + n)
        extra = jnp.where(mine, measured_v[0:1, n : n + 1], extra)
    for out, skip in ((full, 0), (near, NY)):
        out[pl.ds(D0 - skip, 8)] = flipped[:, :128]
        out[pl.ds(D0 - skip + 8, 8)] = flipped[:, 128:]
        out[pl.ds(D0 - skip + 16, 8)] = extra


def write_hots(duct, base, flip, j, at_rows, at_lanes, at_segments):
    rows, lanes, segment = duct_lists(duct, base, flip)
    for c in range(8):
        at = pl.ds(256 * c, 256)
        at_rows[j, :, at] = as_bf16(hot(rows[c : c + 1], CELLS))
        at_lanes[j, :, at] = as_bf16(hot(lanes[c : c + 1], NZ))
    if at_segments is not None:
        at_segments[j] = as_bf16(hot(segment, 128))


def prepare_own_kernel(own, at_rows, at_lanes, at_segments):
    write_hots(own, D0, False, 0, at_rows, at_lanes, at_segments)


def prepare_far_kernel(far1, far2, at_rows, at_lanes, at_segments):
    write_hots(far1, D0, True, 0, at_rows, at_lanes, at_segments)
    write_hots(far2, D0, False, 1, at_rows, at_lanes, at_segments)


def prepare_near_kernel(near2, far_segments, at_segments):
    _, _, segment = duct_lists(near2, D0 - NY, False)
    at_segments[0] = as_bf16(hot(segment, 128))


def slab_rows(near2, near1, own, far1, far2):
    out = []
    for j, slab in enumerate((near2, near1, own, far1, far2)):
        for r in range(2):
            out.append((slab, NY if j == 0 else 0, 1 - r if j in (1, 3) else r))
    return out


def forward_kernel(
    near2, near1, own, far1, far2, at_rows, at_lanes, at_segments,
    temp, sums, cond, kx, ky, kzp, kzm, keep, load,
):
    near, far = validity()
    for i, (slab, skip, r) in enumerate(slab_rows(near2, near1, own, far1, far2)):
        valid = near if i < 4 else (far if i > 7 else 1.0)
        temp[0, i, MID] = slab[pl.ds(U0 - skip + r * NY, NY)]
        cond[i, MID] = jnp.exp(slab[pl.ds(C0 - skip + r * NY, NY)]) * valid
        if 1 <= i <= 8:
            load[i] = DT * slab[pl.ds((Q1 - skip) if r else Q0, NY)]

    def pads(i, carry):
        zero_pads(cond, i)
        for k in range(STEPS):
            zero_pads(temp.at[k], i)
        return carry

    lax.fori_loop(0, EXT, pads, 0)
    coefficients(cond, kx, ky, kzp, kzm, keep)
    coefs = (kx, ky, kzp, kzm, keep)
    for k in range(STEPS):
        advance(temp.at[k], temp.at[k + 1], k + 1, 8 - k, coefs, load, near, far)

    across = jnp.concatenate([temp[STEPS, 4, MID].T, temp[STEPS, 5, MID].T], axis=1)
    stack = jnp.concatenate([part.astype(bf16) for part in parts_of(across, 3)], axis=0)
    picked = jnp.zeros((NZ, 256), f32)
    for c in range(8):
        at = pl.ds(256 * c, 256)
        found = jnp.dot(stack, at_rows[0, :, at], preferred_element_type=f32)
        value = (found[2 * NZ :] + found[NZ : 2 * NZ]) + found[:NZ]
        picked = picked + value * at_lanes[0, :, at].astype(f32)
    partial = 0.5 * jnp.sum(picked, axis=0, keepdims=True)
    by_segment = lax.dot_general(
        stacked_rows(parts_of(partial, 3)),
        at_segments[0],
        (((1,), (1,)), ((), ())),
        preferred_element_type=f32,
    )
    total = jnp.sum(by_segment, axis=0, keepdims=True) - own[pl.ds(D0 + 16, 8)][2:3]
    sums[...] = jnp.broadcast_to(total, sums.shape)


def backward_kernel(
    near2, near1, own_rows, own_lanes, own_segments, far_rows, far_lanes, far_segments, near2_segments,
    temp, sums, cond, kx, ky, kzp, kzm, keep, grad, seg,
    costate, acc, weights, near_rows, near_lanes, near_segments,
):
    g, core, _, _ = position()
    near, far = validity()
    resid = jnp.sum(sums[...], axis=0, keepdims=True)
    shift = lax.rem(128 - seg.shape[1] * g, 128)
    seg[...] = pltpu.roll(jnp.broadcast_to(resid, (8, 128)), shift, 1)[0:1, 0 : seg.shape[1]]
    stack = stacked_rows(parts_of(0.5 * resid, 3))
    write_hots(near2, D0 - NY, False, 0, near_rows, near_lanes, None)
    near_segments[0] = near2_segments[0]
    write_hots(near1, D0, True, 1, near_rows, near_lanes, near_segments)
    own, fars = (own_rows, own_lanes, own_segments), (far_rows, far_lanes, far_segments)
    nears = (near_rows, near_lanes, near_segments)
    places = ((nears, 0, near), (nears, 1, near), (own, 0, 1.0), (fars, 0, 1.0), (fars, 1, far))
    for j, ((at_rows, at_lanes, at_segments), n, valid) in enumerate(places):
        source = jnp.dot(stack, at_segments[n], preferred_element_type=f32)
        source = jnp.sum(source, axis=0, keepdims=True) * valid
        upper, lower = (part.astype(bf16) for part in parts_of(source, 2))
        for c in range(8):
            at = pl.ds(256 * c, 256)
            weights[j, 0:NZ, at] = at_lanes[n, :, at] * upper
            weights[j, NZ : 2 * NZ, at] = at_lanes[n, :, at] * lower
        out = lax.dot_general(
            at_rows[n], weights[j], (((1,), (1,)), ((), ())), preferred_element_type=f32
        )
        out = out[:, :NZ] + out[:, NZ:]
        costate[0, 2 * j, MID] = out[:NY]
        costate[0, 2 * j + 1, MID] = out[NY:]

    def pads(i, carry):
        for k in range(STEPS):
            zero_pads(costate.at[k], i)
        return carry

    lax.fori_loop(0, EXT, pads, 0)
    coefs = (kx, ky, kzp, kzm, keep)
    for k in range(STEPS - 1):
        advance(costate.at[k], costate.at[k + 1], k + 1, 8 - k, coefs, None, near, far)
    ahead_keep, behind_keep = lane_masks(CH)
    share = grad.shape[2]

    def sensitivity(i, carry):
        at = (i - 4) ^ core
        for y in range(0, NY, CH):
            here = pl.ds(PAD + y, CH)
            left, right = pl.ds(PAD + y - 1, CH), pl.ds(PAD + y + 1, CH)
            total = jnp.zeros((CH, NZ), f32)
            for k in range(STEPS):
                u, a = temp.at[k], costate.at[STEPS - 1 - k]
                uc, ac = u[i, here], a[i, here]
                total += (uc - u[i + 1, here]) * (ac - a[i + 1, here])
                total += (uc - u[i - 1, here]) * (ac - a[i - 1, here])
                total += (uc - u[i, right]) * (ac - a[i, right])
                total += (uc - u[i, left]) * (ac - a[i, left])
                side = (uc - ahead_z(uc, ahead_keep)) * (ac - ahead_z(ac, ahead_keep))
                side += (uc - behind_z(uc, behind_keep)) * (ac - behind_z(ac, behind_keep))
                total += 0.5 * side
            acc[pl.ds(y, CH)] = (-WX) * cond[i, here] * total
        for n in range(NY // share):
            grad[n, at] = acc[pl.ds(n * share, share)]
        return carry

    lax.fori_loop(4, 6, sensitivity, 0)


def field(*lead, pad=True):
    return (*lead, YP if pad else NY, NZ)


def in_hbm(values):
    return pltpu.with_memory_space_constraint(values, pltpu.HBM)


def local(log_cond, opening_increase, heat_load, measured, duct_cells, duct_segment):
    grid = lax.axis_size("grid")
    tests = lax.axis_size("tests")
    vmem = pl.BlockSpec(memory_space=pltpu.VMEM)
    params = pltpu.CompilerParams(vmem_limit_bytes=24 * 1024 * 1024)
    pack, pack_near = pl.pallas_call(
        pack_kernel,
        out_shape=(pltpu.VMEM((PACK, NZ), f32), pltpu.VMEM((PACK - NY, NZ), f32)),
        in_specs=[pl.BlockSpec(memory_space=pltpu.HBM)] * 6,
        out_specs=(vmem, vmem),
        scratch_shapes=[
            pltpu.VMEM((8, 256), jnp.int32),
            pltpu.VMEM((1, 256), jnp.int32),
            pltpu.VMEM(measured.shape, f32),
            pltpu.SemaphoreType.DMA((14,)),
        ],
        compiler_params=params,
        name="pack",
    )(*map(in_hbm, (log_cond, opening_increase, heat_load, duct_cells.T, duct_segment.T, measured)))
    to_far = [(s, s - 2) for s in range(2, grid, 2)] + [(s, s + 2) for s in range(1, grid - 2, 2)]
    to_near = [(s, s + 2) for s in range(0, grid - 2, 2)] + [(s, s - 2) for s in range(3, grid, 2)]
    swap = [(s, s ^ 1) for s in range(grid)]
    far2 = lax.ppermute(pack, "grid", to_far)
    far1 = lax.ppermute(pack, "grid", swap)
    near2 = lax.ppermute(pack_near, "grid", to_near)

    def hots(slabs):
        return (
            pltpu.VMEM((slabs, CELLS, 2048), bf16),
            pltpu.VMEM((slabs, NZ, 2048), bf16),
            pltpu.VMEM((slabs, 128, 256), bf16),
        )

    def prepare(kernel, out_shape, name, *slabs):
        return pl.pallas_call(
            kernel,
            out_shape=out_shape,
            in_specs=[vmem] * len(slabs),
            out_specs=(vmem,) * len(out_shape),
            compiler_params=params,
            cost_estimate=pl.CostEstimate(flops=COST_ESTIMATE, bytes_accessed=4_000_000, transcendentals=0),
            name=name,
        )(*slabs)

    own_hots = prepare(prepare_own_kernel, hots(1), "prepare_own", pack)
    far2, *own_hots = lax.optimization_barrier((far2, *own_hots))
    near1 = lax.ppermute(far2, "grid", swap)
    far_hots = prepare(prepare_far_kernel, hots(2), "prepare_far", far1, far2)
    near_hots = prepare(prepare_near_kernel, hots(1)[2:], "prepare_near", near2, far_hots[2])
    near2, near_hots, far_hots = lax.optimization_barrier((near2, near_hots, far_hots))
    packs = (near2, near1, pack, far1, far2)
    coefs = [field(EXT), field(EXT, pad=False), field(EXT), field(EXT, pad=False), field(EXT, pad=False), field(EXT, pad=False)]
    temp, sums, *coefs = pl.pallas_call(
        forward_kernel,
        out_shape=tuple(pltpu.VMEM(shape, f32) for shape in (field(STEPS + 1, EXT), (grid, 128), *coefs)),
        in_specs=[vmem] * 8,
        out_specs=(vmem,) * 8,
        scratch_shapes=[pltpu.VMEM(field(EXT, pad=False), f32)],
        compiler_params=params,
        name="forward",
    )(*packs, *own_hots)
    sums = lax.all_to_all(sums, "grid", split_axis=0, concat_axis=0, tiled=True)
    share = NY // tests
    grad, seg = pl.pallas_call(
        backward_kernel,
        out_shape=(
            pltpu.VMEM((tests, 2, share, NZ), f32),
            jax.ShapeDtypeStruct(measured.shape, f32),
        ),
        in_specs=[vmem] * 17,
        out_specs=(vmem, vmem),
        scratch_shapes=[
            pltpu.VMEM(field(STEPS, EXT), f32),
            pltpu.VMEM((NY, NZ), f32),
            pltpu.VMEM((5, CELLS, 2048), bf16),
            *hots(2),
        ],
        compiler_params=params,
        name="backward",
    )(near2, near1, *own_hots, *far_hots, *near_hots, temp, sums, *coefs)
    grad = lax.all_to_all(grad, "tests", split_axis=0, concat_axis=0, tiled=True)
    return jnp.sum(grad, axis=0), seg


def solution(mesh):
    in_specs = (
        P("grid", None, None),
        P("tests", "grid", None, None),
        P("tests", "grid", None, None),
        P("tests", "grid"),
        P("grid", None),
        P("grid", None),
    )
    out_specs = (P("grid", "tests", None), P("tests", "grid"))
    return jax.shard_map(local, mesh=mesh, in_specs=in_specs, out_specs=out_specs, check_vma=False)
```

```python
import jax
import jax.numpy as jnp
from jax import lax
from jax.experimental import pallas as pl
from jax.experimental.pallas import tpu as pltpu
from jax.sharding import PartitionSpec as P

STEPS = 4
DT = 0.08
WX = 0.5 * DT
WZ = 0.25 * DT
NY = 128
NZ = 128
CELLS = 2 * NY
EXT = 10
SUB = 8
BLOCKS = NY // SUB
Q0 = 0
U0 = NY
C0 = U0 + CELLS
D0 = C0 + CELLS
Q1 = D0 + 24
PACK = Q1 + NY
COST_ESTIMATE = 2_000_000_000
bf16 = jnp.bfloat16
f32 = jnp.float32


def position():
    g = lax.axis_index("grid")
    return g, lax.rem(g, 2), lax.div(g, 2), lax.axis_size("grid") // 2


def validity():
    _, core, chip, chips = position()
    low, high = (chip > 0).astype(f32), (chip < chips - 1).astype(f32)
    near = jnp.where(core == 0, low, high)
    far = jnp.where(core == 0, high, low)
    return near, far


def row_validity(i, near, far):
    return jnp.where(i < 4, near, jnp.where(i < 8, 1.0, far))


def part(n):
    return pl.ds(SUB * n, SUB)


def coordinates():
    s = lax.broadcasted_iota(jnp.int32, (SUB, NZ), 0)
    z = lax.broadcasted_iota(jnp.int32, (SUB, NZ), 1)
    return s, z


def coefficients(cond, kx, ky, kz, keep):
    s, z = coordinates()
    z_ends = jnp.where((z == 0) | (z == NZ - 1), WZ, 0.0)
    first_ends = z_ends + jnp.where(s == 0, WX, 0.0)
    last_ends = z_ends + jnp.where(s == SUB - 1, WX, 0.0)
    z_inside = jnp.where(z < NZ - 1, WZ, 0.0)
    s_inside = jnp.where(s < SUB - 1, WX, 0.0)

    def row(i, carry):
        c = [cond[i, part(n)] for n in range(BLOCKS)]
        for n in range(BLOCKS):
            kx[i, part(n)] = WX * (c[n] + cond[i + 1, part(n)])
            if n < BLOCKS - 1:
                ky[i, part(n)] = WX * (c[n] + c[n + 1])
            else:
                ky[i, part(n)] = s_inside * (c[n] + pltpu.roll(c[0], SUB - 1, 0))
            kz[i, part(n)] = z_inside * (c[n] + pltpu.roll(c[n], NZ - 1, 1))
            ends = first_ends if n == 0 else (last_ends if n == BLOCKS - 1 else z_ends)
            keep[i, part(n)] = 1.0 - ends * c[n]
        return carry

    kx[0] = WX * (cond[0] + cond[1])
    lax.fori_loop(1, EXT - 1, row, 0)


def advance(src, dst, first, last, coefs, load, near, far):
    kx, ky, kz, keep = coefs

    def row(i, below):
        inside = row_validity(i, near, far)
        u = [src[i, part(n)] for n in range(BLOCKS)]
        wrap = ky[i, part(BLOCKS - 1)] * (pltpu.roll(u[0], SUB - 1, 0) - u[-1])
        left = pltpu.roll(wrap, 1, 0)
        above = []
        for n in range(BLOCKS):
            across = kx[i, part(n)] * (src[i + 1, part(n)] - u[n])
            right = ky[i, part(n)] * (u[n + 1] - u[n]) if n < BLOCKS - 1 else wrap
            side = kz[i, part(n)] * (pltpu.roll(u[n], NZ - 1, 1) - u[n])
            new = keep[i, part(n)] * u[n] + (across - below[n])
            new += (right - left) + (side - pltpu.roll(side, 1, 1))
            if load is not None:
                new += load[i, part(n)]
            dst[i, part(n)] = new * inside
            left = right
            above.append(across)
        return tuple(above)

    i = first - 1
    start = tuple(
        kx[i, part(n)] * (src[i + 1, part(n)] - src[i, part(n)]) for n in range(BLOCKS)
    )
    lax.fori_loop(first, last + 1, row, start)


def parts_of(values, count):
    parts = []
    for _ in range(count):
        part = values.astype(bf16).astype(f32)
        parts.append(part)
        values = values - part
    return parts


def stacked_rows(parts):
    row = lax.broadcasted_iota(jnp.int32, (16, parts[0].shape[1]), 0)
    out = jnp.zeros(row.shape, f32)
    for number, part in enumerate(parts):
        out = jnp.where(row == number, part, out)
    return out.astype(bf16)


def hot(index, count):
    return lax.broadcasted_iota(jnp.int32, (count, index.shape[1]), 0) == index


def as_bf16(mask):
    return jnp.where(mask, 1.0, 0.0).astype(bf16)


def duct_lists(duct, base, flip):
    cells = jnp.concatenate([duct[base : base + 8], duct[base + 8 : base + 16]], axis=1)
    cells = cells.astype(jnp.int32)
    if flip:
        cells = cells ^ (NY * NZ)
    extra = duct[base + 16 : base + 24]
    segment = jnp.concatenate([extra[0:1], extra[1:2]], axis=1).astype(jnp.int32)
    return cells >> 7, cells & (NZ - 1), segment


def pack_kernel(
    log_cond, opening, heat, cells, segment, measured, full, near,
    rows_v, cells_v, segment_v, measured_v, sems,
):
    g, core, _, _ = position()
    copies = []

    def copy(src, dst):
        copies.append(pltpu.make_async_copy(src, dst, sems.at[len(copies)]))
        copies[-1].start()

    targets = []
    for r in range(2):
        at = r ^ core
        sources = (
            (opening.at[0, at], U0 + r * NY),
            (log_cond.at[at], C0 + r * NY),
            (heat.at[0, at], Q1 if r else Q0),
        )
        for src, base in sources:
            copy(src, rows_v.at[len(targets)])
            targets.append(base)
    copy(cells, cells_v)
    copy(segment, segment_v)
    copy(measured, measured_v)
    for each in copies:
        each.wait()
    for number, base in enumerate(targets):
        for n in range(BLOCKS):
            vector = rows_v[number, pl.ds(n, SUB, stride=BLOCKS)]
            full[pl.ds(base + SUB * n, SUB)] = vector
            if base >= NY:
                near[pl.ds(base - NY + SUB * n, SUB)] = vector
    cell = cells_v[...] ^ (core * NY * NZ)
    y = (cell >> 7) & (NY - 1)
    y = (y & (BLOCKS - 1)) * SUB + (y >> 4)
    moved = ((cell & (NY * NZ)) + y * NZ + (cell & (NZ - 1))).astype(f32)
    lane = lax.broadcasted_iota(jnp.int32, (8, 128), 1)
    row = lax.broadcasted_iota(jnp.int32, (8, 128), 0)
    seg = segment_v[...].astype(f32)
    extra = jnp.where(row == 0, seg[:, :128], jnp.where(row == 1, seg[:, 128:], 0.0))
    for n in range(measured.shape[1]):
        mine = (row == 2) & (lane == measured.shape[1] * g + n)
        extra = jnp.where(mine, measured_v[0:1, n : n + 1], extra)
    for out, skip in ((full, 0), (near, NY)):
        out[pl.ds(D0 - skip, 8)] = moved[:, :128]
        out[pl.ds(D0 - skip + 8, 8)] = moved[:, 128:]
        out[pl.ds(D0 - skip + 16, 8)] = extra


def write_hots(duct, base, flip, j, at_rows, at_lanes, at_segments):
    rows, lanes, segment = duct_lists(duct, base, flip)
    for c in range(8):
        at = pl.ds(256 * c, 256)
        at_rows[j, :, at] = as_bf16(hot(rows[c : c + 1], CELLS))
        at_lanes[j, :, at] = as_bf16(hot(lanes[c : c + 1], NZ))
    if at_segments is not None:
        at_segments[j] = as_bf16(hot(segment, 128))


def prepare_own_kernel(own, at_rows, at_lanes, at_segments):
    write_hots(own, D0, False, 0, at_rows, at_lanes, at_segments)


def prepare_far_kernel(far1, far2, at_rows, at_lanes, at_segments):
    write_hots(far1, D0, True, 0, at_rows, at_lanes, at_segments)
    write_hots(far2, D0, False, 1, at_rows, at_lanes, at_segments)


def prepare_near_kernel(near2, far_segments, at_segments):
    _, _, segment = duct_lists(near2, D0 - NY, False)
    at_segments[0] = as_bf16(hot(segment, 128))


def slab_rows(near2, near1, own, far1, far2):
    out = []
    for j, slab in enumerate((near2, near1, own, far1, far2)):
        for r in range(2):
            out.append((slab, NY if j == 0 else 0, 1 - r if j in (1, 3) else r))
    return out


def forward_kernel(
    near2, near1, own, far1, far2, at_rows, at_lanes, at_segments,
    temp, sums, cond, kx, ky, kz, keep, load,
):
    near, far = validity()
    for i, (slab, skip, r) in enumerate(slab_rows(near2, near1, own, far1, far2)):
        valid = near if i < 4 else (far if i > 7 else 1.0)
        temp[0, i] = slab[pl.ds(U0 - skip + r * NY, NY)]
        cond[i] = jnp.exp(slab[pl.ds(C0 - skip + r * NY, NY)]) * valid
        if 1 <= i <= 8:
            load[i] = DT * slab[pl.ds((Q1 - skip) if r else Q0, NY)]
    coefs = (kx, ky, kz, keep)
    coefficients(cond, *coefs)
    for k in range(STEPS):
        advance(temp.at[k], temp.at[k + 1], k + 1, 8 - k, coefs, load, near, far)

    across = jnp.concatenate([temp[STEPS, 4].T, temp[STEPS, 5].T], axis=1)
    stack = jnp.concatenate([part.astype(bf16) for part in parts_of(across, 3)], axis=0)
    picked = jnp.zeros((NZ, 256), f32)
    for c in range(8):
        at = pl.ds(256 * c, 256)
        found = jnp.dot(stack, at_rows[0, :, at], preferred_element_type=f32)
        value = (found[2 * NZ :] + found[NZ : 2 * NZ]) + found[:NZ]
        picked = picked + value * at_lanes[0, :, at].astype(f32)
    partial = 0.5 * jnp.sum(picked, axis=0, keepdims=True)
    by_segment = lax.dot_general(
        stacked_rows(parts_of(partial, 3)),
        at_segments[0],
        (((1,), (1,)), ((), ())),
        preferred_element_type=f32,
    )
    total = jnp.sum(by_segment, axis=0, keepdims=True) - own[pl.ds(D0 + 16, 8)][2:3]
    sums[...] = jnp.broadcast_to(total, sums.shape)


def backward_kernel(
    near2, near1, own_rows, own_lanes, own_segments, far_rows, far_lanes, far_segments, near2_segments,
    temp, sums, cond, kx, ky, kz, keep, grad, seg,
    costate, acc, weights, near_rows, near_lanes, near_segments,
):
    g, core, _, _ = position()
    near, far = validity()
    resid = jnp.sum(sums[...], axis=0, keepdims=True)
    shift = lax.rem(128 - seg.shape[1] * g, 128)
    seg[...] = pltpu.roll(jnp.broadcast_to(resid, (8, 128)), shift, 1)[0:1, 0 : seg.shape[1]]
    stack = stacked_rows(parts_of(0.5 * resid, 3))
    write_hots(near2, D0 - NY, False, 0, near_rows, near_lanes, None)
    near_segments[0] = near2_segments[0]
    write_hots(near1, D0, True, 1, near_rows, near_lanes, near_segments)
    own, fars = (own_rows, own_lanes, own_segments), (far_rows, far_lanes, far_segments)
    nears = (near_rows, near_lanes, near_segments)
    places = ((nears, 0, near), (nears, 1, near), (own, 0, 1.0), (fars, 0, 1.0), (fars, 1, far))
    for j, ((at_rows, at_lanes, at_segments), n, valid) in enumerate(places):
        source = jnp.dot(stack, at_segments[n], preferred_element_type=f32)
        source = jnp.sum(source, axis=0, keepdims=True) * valid
        upper, lower = (part.astype(bf16) for part in parts_of(source, 2))
        for c in range(8):
            at = pl.ds(256 * c, 256)
            weights[j, 0:NZ, at] = at_lanes[n, :, at] * upper
            weights[j, NZ : 2 * NZ, at] = at_lanes[n, :, at] * lower
        out = lax.dot_general(
            at_rows[n], weights[j], (((1,), (1,)), ((), ())), preferred_element_type=f32
        )
        out = out[:, :NZ] + out[:, NZ:]
        costate[0, 2 * j] = out[:NY]
        costate[0, 2 * j + 1] = out[NY:]

    coefs = (kx, ky, kz, keep)
    for k in range(STEPS - 1):
        advance(costate.at[k], costate.at[k + 1], k + 1, 8 - k, coefs, None, near, far)
    s, z = coordinates()
    share = grad.shape[2]

    def sensitivity(i, carry):
        at = (i - 4) ^ core

        def products(n):
            across = jnp.zeros((SUB, NZ), f32)
            right, side, own = across, across, across
            for k in range(STEPS):
                u, a = temp.at[k], costate.at[STEPS - 1 - k]
                uc, ac = u[i, part(n)], a[i, part(n)]
                across += (uc - u[i + 1, part(n)]) * (ac - a[i + 1, part(n)])
                across += (uc - u[i - 1, part(n)]) * (ac - a[i - 1, part(n)])
                if n < BLOCKS - 1:
                    ur, ar = u[i, part(n + 1)], a[i, part(n + 1)]
                else:
                    ur = jnp.where(s < SUB - 1, pltpu.roll(u[i, part(0)], SUB - 1, 0), 0.0)
                    ar = jnp.where(s < SUB - 1, pltpu.roll(a[i, part(0)], SUB - 1, 0), 0.0)
                right += (ur - uc) * (ar - ac)
                us = jnp.where(z < NZ - 1, pltpu.roll(uc, NZ - 1, 1), 0.0)
                az = jnp.where(z < NZ - 1, pltpu.roll(ac, NZ - 1, 1), 0.0)
                side += (us - uc) * (az - ac)
                own += uc * ac
            side += jnp.where(z > 0, pltpu.roll(side, 1, 1), own)
            return across + 0.5 * side, right, own

        last, last_right, _ = products(BLOCKS - 1)
        left = None
        for n in range(BLOCKS):
            total, right, own = products(n) if n < BLOCKS - 1 else (last, last_right, None)
            if n == 0:
                left = jnp.where(s > 0, pltpu.roll(last_right, 1, 0), own)
            acc[pl.ds(n, SUB, stride=BLOCKS)] = (-WX) * cond[i, part(n)] * (total + (right + left))
            left = right
        for n in range(NY // share):
            grad[n, at] = acc[pl.ds(n * share, share)]
        return carry

    lax.fori_loop(4, 6, sensitivity, 0)


def field(*lead):
    return (*lead, NY, NZ)


def in_hbm(values):
    return pltpu.with_memory_space_constraint(values, pltpu.HBM)


def local(log_cond, opening_increase, heat_load, measured, duct_cells, duct_segment):
    grid = lax.axis_size("grid")
    tests = lax.axis_size("tests")
    vmem = pl.BlockSpec(memory_space=pltpu.VMEM)
    params = pltpu.CompilerParams(vmem_limit_bytes=24 * 1024 * 1024)
    pack, pack_near = pl.pallas_call(
        pack_kernel,
        out_shape=(pltpu.VMEM((PACK, NZ), f32), pltpu.VMEM((PACK - NY, NZ), f32)),
        in_specs=[pl.BlockSpec(memory_space=pltpu.HBM)] * 6,
        out_specs=(vmem, vmem),
        scratch_shapes=[
            pltpu.VMEM(field(6), f32),
            pltpu.VMEM((8, 256), jnp.int32),
            pltpu.VMEM((1, 256), jnp.int32),
            pltpu.VMEM(measured.shape, f32),
            pltpu.SemaphoreType.DMA((9,)),
        ],
        compiler_params=params,
        name="pack",
    )(*map(in_hbm, (log_cond, opening_increase, heat_load, duct_cells.T, duct_segment.T, measured)))
    to_far = [(s, s - 2) for s in range(2, grid, 2)] + [(s, s + 2) for s in range(1, grid - 2, 2)]
    to_near = [(s, s + 2) for s in range(0, grid - 2, 2)] + [(s, s - 2) for s in range(3, grid, 2)]
    swap = [(s, s ^ 1) for s in range(grid)]
    far2 = lax.ppermute(pack, "grid", to_far)
    far1 = lax.ppermute(pack, "grid", swap)
    near2 = lax.ppermute(pack_near, "grid", to_near)

    def hots(slabs):
        return (
            pltpu.VMEM((slabs, CELLS, 2048), bf16),
            pltpu.VMEM((slabs, NZ, 2048), bf16),
            pltpu.VMEM((slabs, 128, 256), bf16),
        )

    def prepare(kernel, out_shape, name, *slabs):
        return pl.pallas_call(
            kernel,
            out_shape=out_shape,
            in_specs=[vmem] * len(slabs),
            out_specs=(vmem,) * len(out_shape),
            compiler_params=params,
            cost_estimate=pl.CostEstimate(flops=COST_ESTIMATE, bytes_accessed=4_000_000, transcendentals=0),
            name=name,
        )(*slabs)

    own_hots = prepare(prepare_own_kernel, hots(1), "prepare_own", pack)
    far2, *own_hots = lax.optimization_barrier((far2, *own_hots))
    near1 = lax.ppermute(far2, "grid", swap)
    far_hots = prepare(prepare_far_kernel, hots(2), "prepare_far", far1, far2)
    near_hots = prepare(prepare_near_kernel, hots(1)[2:], "prepare_near", near2, far_hots[2])
    near2, near_hots, far_hots = lax.optimization_barrier((near2, near_hots, far_hots))
    packs = (near2, near1, pack, far1, far2)
    coefs = [field(EXT)] * 5
    temp, sums, *coefs = pl.pallas_call(
        forward_kernel,
        out_shape=tuple(pltpu.VMEM(shape, f32) for shape in (field(STEPS + 1, EXT), (grid, 128), *coefs)),
        in_specs=[vmem] * 8,
        out_specs=(vmem,) * 7,
        scratch_shapes=[pltpu.VMEM(field(EXT), f32)],
        compiler_params=params,
        name="forward",
    )(*packs, *own_hots)
    sums = lax.all_to_all(sums, "grid", split_axis=0, concat_axis=0, tiled=True)
    share = NY // tests
    grad, seg = pl.pallas_call(
        backward_kernel,
        out_shape=(
            pltpu.VMEM((tests, 2, share, NZ), f32),
            jax.ShapeDtypeStruct(measured.shape, f32),
        ),
        in_specs=[vmem] * 16,
        out_specs=(vmem, vmem),
        scratch_shapes=[
            pltpu.VMEM(field(STEPS, EXT), f32),
            pltpu.VMEM((NY, NZ), f32),
            pltpu.VMEM((5, CELLS, 2048), bf16),
            *hots(2),
        ],
        compiler_params=params,
        name="backward",
    )(near2, near1, *own_hots, *far_hots, *near_hots, temp, sums, *coefs)
    grad = lax.all_to_all(grad, "tests", split_axis=0, concat_axis=0, tiled=True)
    return jnp.sum(grad, axis=0), seg


def solution(mesh):
    in_specs = (
        P("grid", None, None),
        P("tests", "grid", None, None),
        P("tests", "grid", None, None),
        P("tests", "grid"),
        P("grid", None),
        P("grid", None),
    )
    out_specs = (P("grid", "tests", None), P("tests", "grid"))
    return jax.shard_map(local, mesh=mesh, in_specs=in_specs, out_specs=out_specs, check_vma=False)
```

```python
import jax
import jax.numpy as jnp
from jax import lax
from jax.experimental import pallas as pl
from jax.experimental.pallas import tpu as pltpu
from jax.sharding import PartitionSpec as P

STEPS = 4
DT = 0.08
WX = 0.5 * DT
WZ = 0.25 * DT
NY = 128
NZ = 128
CELLS = 2 * NY
EXT = 10
SUB = 8
BLOCKS = NY // SUB
Q0 = 0
U0 = NY
C0 = U0 + CELLS
D0 = C0 + CELLS
Q1 = D0 + 24
PACK = Q1 + NY
COST_ESTIMATE = 2_000_000_000
bf16 = jnp.bfloat16
f32 = jnp.float32


def position():
    g = lax.axis_index("grid")
    return g, lax.rem(g, 2), lax.div(g, 2), lax.axis_size("grid") // 2


def validity():
    _, core, chip, chips = position()
    low, high = (chip > 0).astype(f32), (chip < chips - 1).astype(f32)
    near = jnp.where(core == 0, low, high)
    far = jnp.where(core == 0, high, low)
    return near, far


def row_validity(i, near, far):
    return jnp.where(i < 4, near, jnp.where(i < 8, 1.0, far))


def part(n):
    return pl.ds(SUB * n, SUB)


def coordinates():
    s = lax.broadcasted_iota(jnp.int32, (SUB, NZ), 0)
    z = lax.broadcasted_iota(jnp.int32, (SUB, NZ), 1)
    return s, z


def coefficients(cond, kx, ky, kzp, kzm, keep):
    s, z = coordinates()
    z_above, z_below = jnp.where(z < NZ - 1, WZ, 0.0), jnp.where(z > 0, WZ, 0.0)
    s_inside = jnp.where(s < SUB - 1, WX, 0.0)
    first_end, last_end = jnp.where(s == 0, WX, 0.0), jnp.where(s == SUB - 1, WX, 0.0)

    def rows(b, carry):
        first = 1 + 2 * b
        for i in (first, first + 1):
            c = [cond[i, part(n)] for n in range(BLOCKS)]
            for n in range(BLOCKS):
                kx[i, part(n)] = WX * (c[n] + cond[i + 1, part(n)])
                if n < BLOCKS - 1:
                    ky[i, part(n)] = WX * (c[n] + c[n + 1])
                else:
                    ky[i, part(n)] = s_inside * (c[n] + pltpu.roll(c[0], SUB - 1, 0))
                above = z_above * (c[n] + pltpu.roll(c[n], NZ - 1, 1))
                below = z_below * (c[n] + pltpu.roll(c[n], 1, 1))
                kzp[i, part(n)], kzm[i, part(n)] = above, below
                ends = jnp.where((z == 0) | (z == NZ - 1), WZ, 0.0)
                if n == 0:
                    ends = ends + first_end
                elif n == BLOCKS - 1:
                    ends = ends + last_end
                keep[i, part(n)] = 1.0 - ((above + below) + ends * c[n])
        return carry

    kx[0] = WX * (cond[0] + cond[1])
    lax.fori_loop(0, EXT // 2 - 1, rows, 0)


def advance(src, dst, first, last, coefs, load, near, far):
    kx, ky, kzp, kzm, keep = coefs
    count = last - first + 1
    group = 3 if count % 3 == 0 else min(count, 4)

    def rows(b, carry):
        base = first + group * b
        places = range(group)
        inside = [row_validity(base + r, near, far) for r in places]
        u = [src[base + r, part(0)] for r in places]
        wrap = [
            ky[base + r, part(BLOCKS - 1)]
            * (pltpu.roll(u[r], SUB - 1, 0) - src[base + r, part(BLOCKS - 1)])
            for r in places
        ]
        left = [pltpu.roll(each, 1, 0) for each in wrap]
        for n in range(BLOCKS):
            below = kx[base - 1, part(n)] * (u[0] - src[base - 1, part(n)])
            following = wrap
            for r in places:
                i = base + r
                beyond = u[r + 1] if r < group - 1 else src[i + 1, part(n)]
                across = kx[i, part(n)] * (beyond - u[r])
                new = keep[i, part(n)] * u[r] + (across - below)
                new += kzp[i, part(n)] * pltpu.roll(u[r], NZ - 1, 1)
                new += kzm[i, part(n)] * pltpu.roll(u[r], 1, 1)
                if load is not None:
                    new += load[i, part(n)]
                below = across
                if n < BLOCKS - 1:
                    after = src[i, part(n + 1)]
                    right = ky[i, part(n)] * (after - u[r])
                else:
                    after, right = None, wrap[r]
                dst[i, part(n)] = (new + (right - left[r])) * inside[r]
                left[r] = right
                if r == 0:
                    following = []
                following.append(after)
            u = following
        return carry

    if group == count:
        rows(0, 0)
    else:
        lax.fori_loop(0, count // group, rows, 0)


def parts_of(values, count):
    parts = []
    for _ in range(count):
        part = values.astype(bf16).astype(f32)
        parts.append(part)
        values = values - part
    return parts


def stacked_rows(parts):
    row = lax.broadcasted_iota(jnp.int32, (16, parts[0].shape[1]), 0)
    out = jnp.zeros(row.shape, f32)
    for number, part in enumerate(parts):
        out = jnp.where(row == number, part, out)
    return out.astype(bf16)


def hot(index, count):
    return lax.broadcasted_iota(jnp.int32, (count, index.shape[1]), 0) == index


def as_bf16(mask):
    return jnp.where(mask, 1.0, 0.0).astype(bf16)


def duct_lists(duct, base, flip):
    cells = jnp.concatenate([duct[base : base + 8], duct[base + 8 : base + 16]], axis=1)
    cells = cells.astype(jnp.int32)
    if flip:
        cells = cells ^ (NY * NZ)
    extra = duct[base + 16 : base + 24]
    segment = jnp.concatenate([extra[0:1], extra[1:2]], axis=1).astype(jnp.int32)
    return cells >> 7, cells & (NZ - 1), segment


def pack_kernel(
    log_cond, opening, heat, cells, segment, measured, full, near,
    rows_v, cells_v, segment_v, measured_v, sems,
):
    g, core, _, _ = position()
    copies = []

    def copy(src, dst):
        copies.append(pltpu.make_async_copy(src, dst, sems.at[len(copies)]))
        copies[-1].start()

    targets = []
    for r in range(2):
        at = r ^ core
        sources = (
            (opening.at[0, at], U0 + r * NY),
            (log_cond.at[at], C0 + r * NY),
            (heat.at[0, at], Q1 if r else Q0),
        )
        for src, base in sources:
            copy(src, rows_v.at[len(targets)])
            targets.append(base)
    copy(cells, cells_v)
    copy(segment, segment_v)
    copy(measured, measured_v)
    for each in copies:
        each.wait()
    for number, base in enumerate(targets):
        for n in range(BLOCKS):
            vector = rows_v[number, pl.ds(n, SUB, stride=BLOCKS)]
            full[pl.ds(base + SUB * n, SUB)] = vector
            if base >= NY:
                near[pl.ds(base - NY + SUB * n, SUB)] = vector
    cell = cells_v[...] ^ (core * NY * NZ)
    y = (cell >> 7) & (NY - 1)
    y = (y & (BLOCKS - 1)) * SUB + (y >> 4)
    moved = ((cell & (NY * NZ)) + y * NZ + (cell & (NZ - 1))).astype(f32)
    lane = lax.broadcasted_iota(jnp.int32, (8, 128), 1)
    row = lax.broadcasted_iota(jnp.int32, (8, 128), 0)
    seg = segment_v[...].astype(f32)
    extra = jnp.where(row == 0, seg[:, :128], jnp.where(row == 1, seg[:, 128:], 0.0))
    for n in range(measured.shape[1]):
        mine = (row == 2) & (lane == measured.shape[1] * g + n)
        extra = jnp.where(mine, measured_v[0:1, n : n + 1], extra)
    for out, skip in ((full, 0), (near, NY)):
        out[pl.ds(D0 - skip, 8)] = moved[:, :128]
        out[pl.ds(D0 - skip + 8, 8)] = moved[:, 128:]
        out[pl.ds(D0 - skip + 16, 8)] = extra


def write_hots(duct, base, flip, j, at_rows, at_lanes, at_segments):
    rows, lanes, segment = duct_lists(duct, base, flip)
    for c in range(8):
        at = pl.ds(256 * c, 256)
        at_rows[j, :, at] = as_bf16(hot(rows[c : c + 1], CELLS))
        at_lanes[j, :, at] = as_bf16(hot(lanes[c : c + 1], NZ))
    if at_segments is not None:
        at_segments[j] = as_bf16(hot(segment, 128))


def prepare_own_kernel(own, at_rows, at_lanes, at_segments):
    write_hots(own, D0, False, 0, at_rows, at_lanes, at_segments)


def prepare_far_kernel(far1, far2, at_rows, at_lanes, at_segments):
    write_hots(far1, D0, True, 0, at_rows, at_lanes, at_segments)
    write_hots(far2, D0, False, 1, at_rows, at_lanes, at_segments)


def prepare_near_kernel(near2, far_segments, at_segments):
    _, _, segment = duct_lists(near2, D0 - NY, False)
    at_segments[0] = as_bf16(hot(segment, 128))


def slab_rows(near2, near1, own, far1, far2):
    out = []
    for j, slab in enumerate((near2, near1, own, far1, far2)):
        for r in range(2):
            out.append((slab, NY if j == 0 else 0, 1 - r if j in (1, 3) else r))
    return out


def forward_kernel(
    near2, near1, own, far1, far2, at_rows, at_lanes, at_segments,
    temp0, temp1, temp2, temp3, temp4, cond, kx, ky, kzp, kzm, keep, sums, load,
):
    near, far = validity()
    temp = (temp0, temp1, temp2, temp3, temp4)
    for i, (slab, skip, r) in enumerate(slab_rows(near2, near1, own, far1, far2)):
        valid = near if i < 4 else (far if i > 7 else 1.0)
        temp0[i] = slab[pl.ds(U0 - skip + r * NY, NY)]
        cond[i] = jnp.exp(slab[pl.ds(C0 - skip + r * NY, NY)]) * valid
        if 1 <= i <= 8:
            load[i] = DT * slab[pl.ds((Q1 - skip) if r else Q0, NY)]
    coefs = (kx, ky, kzp, kzm, keep)
    coefficients(cond, *coefs)
    for k in range(STEPS):
        advance(temp[k], temp[k + 1], k + 1, 8 - k, coefs, load, near, far)

    across = jnp.concatenate([temp4[4].T, temp4[5].T], axis=1)
    stack = jnp.concatenate([part.astype(bf16) for part in parts_of(across, 3)], axis=0)
    picked = jnp.zeros((NZ, 256), f32)
    for c in range(8):
        at = pl.ds(256 * c, 256)
        found = jnp.dot(stack, at_rows[0, :, at], preferred_element_type=f32)
        value = (found[2 * NZ :] + found[NZ : 2 * NZ]) + found[:NZ]
        picked = picked + value * at_lanes[0, :, at].astype(f32)
    partial = 0.5 * jnp.sum(picked, axis=0, keepdims=True)
    by_segment = lax.dot_general(
        stacked_rows(parts_of(partial, 3)),
        at_segments[0],
        (((1,), (1,)), ((), ())),
        preferred_element_type=f32,
    )
    total = jnp.sum(by_segment, axis=0, keepdims=True) - own[pl.ds(D0 + 16, 8)][2:3]
    sums[...] = jnp.broadcast_to(total, sums.shape)


def backward_kernel(
    near2, near1, own_rows, own_lanes, own_segments, far_rows, far_lanes, far_segments, near2_segments,
    sums, temp0, temp1, temp2, temp3, cond, kx, ky, kzp, kzm, keep, grad, seg,
    costate4, costate3, costate2, costate1, acc, weights, near_rows, near_lanes, near_segments,
):
    g, core, _, _ = position()
    near, far = validity()
    temp, costate = (temp0, temp1, temp2, temp3), (costate4, costate3, costate2, costate1)
    resid = jnp.sum(sums[...], axis=0, keepdims=True)
    shift = lax.rem(128 - seg.shape[1] * g, 128)
    seg[...] = pltpu.roll(jnp.broadcast_to(resid, (8, 128)), shift, 1)[0:1, 0 : seg.shape[1]]
    stack = stacked_rows(parts_of(0.5 * resid, 3))
    write_hots(near2, D0 - NY, False, 0, near_rows, near_lanes, None)
    near_segments[0] = near2_segments[0]
    write_hots(near1, D0, True, 1, near_rows, near_lanes, near_segments)
    own, fars = (own_rows, own_lanes, own_segments), (far_rows, far_lanes, far_segments)
    nears = (near_rows, near_lanes, near_segments)
    places = ((nears, 0, near), (nears, 1, near), (own, 0, 1.0), (fars, 0, 1.0), (fars, 1, far))
    for j, ((at_rows, at_lanes, at_segments), n, valid) in enumerate(places):
        source = jnp.dot(stack, at_segments[n], preferred_element_type=f32)
        source = jnp.sum(source, axis=0, keepdims=True) * valid
        upper, lower = (part.astype(bf16) for part in parts_of(source, 2))
        for c in range(8):
            at = pl.ds(256 * c, 256)
            weights[j, 0:NZ, at] = at_lanes[n, :, at] * upper
            weights[j, NZ : 2 * NZ, at] = at_lanes[n, :, at] * lower
        out = lax.dot_general(
            at_rows[n], weights[j], (((1,), (1,)), ((), ())), preferred_element_type=f32
        )
        out = out[:, :NZ] + out[:, NZ:]
        costate4[2 * j] = out[:NY]
        costate4[2 * j + 1] = out[NY:]

    coefs = (kx, ky, kzp, kzm, keep)
    for k in range(STEPS - 1):
        advance(costate[k], costate[k + 1], k + 1, 8 - k, coefs, None, near, far)
    s, z = coordinates()
    share = grad.shape[2]

    def sensitivity(i, carry):
        at = (i - 4) ^ core

        def products(n):
            across = jnp.zeros((SUB, NZ), f32)
            right, side, own = across, across, across
            for k in range(STEPS):
                u, a = temp[k], costate[STEPS - 1 - k]
                uc, ac = u[i, part(n)], a[i, part(n)]
                across += (uc - u[i + 1, part(n)]) * (ac - a[i + 1, part(n)])
                across += (uc - u[i - 1, part(n)]) * (ac - a[i - 1, part(n)])
                if n < BLOCKS - 1:
                    ur, ar = u[i, part(n + 1)], a[i, part(n + 1)]
                else:
                    ur = jnp.where(s < SUB - 1, pltpu.roll(u[i, part(0)], SUB - 1, 0), 0.0)
                    ar = jnp.where(s < SUB - 1, pltpu.roll(a[i, part(0)], SUB - 1, 0), 0.0)
                right += (ur - uc) * (ar - ac)
                us = jnp.where(z < NZ - 1, pltpu.roll(uc, NZ - 1, 1), 0.0)
                az = jnp.where(z < NZ - 1, pltpu.roll(ac, NZ - 1, 1), 0.0)
                side += (us - uc) * (az - ac)
                own += uc * ac
            side += jnp.where(z > 0, pltpu.roll(side, 1, 1), own)
            return across + 0.5 * side, right, own

        last, last_right, _ = products(BLOCKS - 1)
        left = None
        for n in range(BLOCKS):
            total, right, own = products(n) if n < BLOCKS - 1 else (last, last_right, None)
            if n == 0:
                left = jnp.where(s > 0, pltpu.roll(last_right, 1, 0), own)
            acc[pl.ds(n, SUB, stride=BLOCKS)] = (-WX) * cond[i, part(n)] * (total + (right + left))
            left = right
        for n in range(NY // share):
            grad[n, at] = acc[pl.ds(n * share, share)]
        return carry

    lax.fori_loop(4, 6, sensitivity, 0)


def field(*lead):
    return (*lead, NY, NZ)


def in_hbm(values):
    return pltpu.with_memory_space_constraint(values, pltpu.HBM)


def local(log_cond, opening_increase, heat_load, measured, duct_cells, duct_segment):
    grid = lax.axis_size("grid")
    tests = lax.axis_size("tests")
    vmem = pl.BlockSpec(memory_space=pltpu.VMEM)
    params = pltpu.CompilerParams(vmem_limit_bytes=24 * 1024 * 1024)
    pack, pack_near = pl.pallas_call(
        pack_kernel,
        out_shape=(pltpu.VMEM((PACK, NZ), f32), pltpu.VMEM((PACK - NY, NZ), f32)),
        in_specs=[pl.BlockSpec(memory_space=pltpu.HBM)] * 6,
        out_specs=(vmem, vmem),
        scratch_shapes=[
            pltpu.VMEM(field(6), f32),
            pltpu.VMEM((8, 256), jnp.int32),
            pltpu.VMEM((1, 256), jnp.int32),
            pltpu.VMEM(measured.shape, f32),
            pltpu.SemaphoreType.DMA((9,)),
        ],
        compiler_params=params,
        name="pack",
    )(*map(in_hbm, (log_cond, opening_increase, heat_load, duct_cells.T, duct_segment.T, measured)))
    to_far = [(s, s - 2) for s in range(2, grid, 2)] + [(s, s + 2) for s in range(1, grid - 2, 2)]
    to_near = [(s, s + 2) for s in range(0, grid - 2, 2)] + [(s, s - 2) for s in range(3, grid, 2)]
    swap = [(s, s ^ 1) for s in range(grid)]
    far2 = lax.ppermute(pack, "grid", to_far)
    far1 = lax.ppermute(pack, "grid", swap)
    near2 = lax.ppermute(pack_near, "grid", to_near)

    def hots(slabs):
        return (
            pltpu.VMEM((slabs, CELLS, 2048), bf16),
            pltpu.VMEM((slabs, NZ, 2048), bf16),
            pltpu.VMEM((slabs, 128, 256), bf16),
        )

    def prepare(kernel, out_shape, name, *slabs):
        return pl.pallas_call(
            kernel,
            out_shape=out_shape,
            in_specs=[vmem] * len(slabs),
            out_specs=(vmem,) * len(out_shape),
            compiler_params=params,
            cost_estimate=pl.CostEstimate(flops=COST_ESTIMATE, bytes_accessed=4_000_000, transcendentals=0),
            name=name,
        )(*slabs)

    own_hots = prepare(prepare_own_kernel, hots(1), "prepare_own", pack)
    far2, *own_hots = lax.optimization_barrier((far2, *own_hots))
    near1 = lax.ppermute(far2, "grid", swap)
    far_hots = prepare(prepare_far_kernel, hots(2), "prepare_far", far1, far2)
    near_hots = prepare(prepare_near_kernel, hots(1)[2:], "prepare_near", near2, far_hots[2])
    near2, near_hots, far_hots = lax.optimization_barrier((near2, near_hots, far_hots))
    packs = (near2, near1, pack, far1, far2)
    coefs = [field(EXT)] * 6
    levels = [field(EXT)] * (STEPS + 1)
    *results, sums = pl.pallas_call(
        forward_kernel,
        out_shape=tuple(pltpu.VMEM(shape, f32) for shape in (*levels, *coefs, (grid, 128))),
        in_specs=[vmem] * 8,
        out_specs=(vmem,) * 12,
        scratch_shapes=[pltpu.VMEM(field(EXT), f32)],
        compiler_params=params,
        name="forward",
    )(*packs, *own_hots)
    sums = lax.all_to_all(sums, "grid", split_axis=0, concat_axis=0, tiled=True)
    share = NY // tests
    grad, seg = pl.pallas_call(
        backward_kernel,
        out_shape=(
            pltpu.VMEM((tests, 2, share, NZ), f32),
            jax.ShapeDtypeStruct(measured.shape, f32),
        ),
        in_specs=[vmem] * 20,
        out_specs=(vmem, vmem),
        scratch_shapes=[
            *[pltpu.VMEM(field(EXT), f32)] * STEPS,
            pltpu.VMEM((NY, NZ), f32),
            pltpu.VMEM((5, CELLS, 2048), bf16),
            *hots(2),
        ],
        compiler_params=params,
        name="backward",
    )(near2, near1, *own_hots, *far_hots, *near_hots, sums, *results[:STEPS], *results[STEPS + 1 :])
    grad = lax.all_to_all(grad, "tests", split_axis=0, concat_axis=0, tiled=True)
    return jnp.sum(grad, axis=0), seg


def solution(mesh):
    in_specs = (
        P("grid", None, None),
        P("tests", "grid", None, None),
        P("tests", "grid", None, None),
        P("tests", "grid"),
        P("grid", None),
        P("grid", None),
    )
    out_specs = (P("grid", "tests", None), P("tests", "grid"))
    return jax.shard_map(local, mesh=mesh, in_specs=in_specs, out_specs=out_specs, check_vma=False)
```

```python
import jax
import jax.numpy as jnp
from jax import lax
from jax.experimental import pallas as pl
from jax.experimental.pallas import tpu as pltpu
from jax.sharding import PartitionSpec as P

STEPS = 4
DT = 0.08
WX = 0.5 * DT
WZ = 0.25 * DT
NY = 128
NZ = 128
CELLS = 2 * NY
EXT = 10
SUB = 8
BLOCKS = NY // SUB
Q0 = 0
U0 = NY
C0 = U0 + CELLS
D0 = C0 + CELLS
Q1 = D0 + 24
PACK = Q1 + NY
PARTLY = NY
NEAR_C0 = 2 * NY
NEAR_D0 = 4 * NY
NEAR_PACK = NEAR_D0 + 24
COST_ESTIMATE = 2_000_000_000
bf16 = jnp.bfloat16
f32 = jnp.float32


def position():
    g = lax.axis_index("grid")
    return g, lax.rem(g, 2), lax.div(g, 2), lax.axis_size("grid") // 2


def validity():
    _, core, chip, chips = position()
    low, high = (chip > 0).astype(f32), (chip < chips - 1).astype(f32)
    near = jnp.where(core == 0, low, high)
    far = jnp.where(core == 0, high, low)
    return near, far


def row_validity(i, near, far):
    return jnp.where(i < 4, near, jnp.where(i < 8, 1.0, far))


def part(n):
    return pl.ds(SUB * n, SUB)


def coordinates():
    s = lax.broadcasted_iota(jnp.int32, (SUB, NZ), 0)
    z = lax.broadcasted_iota(jnp.int32, (SUB, NZ), 1)
    return s, z


def coefficients(cond, kx, ky, kzp, kzm, keep):
    s, z = coordinates()
    z_above, z_below = jnp.where(z < NZ - 1, WZ, 0.0), jnp.where(z > 0, WZ, 0.0)
    s_inside = jnp.where(s < SUB - 1, WX, 0.0)
    first_end, last_end = jnp.where(s == 0, WX, 0.0), jnp.where(s == SUB - 1, WX, 0.0)

    def rows(b, carry):
        first = 1 + 2 * b
        for i in (first, first + 1):
            c = [cond[i, part(n)] for n in range(BLOCKS)]
            for n in range(BLOCKS):
                kx[i, part(n)] = WX * (c[n] + cond[i + 1, part(n)])
                if n < BLOCKS - 1:
                    ky[i, part(n)] = WX * (c[n] + c[n + 1])
                else:
                    ky[i, part(n)] = s_inside * (c[n] + pltpu.roll(c[0], SUB - 1, 0))
                above = z_above * (c[n] + pltpu.roll(c[n], NZ - 1, 1))
                below = z_below * (c[n] + pltpu.roll(c[n], 1, 1))
                kzp[i, part(n)], kzm[i, part(n)] = above, below
                ends = jnp.where((z == 0) | (z == NZ - 1), WZ, 0.0)
                if n == 0:
                    ends = ends + first_end
                elif n == BLOCKS - 1:
                    ends = ends + last_end
                keep[i, part(n)] = 1.0 - ((above + below) + ends * c[n])
        return carry

    kx[0] = WX * (cond[0] + cond[1])
    lax.fori_loop(0, EXT // 2 - 1, rows, 0)


def advance(src, dst, first, last, coefs, load, near, far):
    kx, ky, kzp, kzm, keep = coefs
    count = last - first + 1
    group = 3 if count % 3 == 0 else min(count, 4)

    def rows(b, carry):
        base = first + group * b
        places = range(group)
        inside = [row_validity(base + r, near, far) for r in places]
        u = [src[base + r, part(0)] for r in places]
        wrap = [
            ky[base + r, part(BLOCKS - 1)]
            * (pltpu.roll(u[r], SUB - 1, 0) - src[base + r, part(BLOCKS - 1)])
            for r in places
        ]
        left = [pltpu.roll(each, 1, 0) for each in wrap]
        for n in range(BLOCKS):
            below = kx[base - 1, part(n)] * (u[0] - src[base - 1, part(n)])
            following = wrap
            for r in places:
                i = base + r
                beyond = u[r + 1] if r < group - 1 else src[i + 1, part(n)]
                across = kx[i, part(n)] * (beyond - u[r])
                new = keep[i, part(n)] * u[r] + (across - below)
                new += kzp[i, part(n)] * pltpu.roll(u[r], NZ - 1, 1)
                new += kzm[i, part(n)] * pltpu.roll(u[r], 1, 1)
                if load is not None:
                    new += load[i, part(n)]
                below = across
                if n < BLOCKS - 1:
                    after = src[i, part(n + 1)]
                    right = ky[i, part(n)] * (after - u[r])
                else:
                    after, right = None, wrap[r]
                dst[i, part(n)] = (new + (right - left[r])) * inside[r]
                left[r] = right
                if r == 0:
                    following = []
                following.append(after)
            u = following
        return carry

    if group == count:
        rows(0, 0)
    else:
        lax.fori_loop(0, count // group, rows, 0)


def parts_of(values, count):
    parts = []
    for _ in range(count):
        part = values.astype(bf16).astype(f32)
        parts.append(part)
        values = values - part
    return parts


def stacked_rows(parts):
    row = lax.broadcasted_iota(jnp.int32, (16, parts[0].shape[1]), 0)
    out = jnp.zeros(row.shape, f32)
    for number, part in enumerate(parts):
        out = jnp.where(row == number, part, out)
    return out.astype(bf16)


def hot(index, count):
    return lax.broadcasted_iota(jnp.int32, (count, index.shape[1]), 0) == index


def as_bf16(mask):
    return jnp.where(mask, 1.0, 0.0).astype(bf16)


def duct_lists(duct, base, flip):
    cells = jnp.concatenate([duct[base : base + 8], duct[base + 8 : base + 16]], axis=1)
    cells = cells.astype(jnp.int32)
    if flip:
        cells = cells ^ (NY * NZ)
    extra = duct[base + 16 : base + 24]
    segment = jnp.concatenate([extra[0:1], extra[1:2]], axis=1).astype(jnp.int32)
    return cells >> 7, cells & (NZ - 1), segment


def pack_kernel(
    log_cond, opening, heat, cells, segment, measured, full,
    rows_v, cells_v, segment_v, measured_v, sems,
):
    g, core, _, _ = position()
    copies = []

    def copy(src, dst):
        copies.append(pltpu.make_async_copy(src, dst, sems.at[len(copies)]))
        copies[-1].start()

    targets = []
    for r in range(2):
        at = r ^ core
        sources = (
            (opening.at[0, at], U0 + r * NY),
            (log_cond.at[at], C0 + r * NY),
            (heat.at[0, at], Q1 if r else Q0),
        )
        for src, base in sources:
            copy(src, rows_v.at[len(targets)])
            targets.append(base)
    copy(cells, cells_v)
    copy(segment, segment_v)
    copy(measured, measured_v)
    for each in copies:
        each.wait()
    for number, base in enumerate(targets):
        for n in range(BLOCKS):
            full[pl.ds(base + SUB * n, SUB)] = rows_v[number, pl.ds(n, SUB, stride=BLOCKS)]
    cell = cells_v[...] ^ (core * NY * NZ)
    y = (cell >> 7) & (NY - 1)
    y = (y & (BLOCKS - 1)) * SUB + (y >> 4)
    moved = ((cell & (NY * NZ)) + y * NZ + (cell & (NZ - 1))).astype(f32)
    lane = lax.broadcasted_iota(jnp.int32, (8, 128), 1)
    row = lax.broadcasted_iota(jnp.int32, (8, 128), 0)
    seg = segment_v[...].astype(f32)
    extra = jnp.where(row == 0, seg[:, :128], jnp.where(row == 1, seg[:, 128:], 0.0))
    for n in range(measured.shape[1]):
        mine = (row == 2) & (lane == measured.shape[1] * g + n)
        extra = jnp.where(mine, measured_v[0:1, n : n + 1], extra)
    full[D0 : D0 + 8] = moved[:, :128]
    full[D0 + 8 : D0 + 16] = moved[:, 128:]
    full[D0 + 16 : D0 + 24] = extra


def pack_near_kernel(full, near):
    s, z = coordinates()
    z_above, z_below = jnp.where(z < NZ - 1, WZ, 0.0), jnp.where(z > 0, WZ, 0.0)
    z_ends = jnp.where((z == 0) | (z == NZ - 1), WZ, 0.0)

    def at(base, n):
        return full[pl.ds(base + SUB * n, SUB)]

    def turned(last, first):
        return jnp.where(s < SUB - 1, pltpu.roll(first, SUB - 1, 0), 0.0), last

    c = [jnp.exp(at(C0 + NY, n)) for n in range(BLOCKS)]
    u = [at(U0 + NY, n) for n in range(BLOCKS)]
    c_next, c_last = turned(c[-1], c[0])
    u_next, u_last = turned(u[-1], u[0])
    top = WX * (c_last + c_next) * (u_next - u_last)
    left = jnp.where(s > 0, pltpu.roll(top, 1, 0), WX * c[0] * u[0])
    for n in range(BLOCKS):
        right = WX * (c[n] + c[n + 1]) * (u[n + 1] - u[n]) if n < BLOCKS - 1 else top
        below = WX * (c[n] + jnp.exp(at(C0, n))) * (at(U0, n) - u[n])
        kzp = z_above * (c[n] + pltpu.roll(c[n], NZ - 1, 1))
        kzm = z_below * (c[n] + pltpu.roll(c[n], 1, 1))
        side = kzp * pltpu.roll(u[n], NZ - 1, 1) + kzm * pltpu.roll(u[n], 1, 1)
        side -= (kzp + kzm + z_ends * c[n]) * u[n]
        near[pl.ds(SUB * n, SUB)] = u[n]
        near[pl.ds(PARTLY + SUB * n, SUB)] = u[n] + DT * at(Q1, n) + (below + (right - left) + side)
        left = right
    near[NEAR_C0 : NEAR_D0] = full[C0 : C0 + CELLS]
    near[NEAR_D0 : NEAR_PACK] = full[D0 : D0 + 24]


def write_hots(duct, base, flip, j, at_rows, at_lanes, at_segments):
    rows, lanes, segment = duct_lists(duct, base, flip)
    for c in range(8):
        at = pl.ds(256 * c, 256)
        at_rows[j, :, at] = as_bf16(hot(rows[c : c + 1], CELLS))
        at_lanes[j, :, at] = as_bf16(hot(lanes[c : c + 1], NZ))
    if at_segments is not None:
        at_segments[j] = as_bf16(hot(segment, 128))


def prepare_own_kernel(own, at_rows, at_lanes, at_segments):
    write_hots(own, D0, False, 0, at_rows, at_lanes, at_segments)


def prepare_far_kernel(far1, far2, at_rows, at_lanes, at_segments):
    write_hots(far1, D0, True, 0, at_rows, at_lanes, at_segments)
    write_hots(far2, D0, False, 1, at_rows, at_lanes, at_segments)


def prepare_near_kernel(near2, far_segments, at_segments):
    _, _, segment = duct_lists(near2, NEAR_D0, False)
    at_segments[0] = as_bf16(hot(segment, 128))


def forward_kernel(
    near2, near1, own, far1, far2, at_rows, at_lanes, at_segments,
    temp0, temp1, temp2, temp3, temp4, cond, kx, ky, kzp, kzm, keep, sums, load,
):
    near, far = validity()
    temp = (temp0, temp1, temp2, temp3, temp4)
    temp0[0] = jnp.zeros((NY, NZ), f32)
    load[1] = jnp.zeros((NY, NZ), f32)
    temp0[1] = near2[0:NY]
    for r in range(2):
        cond[r] = jnp.exp(near2[pl.ds(NEAR_C0 + r * NY, NY)]) * near
    for j, slab in enumerate((near1, own, far1, far2)):
        for r in range(2):
            i, at = 2 * j + 2 + r, 1 - r if j in (0, 2) else r
            temp0[i] = slab[pl.ds(U0 + at * NY, NY)]
            conductivity = jnp.exp(slab[pl.ds(C0 + at * NY, NY)])
            cond[i] = conductivity * (near, 1.0, 1.0, far)[j] if j in (0, 3) else conductivity
            if i <= 8:
                load[i] = DT * slab[pl.ds(Q1 if at else Q0, NY)]
    coefs = (kx, ky, kzp, kzm, keep)
    coefficients(cond, *coefs)
    for k in range(STEPS):
        advance(temp[k], temp[k + 1], k + 1, 8 - k, coefs, load, near, far)
        if k == 0:
            temp1[1] = near * (near2[PARTLY : PARTLY + NY] + kx[1] * (temp0[2] - temp0[1]))

    across = jnp.concatenate([temp4[4].T, temp4[5].T], axis=1)
    stack = jnp.concatenate([part.astype(bf16) for part in parts_of(across, 3)], axis=0)
    picked = jnp.zeros((NZ, 256), f32)
    for c in range(8):
        at = pl.ds(256 * c, 256)
        found = jnp.dot(stack, at_rows[0, :, at], preferred_element_type=f32)
        value = (found[2 * NZ :] + found[NZ : 2 * NZ]) + found[:NZ]
        picked = picked + value * at_lanes[0, :, at].astype(f32)
    partial = 0.5 * jnp.sum(picked, axis=0, keepdims=True)
    by_segment = lax.dot_general(
        stacked_rows(parts_of(partial, 3)),
        at_segments[0],
        (((1,), (1,)), ((), ())),
        preferred_element_type=f32,
    )
    total = jnp.sum(by_segment, axis=0, keepdims=True) - own[pl.ds(D0 + 16, 8)][2:3]
    sums[...] = jnp.broadcast_to(total, sums.shape)


def backward_kernel(
    near2, near1, own_rows, own_lanes, own_segments, far_rows, far_lanes, far_segments, near2_segments,
    sums, temp0, temp1, temp2, temp3, cond, kx, ky, kzp, kzm, keep, grad, seg,
    costate4, costate3, costate2, costate1, acc, weights, near_rows, near_lanes, near_segments,
):
    g, core, _, _ = position()
    near, far = validity()
    temp, costate = (temp0, temp1, temp2, temp3), (costate4, costate3, costate2, costate1)
    resid = jnp.sum(sums[...], axis=0, keepdims=True)
    shift = lax.rem(128 - seg.shape[1] * g, 128)
    seg[...] = pltpu.roll(jnp.broadcast_to(resid, (8, 128)), shift, 1)[0:1, 0 : seg.shape[1]]
    stack = stacked_rows(parts_of(0.5 * resid, 3))
    write_hots(near2, NEAR_D0, False, 0, near_rows, near_lanes, None)
    near_segments[0] = near2_segments[0]
    write_hots(near1, D0, True, 1, near_rows, near_lanes, near_segments)
    own, fars = (own_rows, own_lanes, own_segments), (far_rows, far_lanes, far_segments)
    nears = (near_rows, near_lanes, near_segments)
    places = ((nears, 0, near), (nears, 1, near), (own, 0, 1.0), (fars, 0, 1.0), (fars, 1, far))
    for j, ((at_rows, at_lanes, at_segments), n, valid) in enumerate(places):
        source = jnp.dot(stack, at_segments[n], preferred_element_type=f32)
        source = jnp.sum(source, axis=0, keepdims=True) * valid
        upper, lower = (part.astype(bf16) for part in parts_of(source, 2))
        for c in range(8):
            at = pl.ds(256 * c, 256)
            weights[j, 0:NZ, at] = at_lanes[n, :, at] * upper
            weights[j, NZ : 2 * NZ, at] = at_lanes[n, :, at] * lower
        out = lax.dot_general(
            at_rows[n], weights[j], (((1,), (1,)), ((), ())), preferred_element_type=f32
        )
        out = out[:, :NZ] + out[:, NZ:]
        costate4[2 * j] = out[:NY]
        costate4[2 * j + 1] = out[NY:]

    coefs = (kx, ky, kzp, kzm, keep)
    for k in range(STEPS - 1):
        advance(costate[k], costate[k + 1], k + 1, 8 - k, coefs, None, near, far)
    s, z = coordinates()
    share = grad.shape[2]

    def sensitivity(i, carry):
        at = (i - 4) ^ core

        def products(n):
            across = jnp.zeros((SUB, NZ), f32)
            right, side, own = across, across, across
            for k in range(STEPS):
                u, a = temp[k], costate[STEPS - 1 - k]
                uc, ac = u[i, part(n)], a[i, part(n)]
                across += (uc - u[i + 1, part(n)]) * (ac - a[i + 1, part(n)])
                across += (uc - u[i - 1, part(n)]) * (ac - a[i - 1, part(n)])
                if n < BLOCKS - 1:
                    ur, ar = u[i, part(n + 1)], a[i, part(n + 1)]
                else:
                    ur = jnp.where(s < SUB - 1, pltpu.roll(u[i, part(0)], SUB - 1, 0), 0.0)
                    ar = jnp.where(s < SUB - 1, pltpu.roll(a[i, part(0)], SUB - 1, 0), 0.0)
                right += (ur - uc) * (ar - ac)
                us = jnp.where(z < NZ - 1, pltpu.roll(uc, NZ - 1, 1), 0.0)
                az = jnp.where(z < NZ - 1, pltpu.roll(ac, NZ - 1, 1), 0.0)
                side += (us - uc) * (az - ac)
                own += uc * ac
            side += jnp.where(z > 0, pltpu.roll(side, 1, 1), own)
            return across + 0.5 * side, right, own

        last, last_right, _ = products(BLOCKS - 1)
        left = None
        for n in range(BLOCKS):
            total, right, own = products(n) if n < BLOCKS - 1 else (last, last_right, None)
            if n == 0:
                left = jnp.where(s > 0, pltpu.roll(last_right, 1, 0), own)
            acc[pl.ds(n, SUB, stride=BLOCKS)] = (-WX) * cond[i, part(n)] * (total + (right + left))
            left = right
        for n in range(NY // share):
            grad[n, at] = acc[pl.ds(n * share, share)]
        return carry

    lax.fori_loop(4, 6, sensitivity, 0)


def field(*lead):
    return (*lead, NY, NZ)


def in_hbm(values):
    return pltpu.with_memory_space_constraint(values, pltpu.HBM)


def local(log_cond, opening_increase, heat_load, measured, duct_cells, duct_segment):
    grid = lax.axis_size("grid")
    tests = lax.axis_size("tests")
    vmem = pl.BlockSpec(memory_space=pltpu.VMEM)
    params = pltpu.CompilerParams(vmem_limit_bytes=24 * 1024 * 1024)
    pack = pl.pallas_call(
        pack_kernel,
        out_shape=pltpu.VMEM((PACK, NZ), f32),
        in_specs=[pl.BlockSpec(memory_space=pltpu.HBM)] * 6,
        out_specs=vmem,
        scratch_shapes=[
            pltpu.VMEM(field(6), f32),
            pltpu.VMEM((8, 256), jnp.int32),
            pltpu.VMEM((1, 256), jnp.int32),
            pltpu.VMEM(measured.shape, f32),
            pltpu.SemaphoreType.DMA((9,)),
        ],
        compiler_params=params,
        name="pack",
    )(*map(in_hbm, (log_cond, opening_increase, heat_load, duct_cells.T, duct_segment.T, measured)))
    pack_near = pl.pallas_call(
        pack_near_kernel,
        out_shape=pltpu.VMEM((NEAR_PACK, NZ), f32),
        in_specs=[vmem],
        out_specs=vmem,
        compiler_params=params,
        name="pack_near",
    )(pack)
    to_far = [(s, s - 2) for s in range(2, grid, 2)] + [(s, s + 2) for s in range(1, grid - 2, 2)]
    to_near = [(s, s + 2) for s in range(0, grid - 2, 2)] + [(s, s - 2) for s in range(3, grid, 2)]
    swap = [(s, s ^ 1) for s in range(grid)]
    far2 = lax.ppermute(pack, "grid", to_far)
    far1 = lax.ppermute(pack, "grid", swap)
    near2 = lax.ppermute(pack_near, "grid", to_near)

    def hots(slabs):
        return (
            pltpu.VMEM((slabs, CELLS, 2048), bf16),
            pltpu.VMEM((slabs, NZ, 2048), bf16),
            pltpu.VMEM((slabs, 128, 256), bf16),
        )

    def prepare(kernel, out_shape, name, *slabs):
        return pl.pallas_call(
            kernel,
            out_shape=out_shape,
            in_specs=[vmem] * len(slabs),
            out_specs=(vmem,) * len(out_shape),
            compiler_params=params,
            cost_estimate=pl.CostEstimate(flops=COST_ESTIMATE, bytes_accessed=4_000_000, transcendentals=0),
            name=name,
        )(*slabs)

    own_hots = prepare(prepare_own_kernel, hots(1), "prepare_own", pack)
    far2, *own_hots = lax.optimization_barrier((far2, *own_hots))
    near1 = lax.ppermute(far2, "grid", swap)
    far_hots = prepare(prepare_far_kernel, hots(2), "prepare_far", far1, far2)
    near_hots = prepare(prepare_near_kernel, hots(1)[2:], "prepare_near", near2, far_hots[2])
    near2, near_hots, far_hots = lax.optimization_barrier((near2, near_hots, far_hots))
    packs = (near2, near1, pack, far1, far2)
    coefs = [field(EXT)] * 6
    levels = [field(EXT)] * (STEPS + 1)
    *results, sums = pl.pallas_call(
        forward_kernel,
        out_shape=tuple(pltpu.VMEM(shape, f32) for shape in (*levels, *coefs, (grid, 128))),
        in_specs=[vmem] * 8,
        out_specs=(vmem,) * 12,
        scratch_shapes=[pltpu.VMEM(field(EXT), f32)],
        compiler_params=params,
        name="forward",
    )(*packs, *own_hots)
    sums = lax.all_to_all(sums, "grid", split_axis=0, concat_axis=0, tiled=True)
    share = NY // tests
    grad, seg = pl.pallas_call(
        backward_kernel,
        out_shape=(
            pltpu.VMEM((tests, 2, share, NZ), f32),
            jax.ShapeDtypeStruct(measured.shape, f32),
        ),
        in_specs=[vmem] * 20,
        out_specs=(vmem, vmem),
        scratch_shapes=[
            *[pltpu.VMEM(field(EXT), f32)] * STEPS,
            pltpu.VMEM((NY, NZ), f32),
            pltpu.VMEM((5, CELLS, 2048), bf16),
            *hots(2),
        ],
        compiler_params=params,
        name="backward",
    )(near2, near1, *own_hots, *far_hots, *near_hots, sums, *results[:STEPS], *results[STEPS + 1 :])
    grad = lax.all_to_all(grad, "tests", split_axis=0, concat_axis=0, tiled=True)
    return jnp.sum(grad, axis=0), seg


def solution(mesh):
    in_specs = (
        P("grid", None, None),
        P("tests", "grid", None, None),
        P("tests", "grid", None, None),
        P("tests", "grid"),
        P("grid", None),
        P("grid", None),
    )
    out_specs = (P("grid", "tests", None), P("tests", "grid"))
    return jax.shard_map(local, mesh=mesh, in_specs=in_specs, out_specs=out_specs, check_vma=False)
```

```python
import jax
import jax.numpy as jnp
from jax import lax
from jax.experimental import pallas as pl
from jax.experimental.pallas import tpu as pltpu
from jax.sharding import PartitionSpec as P

STEPS = 4
DT = 0.08
WX = 0.5 * DT
WZ = 0.25 * DT
NY = 128
NZ = 128
CELLS = 2 * NY
EXT = 10
SUB = 8
BLOCKS = NY // SUB
Q0 = 0
U0 = NY
C0 = U0 + CELLS
D0 = C0 + CELLS
Q1 = D0 + 24
PACK = Q1 + NY
PARTLY = NY
NEAR_C0 = 2 * NY
NEAR_D0 = 4 * NY
NEAR_PACK = NEAR_D0 + 24
FIELDS = 10
COST_ESTIMATE = 2_000_000_000
bf16 = jnp.bfloat16
f32 = jnp.float32


def position():
    g = lax.axis_index("grid")
    return g, lax.rem(g, 2), lax.div(g, 2), lax.axis_size("grid") // 2


def validity():
    _, core, chip, chips = position()
    low, high = (chip > 0).astype(f32), (chip < chips - 1).astype(f32)
    near = jnp.where(core == 0, low, high)
    far = jnp.where(core == 0, high, low)
    return near, far


def row_validity(i, near, far):
    return jnp.where(i < 4, near, jnp.where(i < 8, 1.0, far))


def part(n):
    return pl.ds(SUB * n, SUB)


def coordinates():
    s = lax.broadcasted_iota(jnp.int32, (SUB, NZ), 0)
    z = lax.broadcasted_iota(jnp.int32, (SUB, NZ), 1)
    return s, z


def coefficients(cond, kx, ky, kzp, kzm, keep, first_row, pairs):
    s, z = coordinates()
    z_above, z_below = jnp.where(z < NZ - 1, WZ, 0.0), jnp.where(z > 0, WZ, 0.0)
    s_inside = jnp.where(s < SUB - 1, WX, 0.0)
    first_end, last_end = jnp.where(s == 0, WX, 0.0), jnp.where(s == SUB - 1, WX, 0.0)

    def rows(b, carry):
        first = first_row + 2 * b
        for i in (first, first + 1):
            c = [cond[i, part(n)] for n in range(BLOCKS)]
            for n in range(BLOCKS):
                kx[i, part(n)] = WX * (c[n] + cond[i + 1, part(n)])
                if n < BLOCKS - 1:
                    ky[i, part(n)] = WX * (c[n] + c[n + 1])
                else:
                    ky[i, part(n)] = s_inside * (c[n] + pltpu.roll(c[0], SUB - 1, 0))
                above = z_above * (c[n] + pltpu.roll(c[n], NZ - 1, 1))
                below = z_below * (c[n] + pltpu.roll(c[n], 1, 1))
                kzp[i, part(n)], kzm[i, part(n)] = above, below
                ends = jnp.where((z == 0) | (z == NZ - 1), WZ, 0.0)
                if n == 0:
                    ends = ends + first_end
                elif n == BLOCKS - 1:
                    ends = ends + last_end
                keep[i, part(n)] = 1.0 - ((above + below) + ends * c[n])
        return carry

    kx[first_row - 1] = WX * (cond[first_row - 1] + cond[first_row])
    if pairs == 1:
        rows(0, 0)
    else:
        lax.fori_loop(0, pairs, rows, 0)


def advance(src, dst, first, last, coefs, load, near, far):
    kx, ky, kzp, kzm, keep = coefs
    count = last - first + 1
    group = 3 if count % 3 == 0 else min(count, 4)

    def rows(b, carry):
        base = first + group * b
        places = range(group)
        inside = [row_validity(base + r, near, far) for r in places]
        u = [src[base + r, part(0)] for r in places]
        wrap = [
            ky[base + r, part(BLOCKS - 1)]
            * (pltpu.roll(u[r], SUB - 1, 0) - src[base + r, part(BLOCKS - 1)])
            for r in places
        ]
        left = [pltpu.roll(each, 1, 0) for each in wrap]
        for n in range(BLOCKS):
            below = kx[base - 1, part(n)] * (u[0] - src[base - 1, part(n)])
            following = wrap
            for r in places:
                i = base + r
                beyond = u[r + 1] if r < group - 1 else src[i + 1, part(n)]
                across = kx[i, part(n)] * (beyond - u[r])
                new = keep[i, part(n)] * u[r] + (across - below)
                new += kzp[i, part(n)] * pltpu.roll(u[r], NZ - 1, 1)
                new += kzm[i, part(n)] * pltpu.roll(u[r], 1, 1)
                if load is not None:
                    new += load[i, part(n)]
                below = across
                if n < BLOCKS - 1:
                    after = src[i, part(n + 1)]
                    right = ky[i, part(n)] * (after - u[r])
                else:
                    after, right = None, wrap[r]
                dst[i, part(n)] = (new + (right - left[r])) * inside[r]
                left[r] = right
                if r == 0:
                    following = []
                following.append(after)
            u = following
        return carry

    if group == count:
        rows(0, 0)
    else:
        lax.fori_loop(0, count // group, rows, 0)


def parts_of(values, count):
    parts = []
    for _ in range(count):
        part = values.astype(bf16).astype(f32)
        parts.append(part)
        values = values - part
    return parts


def stacked_rows(parts):
    row = lax.broadcasted_iota(jnp.int32, (16, parts[0].shape[1]), 0)
    out = jnp.zeros(row.shape, f32)
    for number, part in enumerate(parts):
        out = jnp.where(row == number, part, out)
    return out.astype(bf16)


def hot(index, count):
    return lax.broadcasted_iota(jnp.int32, (count, index.shape[1]), 0) == index


def as_bf16(mask):
    return jnp.where(mask, 1.0, 0.0).astype(bf16)


def duct_lists(duct, base, flip):
    cells = jnp.concatenate([duct[base : base + 8], duct[base + 8 : base + 16]], axis=1)
    cells = cells.astype(jnp.int32)
    if flip:
        cells = cells ^ (NY * NZ)
    extra = duct[base + 16 : base + 24]
    segment = jnp.concatenate([extra[0:1], extra[1:2]], axis=1).astype(jnp.int32)
    return cells >> 7, cells & (NZ - 1), segment


def pack_kernel(
    log_cond, opening, heat, cells, segment, measured, full,
    rows_v, cells_v, segment_v, measured_v, sems,
):
    g, core, _, _ = position()
    copies = []

    def copy(src, dst):
        copies.append(pltpu.make_async_copy(src, dst, sems.at[len(copies)]))
        copies[-1].start()

    targets = []
    for r in range(2):
        at = r ^ core
        sources = (
            (opening.at[0, at], U0 + r * NY),
            (log_cond.at[at], C0 + r * NY),
            (heat.at[0, at], Q1 if r else Q0),
        )
        for src, base in sources:
            copy(src, rows_v.at[len(targets)])
            targets.append(base)
    copy(cells, cells_v)
    copy(segment, segment_v)
    copy(measured, measured_v)
    for each in copies:
        each.wait()
    for number, base in enumerate(targets):
        for n in range(BLOCKS):
            full[pl.ds(base + SUB * n, SUB)] = rows_v[number, pl.ds(n, SUB, stride=BLOCKS)]
    cell = cells_v[...] ^ (core * NY * NZ)
    y = (cell >> 7) & (NY - 1)
    y = (y & (BLOCKS - 1)) * SUB + (y >> 4)
    moved = ((cell & (NY * NZ)) + y * NZ + (cell & (NZ - 1))).astype(f32)
    lane = lax.broadcasted_iota(jnp.int32, (8, 128), 1)
    row = lax.broadcasted_iota(jnp.int32, (8, 128), 0)
    seg = segment_v[...].astype(f32)
    extra = jnp.where(row == 0, seg[:, :128], jnp.where(row == 1, seg[:, 128:], 0.0))
    for n in range(measured.shape[1]):
        mine = (row == 2) & (lane == measured.shape[1] * g + n)
        extra = jnp.where(mine, measured_v[0:1, n : n + 1], extra)
    full[D0 : D0 + 8] = moved[:, :128]
    full[D0 + 8 : D0 + 16] = moved[:, 128:]
    full[D0 + 16 : D0 + 24] = extra


def pack_near_kernel(full, near):
    s, z = coordinates()
    z_above, z_below = jnp.where(z < NZ - 1, WZ, 0.0), jnp.where(z > 0, WZ, 0.0)
    z_ends = jnp.where((z == 0) | (z == NZ - 1), WZ, 0.0)

    def at(base, n):
        return full[pl.ds(base + SUB * n, SUB)]

    def turned(last, first):
        return jnp.where(s < SUB - 1, pltpu.roll(first, SUB - 1, 0), 0.0), last

    c = [jnp.exp(at(C0 + NY, n)) for n in range(BLOCKS)]
    u = [at(U0 + NY, n) for n in range(BLOCKS)]
    c_next, c_last = turned(c[-1], c[0])
    u_next, u_last = turned(u[-1], u[0])
    top = WX * (c_last + c_next) * (u_next - u_last)
    left = jnp.where(s > 0, pltpu.roll(top, 1, 0), WX * c[0] * u[0])
    for n in range(BLOCKS):
        right = WX * (c[n] + c[n + 1]) * (u[n + 1] - u[n]) if n < BLOCKS - 1 else top
        below = WX * (c[n] + jnp.exp(at(C0, n))) * (at(U0, n) - u[n])
        kzp = z_above * (c[n] + pltpu.roll(c[n], NZ - 1, 1))
        kzm = z_below * (c[n] + pltpu.roll(c[n], 1, 1))
        side = kzp * pltpu.roll(u[n], NZ - 1, 1) + kzm * pltpu.roll(u[n], 1, 1)
        side -= (kzp + kzm + z_ends * c[n]) * u[n]
        near[pl.ds(SUB * n, SUB)] = u[n]
        near[pl.ds(PARTLY + SUB * n, SUB)] = u[n] + DT * at(Q1, n) + (below + (right - left) + side)
        left = right
    near[NEAR_C0 : NEAR_D0] = full[C0 : C0 + CELLS]
    near[NEAR_D0 : NEAR_PACK] = full[D0 : D0 + 24]


def write_hots(duct, base, flip, j, at_rows, at_lanes, at_segments):
    rows, lanes, segment = duct_lists(duct, base, flip)
    for c in range(8):
        at = pl.ds(256 * c, 256)
        at_rows[j, :, at] = as_bf16(hot(rows[c : c + 1], CELLS))
        at_lanes[j, :, at] = as_bf16(hot(lanes[c : c + 1], NZ))
    if at_segments is not None:
        at_segments[j] = as_bf16(hot(segment, 128))


def place(slab, first, turned, valid, temp0, cond, load):
    for r in range(2):
        i, at = first + r, 1 - r if turned else r
        temp0[i] = slab[pl.ds(U0 + at * NY, NY)]
        conductivity = jnp.exp(slab[pl.ds(C0 + at * NY, NY)])
        cond[i] = conductivity if valid is None else conductivity * valid
        if i < EXT - 1:
            load[i] = DT * slab[pl.ds(Q1 if at else Q0, NY)]


def prepare_own_kernel(own, at_rows, at_lanes, at_segments, temp0, load, cond):
    place(own, 4, False, None, temp0, cond, load)
    write_hots(own, D0, False, 0, at_rows, at_lanes, at_segments)


def prepare_far_kernel(far1, far2, *refs):
    at_rows, at_lanes, at_segments, temp2, temp1, kx, ky, kzp, kzm, keep, temp0, load, cond = refs[3:]
    near, far = validity()
    coefs = (kx, ky, kzp, kzm, keep)
    place(far1, 6, True, None, temp0, cond, load)
    place(far2, 8, False, far, temp0, cond, load)
    coefficients(cond, *coefs, 5, 2)
    advance(temp0, temp1, 5, 8, coefs, load, near, far)
    advance(temp1, temp2, 6, 7, coefs, load, near, far)
    write_hots(far1, D0, True, 0, at_rows, at_lanes, at_segments)
    write_hots(far2, D0, False, 1, at_rows, at_lanes, at_segments)


def prepare_near_kernel(near2, far_segments, at_segments):
    _, _, segment = duct_lists(near2, NEAR_D0, False)
    at_segments[0] = as_bf16(hot(segment, 128))


def forward_kernel(near2, near1, own, at_rows, at_lanes, at_segments, *refs):
    temp3, temp4, sums, temp2, temp1, *coefs, temp0, load, cond = refs[FIELDS:]
    near, far = validity()
    temp0[0] = jnp.zeros((NY, NZ), f32)
    load[1] = jnp.zeros((NY, NZ), f32)
    temp0[1] = near2[0:NY]
    for r in range(2):
        cond[r] = jnp.exp(near2[pl.ds(NEAR_C0 + r * NY, NY)]) * near
    place(near1, 2, True, near, temp0, cond, load)
    coefficients(cond, *coefs, 1, 2)
    advance(temp0, temp1, 1, 4, coefs, load, near, far)
    temp1[1] = near * (near2[PARTLY : PARTLY + NY] + coefs[0][1] * (temp0[2] - temp0[1]))
    advance(temp1, temp2, 2, 5, coefs, load, near, far)
    advance(temp2, temp3, 3, 6, coefs, load, near, far)
    advance(temp3, temp4, 4, 5, coefs, load, near, far)

    across = jnp.concatenate([temp4[4].T, temp4[5].T], axis=1)
    stack = jnp.concatenate([part.astype(bf16) for part in parts_of(across, 3)], axis=0)
    picked = jnp.zeros((NZ, 256), f32)
    for c in range(8):
        at = pl.ds(256 * c, 256)
        found = jnp.dot(stack, at_rows[0, :, at], preferred_element_type=f32)
        value = (found[2 * NZ :] + found[NZ : 2 * NZ]) + found[:NZ]
        picked = picked + value * at_lanes[0, :, at].astype(f32)
    partial = 0.5 * jnp.sum(picked, axis=0, keepdims=True)
    by_segment = lax.dot_general(
        stacked_rows(parts_of(partial, 3)),
        at_segments[0],
        (((1,), (1,)), ((), ())),
        preferred_element_type=f32,
    )
    total = jnp.sum(by_segment, axis=0, keepdims=True) - own[pl.ds(D0 + 16, 8)][2:3]
    sums[...] = jnp.broadcast_to(total, sums.shape)


def backward_kernel(
    near2, near1, own_rows, own_lanes, own_segments, far_rows, far_lanes, far_segments, near2_segments,
    sums, temp0, temp1, temp2, temp3, cond, kx, ky, kzp, kzm, keep, grad, seg,
    costate4, costate3, costate2, costate1, acc, weights, near_rows, near_lanes, near_segments,
):
    g, core, _, _ = position()
    near, far = validity()
    temp, costate = (temp0, temp1, temp2, temp3), (costate4, costate3, costate2, costate1)
    resid = jnp.sum(sums[...], axis=0, keepdims=True)
    shift = lax.rem(128 - seg.shape[1] * g, 128)
    seg[...] = pltpu.roll(jnp.broadcast_to(resid, (8, 128)), shift, 1)[0:1, 0 : seg.shape[1]]
    stack = stacked_rows(parts_of(0.5 * resid, 3))
    write_hots(near2, NEAR_D0, False, 0, near_rows, near_lanes, None)
    near_segments[0] = near2_segments[0]
    write_hots(near1, D0, True, 1, near_rows, near_lanes, near_segments)
    own, fars = (own_rows, own_lanes, own_segments), (far_rows, far_lanes, far_segments)
    nears = (near_rows, near_lanes, near_segments)
    places = ((nears, 0, near), (nears, 1, near), (own, 0, 1.0), (fars, 0, 1.0), (fars, 1, far))
    for j, ((at_rows, at_lanes, at_segments), n, valid) in enumerate(places):
        source = jnp.dot(stack, at_segments[n], preferred_element_type=f32)
        source = jnp.sum(source, axis=0, keepdims=True) * valid
        upper, lower = (part.astype(bf16) for part in parts_of(source, 2))
        for c in range(8):
            at = pl.ds(256 * c, 256)
            weights[j, 0:NZ, at] = at_lanes[n, :, at] * upper
            weights[j, NZ : 2 * NZ, at] = at_lanes[n, :, at] * lower
        out = lax.dot_general(
            at_rows[n], weights[j], (((1,), (1,)), ((), ())), preferred_element_type=f32
        )
        out = out[:, :NZ] + out[:, NZ:]
        costate4[2 * j] = out[:NY]
        costate4[2 * j + 1] = out[NY:]

    coefs = (kx, ky, kzp, kzm, keep)
    for k in range(STEPS - 1):
        advance(costate[k], costate[k + 1], k + 1, 8 - k, coefs, None, near, far)
    s, z = coordinates()
    share = grad.shape[2]

    def sensitivity(i, carry):
        at = (i - 4) ^ core

        def products(n):
            across = jnp.zeros((SUB, NZ), f32)
            right, side, own = across, across, across
            for k in range(STEPS):
                u, a = temp[k], costate[STEPS - 1 - k]
                uc, ac = u[i, part(n)], a[i, part(n)]
                across += (uc - u[i + 1, part(n)]) * (ac - a[i + 1, part(n)])
                across += (uc - u[i - 1, part(n)]) * (ac - a[i - 1, part(n)])
                if n < BLOCKS - 1:
                    ur, ar = u[i, part(n + 1)], a[i, part(n + 1)]
                else:
                    ur = jnp.where(s < SUB - 1, pltpu.roll(u[i, part(0)], SUB - 1, 0), 0.0)
                    ar = jnp.where(s < SUB - 1, pltpu.roll(a[i, part(0)], SUB - 1, 0), 0.0)
                right += (ur - uc) * (ar - ac)
                us = jnp.where(z < NZ - 1, pltpu.roll(uc, NZ - 1, 1), 0.0)
                az = jnp.where(z < NZ - 1, pltpu.roll(ac, NZ - 1, 1), 0.0)
                side += (us - uc) * (az - ac)
                own += uc * ac
            side += jnp.where(z > 0, pltpu.roll(side, 1, 1), own)
            return across + 0.5 * side, right, own

        last, last_right, _ = products(BLOCKS - 1)
        left = None
        for n in range(BLOCKS):
            total, right, own = products(n) if n < BLOCKS - 1 else (last, last_right, None)
            if n == 0:
                left = jnp.where(s > 0, pltpu.roll(last_right, 1, 0), own)
            acc[pl.ds(n, SUB, stride=BLOCKS)] = (-WX) * cond[i, part(n)] * (total + (right + left))
            left = right
        for n in range(NY // share):
            grad[n, at] = acc[pl.ds(n * share, share)]
        return carry

    lax.fori_loop(4, 6, sensitivity, 0)


def field(*lead):
    return (*lead, NY, NZ)


def in_hbm(values):
    return pltpu.with_memory_space_constraint(values, pltpu.HBM)


def local(log_cond, opening_increase, heat_load, measured, duct_cells, duct_segment):
    grid = lax.axis_size("grid")
    tests = lax.axis_size("tests")
    vmem = pl.BlockSpec(memory_space=pltpu.VMEM)
    params = pltpu.CompilerParams(vmem_limit_bytes=24 * 1024 * 1024)
    pack = pl.pallas_call(
        pack_kernel,
        out_shape=pltpu.VMEM((PACK, NZ), f32),
        in_specs=[pl.BlockSpec(memory_space=pltpu.HBM)] * 6,
        out_specs=vmem,
        scratch_shapes=[
            pltpu.VMEM(field(6), f32),
            pltpu.VMEM((8, 256), jnp.int32),
            pltpu.VMEM((1, 256), jnp.int32),
            pltpu.VMEM(measured.shape, f32),
            pltpu.SemaphoreType.DMA((9,)),
        ],
        compiler_params=params,
        name="pack",
    )(*map(in_hbm, (log_cond, opening_increase, heat_load, duct_cells.T, duct_segment.T, measured)))
    pack_near = pl.pallas_call(
        pack_near_kernel,
        out_shape=pltpu.VMEM((NEAR_PACK, NZ), f32),
        in_specs=[vmem],
        out_specs=vmem,
        compiler_params=params,
        name="pack_near",
    )(pack)
    to_far = [(s, s - 2) for s in range(2, grid, 2)] + [(s, s + 2) for s in range(1, grid - 2, 2)]
    to_near = [(s, s + 2) for s in range(0, grid - 2, 2)] + [(s, s - 2) for s in range(3, grid, 2)]
    swap = [(s, s ^ 1) for s in range(grid)]
    far2 = lax.ppermute(pack, "grid", to_far)
    far1 = lax.ppermute(pack, "grid", swap)
    near2 = lax.ppermute(pack_near, "grid", to_near)

    def hots(slabs):
        return (
            pltpu.VMEM((slabs, CELLS, 2048), bf16),
            pltpu.VMEM((slabs, NZ, 2048), bf16),
            pltpu.VMEM((slabs, 128, 256), bf16),
        )

    field_shape = pltpu.VMEM(field(EXT), f32)

    def stage(kernel, out_shape, name, *operands, fields=(), cost=COST_ESTIMATE):
        shapes = (*out_shape, *[field_shape] * len(fields))
        return pl.pallas_call(
            kernel,
            out_shape=shapes,
            in_specs=[vmem] * (len(operands) + len(fields)),
            out_specs=(vmem,) * len(shapes),
            input_output_aliases={len(operands) + n: len(out_shape) + n for n in range(len(fields))},
            compiler_params=params,
            cost_estimate=pl.CostEstimate(flops=cost, bytes_accessed=4_000_000, transcendentals=0),
            name=name,
        )(*operands, *fields)

    results = stage(prepare_own_kernel, (*hots(1), *[field_shape] * 3), "prepare_own", pack)
    own_hots, fields = results[:3], results[3:]
    far2, own_hots = lax.optimization_barrier((far2, own_hots))
    near1 = lax.ppermute(far2, "grid", swap)
    results = stage(
        prepare_far_kernel, (*hots(2), *[field_shape] * 7), "prepare_far", far1, far2, fields=fields
    )
    far_hots, fields = results[:3], results[3:]
    near_hots = stage(prepare_near_kernel, hots(1)[2:], "prepare_near", near2, far_hots[2])
    near2, near_hots, far_hots = lax.optimization_barrier((near2, near_hots, far_hots))
    out_shape = (field_shape, field_shape, pltpu.VMEM((grid, 128), f32))
    temp3, _, sums, temp2, temp1, *coefs, temp0, _, cond = stage(
        forward_kernel, out_shape, "forward", near2, near1, pack, *own_hots, fields=fields
    )
    sums = lax.all_to_all(sums, "grid", split_axis=0, concat_axis=0, tiled=True)
    share = NY // tests
    grad, seg = pl.pallas_call(
        backward_kernel,
        out_shape=(
            pltpu.VMEM((tests, 2, share, NZ), f32),
            jax.ShapeDtypeStruct(measured.shape, f32),
        ),
        in_specs=[vmem] * 20,
        out_specs=(vmem, vmem),
        scratch_shapes=[
            *[pltpu.VMEM(field(EXT), f32)] * STEPS,
            pltpu.VMEM((NY, NZ), f32),
            pltpu.VMEM((5, CELLS, 2048), bf16),
            *hots(2),
        ],
        compiler_params=params,
        name="backward",
    )(near2, near1, *own_hots, *far_hots, *near_hots, sums, temp0, temp1, temp2, temp3, cond, *coefs)
    grad = lax.all_to_all(grad, "tests", split_axis=0, concat_axis=0, tiled=True)
    return jnp.sum(grad, axis=0), seg


def solution(mesh):
    in_specs = (
        P("grid", None, None),
        P("tests", "grid", None, None),
        P("tests", "grid", None, None),
        P("tests", "grid"),
        P("grid", None),
        P("grid", None),
    )
    out_specs = (P("grid", "tests", None), P("tests", "grid"))
    return jax.shard_map(local, mesh=mesh, in_specs=in_specs, out_specs=out_specs, check_vma=False)
```

```python
import jax
import jax.numpy as jnp
from jax import lax
from jax.experimental import pallas as pl
from jax.experimental.pallas import tpu as pltpu
from jax.sharding import PartitionSpec as P

STEPS = 4
DT = 0.08
WX = 0.5 * DT
WZ = 0.25 * DT
NY = 128
NZ = 128
CELLS = 2 * NY
EXT = 10
SUB = 8
BLOCKS = NY // SUB
Q0 = 0
U0 = NY
C0 = U0 + CELLS
D0 = C0 + CELLS
Q1 = D0 + 24
PACK = Q1 + NY
PARTLY = NY
NEAR_C0 = 2 * NY
NEAR_D0 = 4 * NY
NEAR_PACK = NEAR_D0 + 24
FIELDS = 10
COST_ESTIMATE = 2_000_000_000
bf16 = jnp.bfloat16
f32 = jnp.float32


def position():
    g = lax.axis_index("grid")
    return g, lax.rem(g, 2), lax.div(g, 2), lax.axis_size("grid") // 2


def validity():
    _, core, chip, chips = position()
    low, high = (chip > 0).astype(f32), (chip < chips - 1).astype(f32)
    near = jnp.where(core == 0, low, high)
    far = jnp.where(core == 0, high, low)
    return near, far


def row_validity(i, near, far):
    return jnp.where(i < 4, near, jnp.where(i < 8, 1.0, far))


def part(n):
    return pl.ds(SUB * n, SUB)


def coordinates():
    s = lax.broadcasted_iota(jnp.int32, (SUB, NZ), 0)
    z = lax.broadcasted_iota(jnp.int32, (SUB, NZ), 1)
    return s, z


def coefficients(cond, kx, ky, kzp, kzm, keep, first_row, pairs):
    s, z = coordinates()
    z_above, z_below = jnp.where(z < NZ - 1, WZ, 0.0), jnp.where(z > 0, WZ, 0.0)
    s_inside = jnp.where(s < SUB - 1, WX, 0.0)
    first_end, last_end = jnp.where(s == 0, WX, 0.0), jnp.where(s == SUB - 1, WX, 0.0)

    def rows(b, carry):
        first = first_row + 2 * b
        for i in (first, first + 1):
            c = [cond[i, part(n)] for n in range(BLOCKS)]
            for n in range(BLOCKS):
                kx[i, part(n)] = WX * (c[n] + cond[i + 1, part(n)])
                if n < BLOCKS - 1:
                    ky[i, part(n)] = WX * (c[n] + c[n + 1])
                else:
                    ky[i, part(n)] = s_inside * (c[n] + pltpu.roll(c[0], SUB - 1, 0))
                above = z_above * (c[n] + pltpu.roll(c[n], NZ - 1, 1))
                below = z_below * (c[n] + pltpu.roll(c[n], 1, 1))
                kzp[i, part(n)], kzm[i, part(n)] = above, below
                ends = jnp.where((z == 0) | (z == NZ - 1), WZ, 0.0)
                if n == 0:
                    ends = ends + first_end
                elif n == BLOCKS - 1:
                    ends = ends + last_end
                keep[i, part(n)] = 1.0 - ((above + below) + ends * c[n])
        return carry

    kx[first_row - 1] = WX * (cond[first_row - 1] + cond[first_row])
    if pairs == 1:
        rows(0, 0)
    else:
        lax.fori_loop(0, pairs, rows, 0)


def advance(src, dst, first, last, coefs, load, near, far):
    kx, ky, kzp, kzm, keep = coefs
    count = last - first + 1
    group = 3 if count % 3 == 0 else min(count, 4)

    def rows(b, carry):
        base = first + group * b
        places = range(group)
        inside = [row_validity(base + r, near, far) for r in places]
        u = [src[base + r, part(0)] for r in places]
        wrap = [
            ky[base + r, part(BLOCKS - 1)]
            * (pltpu.roll(u[r], SUB - 1, 0) - src[base + r, part(BLOCKS - 1)])
            for r in places
        ]
        left = [pltpu.roll(each, 1, 0) for each in wrap]
        for n in range(BLOCKS):
            below = kx[base - 1, part(n)] * (u[0] - src[base - 1, part(n)])
            following = wrap
            for r in places:
                i = base + r
                beyond = u[r + 1] if r < group - 1 else src[i + 1, part(n)]
                across = kx[i, part(n)] * (beyond - u[r])
                new = keep[i, part(n)] * u[r] + (across - below)
                new += kzp[i, part(n)] * pltpu.roll(u[r], NZ - 1, 1)
                new += kzm[i, part(n)] * pltpu.roll(u[r], 1, 1)
                if load is not None:
                    new += load[i, part(n)]
                below = across
                if n < BLOCKS - 1:
                    after = src[i, part(n + 1)]
                    right = ky[i, part(n)] * (after - u[r])
                else:
                    after, right = None, wrap[r]
                dst[i, part(n)] = (new + (right - left[r])) * inside[r]
                left[r] = right
                if r == 0:
                    following = []
                following.append(after)
            u = following
        return carry

    if group == count:
        rows(0, 0)
    else:
        lax.fori_loop(0, count // group, rows, 0)


def parts_of(values, count):
    parts = []
    for _ in range(count):
        part = values.astype(bf16).astype(f32)
        parts.append(part)
        values = values - part
    return parts


def stacked_rows(parts):
    row = lax.broadcasted_iota(jnp.int32, (16, parts[0].shape[1]), 0)
    out = jnp.zeros(row.shape, f32)
    for number, part in enumerate(parts):
        out = jnp.where(row == number, part, out)
    return out.astype(bf16)


def hot(index, count):
    return lax.broadcasted_iota(jnp.int32, (count, index.shape[1]), 0) == index


def as_bf16(mask):
    return jnp.where(mask, 1.0, 0.0).astype(bf16)


def duct_lists(duct, base, flip):
    cells = jnp.concatenate([duct[base : base + 8], duct[base + 8 : base + 16]], axis=1)
    cells = cells.astype(jnp.int32)
    if flip:
        cells = cells ^ (NY * NZ)
    extra = duct[base + 16 : base + 24]
    segment = jnp.concatenate([extra[0:1], extra[1:2]], axis=1).astype(jnp.int32)
    return cells >> 7, cells & (NZ - 1), segment


def pack_kernel(
    log_cond, opening, heat, cells, segment, measured, full,
    rows_v, cells_v, segment_v, measured_v, sems,
):
    g, core, _, _ = position()
    copies = []

    def copy(src, dst):
        copies.append(pltpu.make_async_copy(src, dst, sems.at[len(copies)]))
        copies[-1].start()

    targets = []
    for r in range(2):
        at = r ^ core
        sources = (
            (opening.at[0, at], U0 + r * NY),
            (log_cond.at[at], C0 + r * NY),
            (heat.at[0, at], Q1 if r else Q0),
        )
        for src, base in sources:
            copy(src, rows_v.at[len(targets)])
            targets.append(base)
    copy(cells, cells_v)
    copy(segment, segment_v)
    copy(measured, measured_v)
    for each in copies:
        each.wait()
    for number, base in enumerate(targets):
        for n in range(BLOCKS):
            full[pl.ds(base + SUB * n, SUB)] = rows_v[number, pl.ds(n, SUB, stride=BLOCKS)]
    cell = cells_v[...] ^ (core * NY * NZ)
    y = (cell >> 7) & (NY - 1)
    y = (y & (BLOCKS - 1)) * SUB + (y >> 4)
    moved = ((cell & (NY * NZ)) + y * NZ + (cell & (NZ - 1))).astype(f32)
    lane = lax.broadcasted_iota(jnp.int32, (8, 128), 1)
    row = lax.broadcasted_iota(jnp.int32, (8, 128), 0)
    seg = segment_v[...].astype(f32)
    extra = jnp.where(row == 0, seg[:, :128], jnp.where(row == 1, seg[:, 128:], 0.0))
    for n in range(measured.shape[1]):
        mine = (row == 2) & (lane == measured.shape[1] * g + n)
        extra = jnp.where(mine, measured_v[0:1, n : n + 1], extra)
    full[D0 : D0 + 8] = moved[:, :128]
    full[D0 + 8 : D0 + 16] = moved[:, 128:]
    full[D0 + 16 : D0 + 24] = extra


def pack_near_kernel(full, near):
    s, z = coordinates()
    z_above, z_below = jnp.where(z < NZ - 1, WZ, 0.0), jnp.where(z > 0, WZ, 0.0)
    z_ends = jnp.where((z == 0) | (z == NZ - 1), WZ, 0.0)

    def at(base, n):
        return full[pl.ds(base + SUB * n, SUB)]

    def turned(last, first):
        return jnp.where(s < SUB - 1, pltpu.roll(first, SUB - 1, 0), 0.0), last

    c = [jnp.exp(at(C0 + NY, n)) for n in range(BLOCKS)]
    u = [at(U0 + NY, n) for n in range(BLOCKS)]
    c_next, c_last = turned(c[-1], c[0])
    u_next, u_last = turned(u[-1], u[0])
    top = WX * (c_last + c_next) * (u_next - u_last)
    left = jnp.where(s > 0, pltpu.roll(top, 1, 0), WX * c[0] * u[0])
    for n in range(BLOCKS):
        right = WX * (c[n] + c[n + 1]) * (u[n + 1] - u[n]) if n < BLOCKS - 1 else top
        below = WX * (c[n] + jnp.exp(at(C0, n))) * (at(U0, n) - u[n])
        kzp = z_above * (c[n] + pltpu.roll(c[n], NZ - 1, 1))
        kzm = z_below * (c[n] + pltpu.roll(c[n], 1, 1))
        side = kzp * pltpu.roll(u[n], NZ - 1, 1) + kzm * pltpu.roll(u[n], 1, 1)
        side -= (kzp + kzm + z_ends * c[n]) * u[n]
        near[pl.ds(SUB * n, SUB)] = u[n]
        near[pl.ds(PARTLY + SUB * n, SUB)] = u[n] + DT * at(Q1, n) + (below + (right - left) + side)
        left = right
    near[NEAR_C0 : NEAR_D0] = full[C0 : C0 + CELLS]
    near[NEAR_D0 : NEAR_PACK] = full[D0 : D0 + 24]


def write_hots(duct, base, flip, j, at_rows, at_lanes, at_segments):
    rows, lanes, segment = duct_lists(duct, base, flip)
    for c in range(8):
        at = pl.ds(256 * c, 256)
        at_rows[j, :, at] = as_bf16(hot(rows[c : c + 1], CELLS))
        at_lanes[j, :, at] = as_bf16(hot(lanes[c : c + 1], NZ))
    if at_segments is not None:
        at_segments[j] = as_bf16(hot(segment, 128))


def place(slab, first, turned, valid, temp0, cond, load):
    for r in range(2):
        i, at = first + r, 1 - r if turned else r
        temp0[i] = slab[pl.ds(U0 + at * NY, NY)]
        conductivity = jnp.exp(slab[pl.ds(C0 + at * NY, NY)])
        cond[i] = conductivity if valid is None else conductivity * valid
        if i < EXT - 1:
            load[i] = DT * slab[pl.ds(Q1 if at else Q0, NY)]


def prepare_own_kernel(own, at_rows, at_lanes, at_segments, temp0, load, cond):
    place(own, 4, False, None, temp0, cond, load)
    write_hots(own, D0, False, 0, at_rows, at_lanes, at_segments)


def prepare_chip_kernel(far1, *refs):
    at_rows, at_lanes, at_segments, temp1, kx, ky, kzp, kzm, keep, temp0, load, cond = refs[3:]
    near, far = validity()
    coefs = (kx, ky, kzp, kzm, keep)
    place(far1, 6, True, None, temp0, cond, load)
    coefficients(cond, *coefs, 5, 1)
    advance(temp0, temp1, 5, 6, coefs, load, near, far)
    write_hots(far1, D0, True, 0, at_rows, at_lanes, at_segments)


def prepare_far_kernel(far2, *refs):
    at_rows, at_lanes, at_segments, temp2, temp1, kx, ky, kzp, kzm, keep, temp0, load, cond = refs[FIELDS - 1 :]
    near, far = validity()
    coefs = (kx, ky, kzp, kzm, keep)
    place(far2, 8, False, far, temp0, cond, load)
    coefficients(cond, *coefs, 7, 1)
    advance(temp0, temp1, 7, 8, coefs, load, near, far)
    advance(temp1, temp2, 6, 7, coefs, load, near, far)
    write_hots(far2, D0, False, 0, at_rows, at_lanes, at_segments)


def prepare_near_kernel(near2, far_segments, at_segments):
    _, _, segment = duct_lists(near2, NEAR_D0, False)
    at_segments[0] = as_bf16(hot(segment, 128))


def forward_kernel(near2, near1, own, at_rows, at_lanes, at_segments, *refs):
    temp3, temp4, sums, temp2, temp1, *coefs, temp0, load, cond = refs[FIELDS:]
    near, far = validity()
    temp0[0] = jnp.zeros((NY, NZ), f32)
    load[1] = jnp.zeros((NY, NZ), f32)
    temp0[1] = near2[0:NY]
    for r in range(2):
        cond[r] = jnp.exp(near2[pl.ds(NEAR_C0 + r * NY, NY)]) * near
    place(near1, 2, True, near, temp0, cond, load)
    coefficients(cond, *coefs, 1, 2)
    advance(temp0, temp1, 1, 4, coefs, load, near, far)
    temp1[1] = near * (near2[PARTLY : PARTLY + NY] + coefs[0][1] * (temp0[2] - temp0[1]))
    advance(temp1, temp2, 2, 5, coefs, load, near, far)
    advance(temp2, temp3, 3, 6, coefs, load, near, far)
    advance(temp3, temp4, 4, 5, coefs, load, near, far)

    across = jnp.concatenate([temp4[4].T, temp4[5].T], axis=1)
    stack = jnp.concatenate([part.astype(bf16) for part in parts_of(across, 3)], axis=0)
    picked = jnp.zeros((NZ, 256), f32)
    for c in range(8):
        at = pl.ds(256 * c, 256)
        found = jnp.dot(stack, at_rows[0, :, at], preferred_element_type=f32)
        value = (found[2 * NZ :] + found[NZ : 2 * NZ]) + found[:NZ]
        picked = picked + value * at_lanes[0, :, at].astype(f32)
    partial = 0.5 * jnp.sum(picked, axis=0, keepdims=True)
    by_segment = lax.dot_general(
        stacked_rows(parts_of(partial, 3)),
        at_segments[0],
        (((1,), (1,)), ((), ())),
        preferred_element_type=f32,
    )
    total = jnp.sum(by_segment, axis=0, keepdims=True) - own[pl.ds(D0 + 16, 8)][2:3]
    sums[...] = jnp.broadcast_to(total, sums.shape)


def backward_kernel(
    near2, near1, own_rows, own_lanes, own_segments, next_rows, next_lanes, next_segments,
    far_rows, far_lanes, far_segments, near2_segments,
    sums, temp0, temp1, temp2, temp3, cond, kx, ky, kzp, kzm, keep, grad, seg,
    costate4, costate3, costate2, costate1, acc, weights, near_rows, near_lanes, near_segments,
):
    g, core, _, _ = position()
    near, far = validity()
    temp, costate = (temp0, temp1, temp2, temp3), (costate4, costate3, costate2, costate1)
    resid = jnp.sum(sums[...], axis=0, keepdims=True)
    shift = lax.rem(128 - seg.shape[1] * g, 128)
    seg[...] = pltpu.roll(jnp.broadcast_to(resid, (8, 128)), shift, 1)[0:1, 0 : seg.shape[1]]
    stack = stacked_rows(parts_of(0.5 * resid, 3))
    write_hots(near2, NEAR_D0, False, 0, near_rows, near_lanes, None)
    near_segments[0] = near2_segments[0]
    write_hots(near1, D0, True, 1, near_rows, near_lanes, near_segments)
    beside = (next_rows, next_lanes, next_segments)
    own, fars = (own_rows, own_lanes, own_segments), (far_rows, far_lanes, far_segments)
    nears = (near_rows, near_lanes, near_segments)
    places = ((nears, 0, near), (nears, 1, near), (own, 0, 1.0), (beside, 0, 1.0), (fars, 0, far))
    for j, ((at_rows, at_lanes, at_segments), n, valid) in enumerate(places):
        source = jnp.dot(stack, at_segments[n], preferred_element_type=f32)
        source = jnp.sum(source, axis=0, keepdims=True) * valid
        upper, lower = (part.astype(bf16) for part in parts_of(source, 2))
        for c in range(8):
            at = pl.ds(256 * c, 256)
            weights[j, 0:NZ, at] = at_lanes[n, :, at] * upper
            weights[j, NZ : 2 * NZ, at] = at_lanes[n, :, at] * lower
        out = lax.dot_general(
            at_rows[n], weights[j], (((1,), (1,)), ((), ())), preferred_element_type=f32
        )
        out = out[:, :NZ] + out[:, NZ:]
        costate4[2 * j] = out[:NY]
        costate4[2 * j + 1] = out[NY:]

    coefs = (kx, ky, kzp, kzm, keep)
    for k in range(STEPS - 1):
        advance(costate[k], costate[k + 1], k + 1, 8 - k, coefs, None, near, far)
    s, z = coordinates()
    share = grad.shape[2]

    def sensitivity(i, carry):
        at = (i - 4) ^ core

        def products(n):
            across = jnp.zeros((SUB, NZ), f32)
            right, side, own = across, across, across
            for k in range(STEPS):
                u, a = temp[k], costate[STEPS - 1 - k]
                uc, ac = u[i, part(n)], a[i, part(n)]
                across += (uc - u[i + 1, part(n)]) * (ac - a[i + 1, part(n)])
                across += (uc - u[i - 1, part(n)]) * (ac - a[i - 1, part(n)])
                if n < BLOCKS - 1:
                    ur, ar = u[i, part(n + 1)], a[i, part(n + 1)]
                else:
                    ur = jnp.where(s < SUB - 1, pltpu.roll(u[i, part(0)], SUB - 1, 0), 0.0)
                    ar = jnp.where(s < SUB - 1, pltpu.roll(a[i, part(0)], SUB - 1, 0), 0.0)
                right += (ur - uc) * (ar - ac)
                us = jnp.where(z < NZ - 1, pltpu.roll(uc, NZ - 1, 1), 0.0)
                az = jnp.where(z < NZ - 1, pltpu.roll(ac, NZ - 1, 1), 0.0)
                side += (us - uc) * (az - ac)
                own += uc * ac
            side += jnp.where(z > 0, pltpu.roll(side, 1, 1), own)
            return across + 0.5 * side, right, own

        last, last_right, _ = products(BLOCKS - 1)
        left = None
        for n in range(BLOCKS):
            total, right, own = products(n) if n < BLOCKS - 1 else (last, last_right, None)
            if n == 0:
                left = jnp.where(s > 0, pltpu.roll(last_right, 1, 0), own)
            acc[pl.ds(n, SUB, stride=BLOCKS)] = (-WX) * cond[i, part(n)] * (total + (right + left))
            left = right
        for n in range(NY // share):
            grad[n, at] = acc[pl.ds(n * share, share)]
        return carry

    lax.fori_loop(4, 6, sensitivity, 0)


def field(*lead):
    return (*lead, NY, NZ)


def in_hbm(values):
    return pltpu.with_memory_space_constraint(values, pltpu.HBM)


def local(log_cond, opening_increase, heat_load, measured, duct_cells, duct_segment):
    grid = lax.axis_size("grid")
    tests = lax.axis_size("tests")
    vmem = pl.BlockSpec(memory_space=pltpu.VMEM)
    params = pltpu.CompilerParams(vmem_limit_bytes=24 * 1024 * 1024)
    pack = pl.pallas_call(
        pack_kernel,
        out_shape=pltpu.VMEM((PACK, NZ), f32),
        in_specs=[pl.BlockSpec(memory_space=pltpu.HBM)] * 6,
        out_specs=vmem,
        scratch_shapes=[
            pltpu.VMEM(field(6), f32),
            pltpu.VMEM((8, 256), jnp.int32),
            pltpu.VMEM((1, 256), jnp.int32),
            pltpu.VMEM(measured.shape, f32),
            pltpu.SemaphoreType.DMA((9,)),
        ],
        compiler_params=params,
        name="pack",
    )(*map(in_hbm, (log_cond, opening_increase, heat_load, duct_cells.T, duct_segment.T, measured)))
    pack_near = pl.pallas_call(
        pack_near_kernel,
        out_shape=pltpu.VMEM((NEAR_PACK, NZ), f32),
        in_specs=[vmem],
        out_specs=vmem,
        compiler_params=params,
        name="pack_near",
    )(pack)
    to_far = [(s, s - 2) for s in range(2, grid, 2)] + [(s, s + 2) for s in range(1, grid - 2, 2)]
    to_near = [(s, s + 2) for s in range(0, grid - 2, 2)] + [(s, s - 2) for s in range(3, grid, 2)]
    swap = [(s, s ^ 1) for s in range(grid)]
    far2 = lax.ppermute(pack, "grid", to_far)
    far1 = lax.ppermute(pack, "grid", swap)

    def hots(slabs):
        return (
            pltpu.VMEM((slabs, CELLS, 2048), bf16),
            pltpu.VMEM((slabs, NZ, 2048), bf16),
            pltpu.VMEM((slabs, 128, 256), bf16),
        )

    field_shape = pltpu.VMEM(field(EXT), f32)

    def stage(kernel, out_shape, name, *operands, fields=(), cost=COST_ESTIMATE):
        shapes = (*out_shape, *[field_shape] * len(fields))
        return pl.pallas_call(
            kernel,
            out_shape=shapes,
            in_specs=[vmem] * (len(operands) + len(fields)),
            out_specs=(vmem,) * len(shapes),
            input_output_aliases={len(operands) + n: len(out_shape) + n for n in range(len(fields))},
            compiler_params=params,
            cost_estimate=pl.CostEstimate(flops=cost, bytes_accessed=4_000_000, transcendentals=0),
            name=name,
        )(*operands, *fields)

    results = stage(prepare_own_kernel, (*hots(1), *[field_shape] * 3), "prepare_own", pack, cost=1000)
    own_hots, fields = results[:3], results[3:]
    results = stage(
        prepare_chip_kernel, (*hots(1), *[field_shape] * 6), "prepare_chip", far1, fields=fields, cost=1000
    )
    next_hots, fields = results[:3], results[3:]
    pack_near, next_hots = lax.optimization_barrier((pack_near, next_hots))
    near2 = lax.ppermute(pack_near, "grid", to_near)
    near1 = lax.ppermute(far2, "grid", swap)
    results = stage(prepare_far_kernel, (*hots(1), field_shape), "prepare_far", far2, fields=fields)
    far_hots, fields = results[:3], results[3:]
    near_hots = stage(prepare_near_kernel, hots(1)[2:], "prepare_near", near2, far_hots[2])
    near2, near_hots, far_hots = lax.optimization_barrier((near2, near_hots, far_hots))
    out_shape = (field_shape, field_shape, pltpu.VMEM((grid, 128), f32))
    temp3, _, sums, temp2, temp1, *coefs, temp0, _, cond = stage(
        forward_kernel, out_shape, "forward", near2, near1, pack, *own_hots, fields=fields
    )
    sums = lax.all_to_all(sums, "grid", split_axis=0, concat_axis=0, tiled=True)
    share = NY // tests
    grad, seg = pl.pallas_call(
        backward_kernel,
        out_shape=(
            pltpu.VMEM((tests, 2, share, NZ), f32),
            jax.ShapeDtypeStruct(measured.shape, f32),
        ),
        in_specs=[vmem] * 23,
        out_specs=(vmem, vmem),
        scratch_shapes=[
            *[pltpu.VMEM(field(EXT), f32)] * STEPS,
            pltpu.VMEM((NY, NZ), f32),
            pltpu.VMEM((5, CELLS, 2048), bf16),
            *hots(2),
        ],
        compiler_params=params,
        name="backward",
    )(near2, near1, *own_hots, *next_hots, *far_hots, *near_hots, sums, temp0, temp1, temp2, temp3, cond, *coefs)
    grad = lax.all_to_all(grad, "tests", split_axis=0, concat_axis=0, tiled=True)
    return jnp.sum(grad, axis=0), seg


def solution(mesh):
    in_specs = (
        P("grid", None, None),
        P("tests", "grid", None, None),
        P("tests", "grid", None, None),
        P("tests", "grid"),
        P("grid", None),
        P("grid", None),
    )
    out_specs = (P("grid", "tests", None), P("tests", "grid"))
    return jax.shard_map(local, mesh=mesh, in_specs=in_specs, out_specs=out_specs, check_vma=False)
```

```python
import jax
import jax.numpy as jnp
from jax import lax
from jax.experimental import pallas as pl
from jax.experimental.pallas import tpu as pltpu
from jax.sharding import PartitionSpec as P

STEPS = 4
DT = 0.08
WX = 0.5 * DT
WZ = 0.25 * DT
NY = 128
NZ = 128
CELLS = 2 * NY
EXT = 10
SUB = 8
BLOCKS = NY // SUB
Q0 = 0
U0 = NY
C0 = U0 + CELLS
D0 = C0 + CELLS
Q1 = D0 + 24
PACK = Q1 + NY
PARTLY = NY
NEAR_C0 = 2 * NY
NEAR_D0 = 4 * NY
NEAR_PACK = NEAR_D0 + 24
FIELDS = 10
COST_ESTIMATE = 2_000_000_000
bf16 = jnp.bfloat16
f32 = jnp.float32


def position():
    g = lax.axis_index("grid")
    return g, lax.rem(g, 2), lax.div(g, 2), lax.axis_size("grid") // 2


def validity():
    _, core, chip, chips = position()
    low, high = (chip > 0).astype(f32), (chip < chips - 1).astype(f32)
    near = jnp.where(core == 0, low, high)
    far = jnp.where(core == 0, high, low)
    return near, far


def row_validity(i, near, far):
    return jnp.where(i < 4, near, jnp.where(i < 8, 1.0, far))


def part(n):
    return pl.ds(SUB * n, SUB)


def coordinates():
    s = lax.broadcasted_iota(jnp.int32, (SUB, NZ), 0)
    z = lax.broadcasted_iota(jnp.int32, (SUB, NZ), 1)
    return s, z


def coefficients(cond, kx, ky, kzp, kzm, keep, first_row, pairs):
    s, z = coordinates()
    z_above, z_below = jnp.where(z < NZ - 1, WZ, 0.0), jnp.where(z > 0, WZ, 0.0)
    s_inside = jnp.where(s < SUB - 1, WX, 0.0)
    first_end, last_end = jnp.where(s == 0, WX, 0.0), jnp.where(s == SUB - 1, WX, 0.0)

    def rows(b, carry):
        first = first_row + 2 * b
        for i in (first, first + 1):
            c = [cond[i, part(n)] for n in range(BLOCKS)]
            for n in range(BLOCKS):
                kx[i, part(n)] = WX * (c[n] + cond[i + 1, part(n)])
                if n < BLOCKS - 1:
                    ky[i, part(n)] = WX * (c[n] + c[n + 1])
                else:
                    ky[i, part(n)] = s_inside * (c[n] + pltpu.roll(c[0], SUB - 1, 0))
                above = z_above * (c[n] + pltpu.roll(c[n], NZ - 1, 1))
                below = z_below * (c[n] + pltpu.roll(c[n], 1, 1))
                kzp[i, part(n)], kzm[i, part(n)] = above, below
                ends = jnp.where((z == 0) | (z == NZ - 1), WZ, 0.0)
                if n == 0:
                    ends = ends + first_end
                elif n == BLOCKS - 1:
                    ends = ends + last_end
                keep[i, part(n)] = 1.0 - ((above + below) + ends * c[n])
        return carry

    kx[first_row - 1] = WX * (cond[first_row - 1] + cond[first_row])
    if pairs == 1:
        rows(0, 0)
    else:
        lax.fori_loop(0, pairs, rows, 0)


def advance(src, dst, first, last, coefs, load, near, far):
    kx, ky, kzp, kzm, keep = coefs
    count = last - first + 1
    group = 3 if count % 3 == 0 else min(count, 4)

    def rows(b, carry):
        base = first + group * b
        places = range(group)
        inside = [row_validity(base + r, near, far) for r in places]
        u = [src[base + r, part(0)] for r in places]
        wrap = [
            ky[base + r, part(BLOCKS - 1)]
            * (pltpu.roll(u[r], SUB - 1, 0) - src[base + r, part(BLOCKS - 1)])
            for r in places
        ]
        left = [pltpu.roll(each, 1, 0) for each in wrap]
        for n in range(BLOCKS):
            below = kx[base - 1, part(n)] * (u[0] - src[base - 1, part(n)])
            following = wrap
            for r in places:
                i = base + r
                beyond = u[r + 1] if r < group - 1 else src[i + 1, part(n)]
                across = kx[i, part(n)] * (beyond - u[r])
                new = keep[i, part(n)] * u[r] + (across - below)
                new += kzp[i, part(n)] * pltpu.roll(u[r], NZ - 1, 1)
                new += kzm[i, part(n)] * pltpu.roll(u[r], 1, 1)
                if load is not None:
                    new += load[i, part(n)]
                below = across
                if n < BLOCKS - 1:
                    after = src[i, part(n + 1)]
                    right = ky[i, part(n)] * (after - u[r])
                else:
                    after, right = None, wrap[r]
                dst[i, part(n)] = (new + (right - left[r])) * inside[r]
                left[r] = right
                if r == 0:
                    following = []
                following.append(after)
            u = following
        return carry

    if group == count:
        rows(0, 0)
    else:
        lax.fori_loop(0, count // group, rows, 0)


def parts_of(values, count):
    parts = []
    for _ in range(count):
        part = values.astype(bf16).astype(f32)
        parts.append(part)
        values = values - part
    return parts


def stacked_rows(parts):
    row = lax.broadcasted_iota(jnp.int32, (16, parts[0].shape[1]), 0)
    out = jnp.zeros(row.shape, f32)
    for number, part in enumerate(parts):
        out = jnp.where(row == number, part, out)
    return out.astype(bf16)


def hot(index, count):
    return lax.broadcasted_iota(jnp.int32, (count, index.shape[1]), 0) == index


def as_bf16(mask):
    return jnp.where(mask, 1.0, 0.0).astype(bf16)


def duct_lists(duct, base, flip):
    cells = jnp.concatenate([duct[base : base + 8], duct[base + 8 : base + 16]], axis=1)
    cells = cells.astype(jnp.int32)
    if flip:
        cells = cells ^ (NY * NZ)
    extra = duct[base + 16 : base + 24]
    segment = jnp.concatenate([extra[0:1], extra[1:2]], axis=1).astype(jnp.int32)
    return cells >> 7, cells & (NZ - 1), segment


def pack_kernel(
    log_cond, opening, heat, cells, segment, measured, full,
    rows_v, cells_v, segment_v, measured_v, sems,
):
    g, core, _, _ = position()
    copies = []

    def copy(src, dst):
        copies.append(pltpu.make_async_copy(src, dst, sems.at[len(copies)]))
        copies[-1].start()

    targets = []
    for r in range(2):
        at = r ^ core
        sources = (
            (opening.at[0, at], U0 + r * NY),
            (log_cond.at[at], C0 + r * NY),
            (heat.at[0, at], Q1 if r else Q0),
        )
        for src, base in sources:
            copy(src, rows_v.at[len(targets)])
            targets.append(base)
    copy(cells, cells_v)
    copy(segment, segment_v)
    copy(measured, measured_v)
    for each in copies:
        each.wait()
    for number, base in enumerate(targets):
        for n in range(BLOCKS):
            full[pl.ds(base + SUB * n, SUB)] = rows_v[number, pl.ds(n, SUB, stride=BLOCKS)]
    cell = cells_v[...] ^ (core * NY * NZ)
    y = (cell >> 7) & (NY - 1)
    y = (y & (BLOCKS - 1)) * SUB + (y >> 4)
    moved = ((cell & (NY * NZ)) + y * NZ + (cell & (NZ - 1))).astype(f32)
    lane = lax.broadcasted_iota(jnp.int32, (8, 128), 1)
    row = lax.broadcasted_iota(jnp.int32, (8, 128), 0)
    seg = segment_v[...].astype(f32)
    extra = jnp.where(row == 0, seg[:, :128], jnp.where(row == 1, seg[:, 128:], 0.0))
    for n in range(measured.shape[1]):
        mine = (row == 2) & (lane == measured.shape[1] * g + n)
        extra = jnp.where(mine, measured_v[0:1, n : n + 1], extra)
    full[D0 : D0 + 8] = moved[:, :128]
    full[D0 + 8 : D0 + 16] = moved[:, 128:]
    full[D0 + 16 : D0 + 24] = extra


def pack_near_kernel(full, near):
    s, z = coordinates()
    z_above, z_below = jnp.where(z < NZ - 1, WZ, 0.0), jnp.where(z > 0, WZ, 0.0)
    z_ends = jnp.where((z == 0) | (z == NZ - 1), WZ, 0.0)

    def at(base, n):
        return full[pl.ds(base + SUB * n, SUB)]

    def turned(last, first):
        return jnp.where(s < SUB - 1, pltpu.roll(first, SUB - 1, 0), 0.0), last

    c = [jnp.exp(at(C0 + NY, n)) for n in range(BLOCKS)]
    u = [at(U0 + NY, n) for n in range(BLOCKS)]
    c_next, c_last = turned(c[-1], c[0])
    u_next, u_last = turned(u[-1], u[0])
    top = WX * (c_last + c_next) * (u_next - u_last)
    left = jnp.where(s > 0, pltpu.roll(top, 1, 0), WX * c[0] * u[0])
    for n in range(BLOCKS):
        right = WX * (c[n] + c[n + 1]) * (u[n + 1] - u[n]) if n < BLOCKS - 1 else top
        below = WX * (c[n] + jnp.exp(at(C0, n))) * (at(U0, n) - u[n])
        kzp = z_above * (c[n] + pltpu.roll(c[n], NZ - 1, 1))
        kzm = z_below * (c[n] + pltpu.roll(c[n], 1, 1))
        side = kzp * pltpu.roll(u[n], NZ - 1, 1) + kzm * pltpu.roll(u[n], 1, 1)
        side -= (kzp + kzm + z_ends * c[n]) * u[n]
        near[pl.ds(SUB * n, SUB)] = u[n]
        near[pl.ds(PARTLY + SUB * n, SUB)] = u[n] + DT * at(Q1, n) + (below + (right - left) + side)
        left = right
    near[NEAR_C0 : NEAR_D0] = full[C0 : C0 + CELLS]
    near[NEAR_D0 : NEAR_PACK] = full[D0 : D0 + 24]


def write_hots(duct, base, flip, j, at_rows, at_lanes, at_segments):
    rows, lanes, segment = duct_lists(duct, base, flip)
    for c in range(8):
        at = pl.ds(256 * c, 256)
        at_rows[j, :, at] = as_bf16(hot(rows[c : c + 1], CELLS))
        at_lanes[j, :, at] = as_bf16(hot(lanes[c : c + 1], NZ))
    if at_segments is not None:
        at_segments[j] = as_bf16(hot(segment, 128))


def place(slab, first, turned, valid, temp0, cond, load):
    for r in range(2):
        i, at = first + r, 1 - r if turned else r
        temp0[i] = slab[pl.ds(U0 + at * NY, NY)]
        conductivity = jnp.exp(slab[pl.ds(C0 + at * NY, NY)])
        cond[i] = conductivity if valid is None else conductivity * valid
        if i < EXT - 1:
            load[i] = DT * slab[pl.ds(Q1 if at else Q0, NY)]


def prepare_own_kernel(own, at_rows, at_lanes, at_segments, temp0, load, cond):
    place(own, 4, False, None, temp0, cond, load)
    write_hots(own, D0, False, 0, at_rows, at_lanes, at_segments)


def prepare_far_kernel(far1, far2, *refs):
    at_rows, at_lanes, at_segments, temp2, temp1, kx, ky, kzp, kzm, keep, temp0, load, cond = refs[3:]
    near, far = validity()
    coefs = (kx, ky, kzp, kzm, keep)
    place(far1, 6, True, None, temp0, cond, load)
    place(far2, 8, False, far, temp0, cond, load)
    coefficients(cond, *coefs, 5, 2)
    advance(temp0, temp1, 5, 8, coefs, load, near, far)
    advance(temp1, temp2, 6, 7, coefs, load, near, far)
    write_hots(far1, D0, True, 0, at_rows, at_lanes, at_segments)
    write_hots(far2, D0, False, 1, at_rows, at_lanes, at_segments)


def prepare_near_kernel(near2, far_segments, at_segments):
    _, _, segment = duct_lists(near2, NEAR_D0, False)
    at_segments[0] = as_bf16(hot(segment, 128))


def forward_kernel(near2, near1, own, at_rows, at_lanes, at_segments, *refs):
    temp3, temp4, sums, temp2, temp1, *coefs, temp0, load, cond = refs[FIELDS:]
    near, far = validity()
    temp0[0] = jnp.zeros((NY, NZ), f32)
    load[1] = jnp.zeros((NY, NZ), f32)
    temp0[1] = near2[0:NY]
    for r in range(2):
        cond[r] = jnp.exp(near2[pl.ds(NEAR_C0 + r * NY, NY)]) * near
    place(near1, 2, True, near, temp0, cond, load)
    coefficients(cond, *coefs, 1, 2)
    advance(temp0, temp1, 1, 4, coefs, load, near, far)
    temp1[1] = near * (near2[PARTLY : PARTLY + NY] + coefs[0][1] * (temp0[2] - temp0[1]))
    advance(temp1, temp2, 2, 5, coefs, load, near, far)
    advance(temp2, temp3, 3, 6, coefs, load, near, far)
    advance(temp3, temp4, 4, 5, coefs, load, near, far)

    across = jnp.concatenate([temp4[4].T, temp4[5].T], axis=1)
    stack = jnp.concatenate([part.astype(bf16) for part in parts_of(across, 3)], axis=0)
    picked = jnp.zeros((NZ, 256), f32)
    for c in range(8):
        at = pl.ds(256 * c, 256)
        found = jnp.dot(stack, at_rows[0, :, at], preferred_element_type=f32)
        value = (found[2 * NZ :] + found[NZ : 2 * NZ]) + found[:NZ]
        picked = picked + value * at_lanes[0, :, at].astype(f32)
    partial = 0.5 * jnp.sum(picked, axis=0, keepdims=True)
    by_segment = lax.dot_general(
        stacked_rows(parts_of(partial, 3)),
        at_segments[0],
        (((1,), (1,)), ((), ())),
        preferred_element_type=f32,
    )
    total = jnp.sum(by_segment, axis=0, keepdims=True) - own[pl.ds(D0 + 16, 8)][2:3]
    sums[...] = jnp.broadcast_to(total, sums.shape)


def backward_kernel(
    near2, near1, own_rows, own_lanes, own_segments, far_rows, far_lanes, far_segments, near2_segments,
    sums, temp0, temp1, temp2, temp3, cond, kx, ky, kzp, kzm, keep, grad, seg,
    costate4, costate3, costate2, costate1, acc, weights, near_rows, near_lanes, near_segments,
):
    g, core, _, _ = position()
    near, far = validity()
    temp, costate = (temp0, temp1, temp2, temp3), (costate4, costate3, costate2, costate1)
    resid = jnp.sum(sums[...], axis=0, keepdims=True)
    shift = lax.rem(128 - seg.shape[1] * g, 128)
    seg[...] = pltpu.roll(jnp.broadcast_to(resid, (8, 128)), shift, 1)[0:1, 0 : seg.shape[1]]
    stack = stacked_rows(parts_of(0.5 * resid, 3))
    write_hots(near2, NEAR_D0, False, 0, near_rows, near_lanes, None)
    near_segments[0] = near2_segments[0]
    write_hots(near1, D0, True, 1, near_rows, near_lanes, near_segments)
    own, fars = (own_rows, own_lanes, own_segments), (far_rows, far_lanes, far_segments)
    nears = (near_rows, near_lanes, near_segments)
    places = ((nears, 0, near), (nears, 1, near), (own, 0, 1.0), (fars, 0, 1.0), (fars, 1, far))
    for j, ((at_rows, at_lanes, at_segments), n, valid) in enumerate(places):
        source = jnp.dot(stack, at_segments[n], preferred_element_type=f32)
        source = jnp.sum(source, axis=0, keepdims=True) * valid
        upper, lower = (part.astype(bf16) for part in parts_of(source, 2))
        for c in range(8):
            at = pl.ds(256 * c, 256)
            weights[j, 0:NZ, at] = at_lanes[n, :, at] * upper
            weights[j, NZ : 2 * NZ, at] = at_lanes[n, :, at] * lower
        out = lax.dot_general(
            weights[j], at_rows[n], (((1,), (1,)), ((), ())), preferred_element_type=f32
        )
        out = (out[:NZ] + out[NZ:]).T
        costate4[2 * j] = out[:NY]
        costate4[2 * j + 1] = out[NY:]

    coefs = (kx, ky, kzp, kzm, keep)
    for k in range(STEPS - 1):
        advance(costate[k], costate[k + 1], k + 1, 8 - k, coefs, None, near, far)
    s, z = coordinates()
    share = grad.shape[2]

    def sensitivity(i, carry):
        at = (i - 4) ^ core

        def products(n):
            across = jnp.zeros((SUB, NZ), f32)
            right, side, own = across, across, across
            for k in range(STEPS):
                u, a = temp[k], costate[STEPS - 1 - k]
                uc, ac = u[i, part(n)], a[i, part(n)]
                across += (uc - u[i + 1, part(n)]) * (ac - a[i + 1, part(n)])
                across += (uc - u[i - 1, part(n)]) * (ac - a[i - 1, part(n)])
                if n < BLOCKS - 1:
                    ur, ar = u[i, part(n + 1)], a[i, part(n + 1)]
                else:
                    ur = jnp.where(s < SUB - 1, pltpu.roll(u[i, part(0)], SUB - 1, 0), 0.0)
                    ar = jnp.where(s < SUB - 1, pltpu.roll(a[i, part(0)], SUB - 1, 0), 0.0)
                right += (ur - uc) * (ar - ac)
                us = jnp.where(z < NZ - 1, pltpu.roll(uc, NZ - 1, 1), 0.0)
                az = jnp.where(z < NZ - 1, pltpu.roll(ac, NZ - 1, 1), 0.0)
                side += (us - uc) * (az - ac)
                own += uc * ac
            side += jnp.where(z > 0, pltpu.roll(side, 1, 1), own)
            return across + 0.5 * side, right, own

        last, last_right, _ = products(BLOCKS - 1)
        left = None
        for n in range(BLOCKS):
            total, right, own = products(n) if n < BLOCKS - 1 else (last, last_right, None)
            if n == 0:
                left = jnp.where(s > 0, pltpu.roll(last_right, 1, 0), own)
            acc[pl.ds(n, SUB, stride=BLOCKS)] = (-WX) * cond[i, part(n)] * (total + (right + left))
            left = right
        for n in range(NY // share):
            grad[n, at] = acc[pl.ds(n * share, share)]
        return carry

    lax.fori_loop(4, 6, sensitivity, 0)


def field(*lead):
    return (*lead, NY, NZ)


def in_hbm(values):
    return pltpu.with_memory_space_constraint(values, pltpu.HBM)


def local(log_cond, opening_increase, heat_load, measured, duct_cells, duct_segment):
    grid = lax.axis_size("grid")
    tests = lax.axis_size("tests")
    vmem = pl.BlockSpec(memory_space=pltpu.VMEM)
    params = pltpu.CompilerParams(vmem_limit_bytes=24 * 1024 * 1024)
    pack = pl.pallas_call(
        pack_kernel,
        out_shape=pltpu.VMEM((PACK, NZ), f32),
        in_specs=[pl.BlockSpec(memory_space=pltpu.HBM)] * 6,
        out_specs=vmem,
        scratch_shapes=[
            pltpu.VMEM(field(6), f32),
            pltpu.VMEM((8, 256), jnp.int32),
            pltpu.VMEM((1, 256), jnp.int32),
            pltpu.VMEM(measured.shape, f32),
            pltpu.SemaphoreType.DMA((9,)),
        ],
        compiler_params=params,
        name="pack",
    )(*map(in_hbm, (log_cond, opening_increase, heat_load, duct_cells.T, duct_segment.T, measured)))
    pack_near = pl.pallas_call(
        pack_near_kernel,
        out_shape=pltpu.VMEM((NEAR_PACK, NZ), f32),
        in_specs=[vmem],
        out_specs=vmem,
        compiler_params=params,
        name="pack_near",
    )(pack)
    to_far = [(s, s - 2) for s in range(2, grid, 2)] + [(s, s + 2) for s in range(1, grid - 2, 2)]
    to_near = [(s, s + 2) for s in range(0, grid - 2, 2)] + [(s, s - 2) for s in range(3, grid, 2)]
    swap = [(s, s ^ 1) for s in range(grid)]
    far2 = lax.ppermute(pack, "grid", to_far)
    far1 = lax.ppermute(pack, "grid", swap)

    def hots(slabs):
        return (
            pltpu.VMEM((slabs, CELLS, 2048), bf16),
            pltpu.VMEM((slabs, NZ, 2048), bf16),
            pltpu.VMEM((slabs, 128, 256), bf16),
        )

    field_shape = pltpu.VMEM(field(EXT), f32)

    def stage(kernel, out_shape, name, *operands, fields=(), cost=COST_ESTIMATE):
        shapes = (*out_shape, *[field_shape] * len(fields))
        return pl.pallas_call(
            kernel,
            out_shape=shapes,
            in_specs=[vmem] * (len(operands) + len(fields)),
            out_specs=(vmem,) * len(shapes),
            input_output_aliases={len(operands) + n: len(out_shape) + n for n in range(len(fields))},
            compiler_params=params,
            cost_estimate=pl.CostEstimate(flops=cost, bytes_accessed=4_000_000, transcendentals=0),
            name=name,
        )(*operands, *fields)

    results = stage(prepare_own_kernel, (*hots(1), *[field_shape] * 3), "prepare_own", pack)
    own_hots, fields = results[:3], results[3:]
    pack_near, own_hots = lax.optimization_barrier((pack_near, own_hots))
    near2 = lax.ppermute(pack_near, "grid", to_near)
    far2, own_hots = lax.optimization_barrier((far2, own_hots))
    near1 = lax.ppermute(far2, "grid", swap)
    results = stage(
        prepare_far_kernel, (*hots(2), *[field_shape] * 7), "prepare_far", far1, far2, fields=fields
    )
    far_hots, fields = results[:3], results[3:]
    near_hots = stage(prepare_near_kernel, hots(1)[2:], "prepare_near", near2, far_hots[2])
    near2, near_hots, far_hots = lax.optimization_barrier((near2, near_hots, far_hots))
    out_shape = (field_shape, field_shape, pltpu.VMEM((grid, 128), f32))
    temp3, _, sums, temp2, temp1, *coefs, temp0, _, cond = stage(
        forward_kernel, out_shape, "forward", near2, near1, pack, *own_hots, fields=fields
    )
    sums = lax.all_to_all(sums, "grid", split_axis=0, concat_axis=0, tiled=True)
    share = NY // tests
    grad, seg = pl.pallas_call(
        backward_kernel,
        out_shape=(
            pltpu.VMEM((tests, 2, share, NZ), f32),
            jax.ShapeDtypeStruct(measured.shape, f32),
        ),
        in_specs=[vmem] * 20,
        out_specs=(vmem, vmem),
        scratch_shapes=[
            *[pltpu.VMEM(field(EXT), f32)] * STEPS,
            pltpu.VMEM((NY, NZ), f32),
            pltpu.VMEM((5, CELLS, 2048), bf16),
            *hots(2),
        ],
        compiler_params=params,
        name="backward",
    )(near2, near1, *own_hots, *far_hots, *near_hots, sums, temp0, temp1, temp2, temp3, cond, *coefs)
    grad = lax.all_to_all(grad, "tests", split_axis=0, concat_axis=0, tiled=True)
    return jnp.sum(grad, axis=0), seg


def solution(mesh):
    in_specs = (
        P("grid", None, None),
        P("tests", "grid", None, None),
        P("tests", "grid", None, None),
        P("tests", "grid"),
        P("grid", None),
        P("grid", None),
    )
    out_specs = (P("grid", "tests", None), P("tests", "grid"))
    return jax.shard_map(local, mesh=mesh, in_specs=in_specs, out_specs=out_specs, check_vma=False)
```

```python
import jax
import jax.numpy as jnp
from jax import lax
from jax.experimental import pallas as pl
from jax.experimental.pallas import tpu as pltpu
from jax.sharding import PartitionSpec as P

STEPS = 4
DT = 0.08
WX = 0.5 * DT
WZ = 0.25 * DT
NY = 128
NZ = 128
CELLS = 2 * NY
EXT = 10
SUB = 8
BLOCKS = NY // SUB
Q0 = 0
U0 = NY
C0 = U0 + CELLS
D0 = C0 + CELLS
Q1 = D0 + 24
PACK = Q1 + NY
PARTLY = NY
NEAR_C0 = 2 * NY
NEAR_D0 = 4 * NY
NEAR_PACK = NEAR_D0 + 24
FIELDS = 10
COST_ESTIMATE = 2_000_000_000
bf16 = jnp.bfloat16
f32 = jnp.float32


def position():
    g = lax.axis_index("grid")
    return g, lax.rem(g, 2), lax.div(g, 2), lax.axis_size("grid") // 2


def validity():
    _, core, chip, chips = position()
    low, high = (chip > 0).astype(f32), (chip < chips - 1).astype(f32)
    near = jnp.where(core == 0, low, high)
    far = jnp.where(core == 0, high, low)
    return near, far


def row_validity(i, near, far):
    return jnp.where(i < 4, near, jnp.where(i < 8, 1.0, far))


def part(n):
    return pl.ds(SUB * n, SUB)


def coordinates():
    s = lax.broadcasted_iota(jnp.int32, (SUB, NZ), 0)
    z = lax.broadcasted_iota(jnp.int32, (SUB, NZ), 1)
    return s, z


def coefficients(cond, kx, ky, kzp, kzm, keep, first_row, pairs):
    s, z = coordinates()
    z_above, z_below = jnp.where(z < NZ - 1, WZ, 0.0), jnp.where(z > 0, WZ, 0.0)
    s_inside = jnp.where(s < SUB - 1, WX, 0.0)
    first_end, last_end = jnp.where(s == 0, WX, 0.0), jnp.where(s == SUB - 1, WX, 0.0)

    def rows(b, carry):
        first = first_row + 2 * b
        for i in (first, first + 1):
            c = [cond[i, part(n)] for n in range(BLOCKS)]
            for n in range(BLOCKS):
                kx[i, part(n)] = WX * (c[n] + cond[i + 1, part(n)])
                if n < BLOCKS - 1:
                    ky[i, part(n)] = WX * (c[n] + c[n + 1])
                else:
                    ky[i, part(n)] = s_inside * (c[n] + pltpu.roll(c[0], SUB - 1, 0))
                above = z_above * (c[n] + pltpu.roll(c[n], NZ - 1, 1))
                below = z_below * (c[n] + pltpu.roll(c[n], 1, 1))
                kzp[i, part(n)], kzm[i, part(n)] = above, below
                ends = jnp.where((z == 0) | (z == NZ - 1), WZ, 0.0)
                if n == 0:
                    ends = ends + first_end
                elif n == BLOCKS - 1:
                    ends = ends + last_end
                keep[i, part(n)] = 1.0 - ((above + below) + ends * c[n])
        return carry

    kx[first_row - 1] = WX * (cond[first_row - 1] + cond[first_row])
    if pairs == 1:
        rows(0, 0)
    else:
        lax.fori_loop(0, pairs, rows, 0)


def advance(src, dst, first, last, coefs, load, near, far):
    kx, ky, kzp, kzm, keep = coefs
    count = last - first + 1
    group = 3 if count % 3 == 0 else min(count, 4)

    def rows(b, carry):
        base = first + group * b
        places = range(group)
        inside = [row_validity(base + r, near, far) for r in places]
        u = [src[base + r, part(0)] for r in places]
        wrap = [
            ky[base + r, part(BLOCKS - 1)]
            * (pltpu.roll(u[r], SUB - 1, 0) - src[base + r, part(BLOCKS - 1)])
            for r in places
        ]
        left = [pltpu.roll(each, 1, 0) for each in wrap]
        for n in range(BLOCKS):
            below = kx[base - 1, part(n)] * (u[0] - src[base - 1, part(n)])
            following = wrap
            for r in places:
                i = base + r
                beyond = u[r + 1] if r < group - 1 else src[i + 1, part(n)]
                across = kx[i, part(n)] * (beyond - u[r])
                new = keep[i, part(n)] * u[r] + (across - below)
                new += kzp[i, part(n)] * pltpu.roll(u[r], NZ - 1, 1)
                new += kzm[i, part(n)] * pltpu.roll(u[r], 1, 1)
                if load is not None:
                    new += load[i, part(n)]
                below = across
                if n < BLOCKS - 1:
                    after = src[i, part(n + 1)]
                    right = ky[i, part(n)] * (after - u[r])
                else:
                    after, right = None, wrap[r]
                dst[i, part(n)] = (new + (right - left[r])) * inside[r]
                left[r] = right
                if r == 0:
                    following = []
                following.append(after)
            u = following
        return carry

    if group == count:
        rows(0, 0)
    else:
        lax.fori_loop(0, count // group, rows, 0)


def parts_of(values, count):
    parts = []
    for _ in range(count):
        part = values.astype(bf16).astype(f32)
        parts.append(part)
        values = values - part
    return parts


def stacked_rows(parts):
    row = lax.broadcasted_iota(jnp.int32, (16, parts[0].shape[1]), 0)
    out = jnp.zeros(row.shape, f32)
    for number, part in enumerate(parts):
        out = jnp.where(row == number, part, out)
    return out.astype(bf16)


def hot(index, count):
    return lax.broadcasted_iota(jnp.int32, (count, index.shape[1]), 0) == index


def as_bf16(mask):
    return jnp.where(mask, 1.0, 0.0).astype(bf16)


def duct_lists(duct, base, flip):
    cells = jnp.concatenate([duct[base : base + 8], duct[base + 8 : base + 16]], axis=1)
    cells = cells.astype(jnp.int32)
    if flip:
        cells = cells ^ (NY * NZ)
    extra = duct[base + 16 : base + 24]
    segment = jnp.concatenate([extra[0:1], extra[1:2]], axis=1).astype(jnp.int32)
    return cells >> 7, cells & (NZ - 1), segment


def pack_kernel(
    log_cond, opening, heat, cells, segment, measured, full,
    rows_v, cells_v, segment_v, measured_v, sems,
):
    g, core, _, _ = position()
    copies = []

    def copy(src, dst):
        copies.append(pltpu.make_async_copy(src, dst, sems.at[len(copies)]))
        copies[-1].start()

    targets = []
    for r in range(2):
        at = r ^ core
        sources = (
            (opening.at[0, at], U0 + r * NY),
            (log_cond.at[at], C0 + r * NY),
            (heat.at[0, at], Q1 if r else Q0),
        )
        for src, base in sources:
            copy(src, rows_v.at[len(targets)])
            targets.append(base)
    copy(cells, cells_v)
    copy(segment, segment_v)
    copy(measured, measured_v)
    for each in copies:
        each.wait()
    for number, base in enumerate(targets):
        for n in range(BLOCKS):
            full[pl.ds(base + SUB * n, SUB)] = rows_v[number, pl.ds(n, SUB, stride=BLOCKS)]
    cell = cells_v[...] ^ (core * NY * NZ)
    y = (cell >> 7) & (NY - 1)
    y = (y & (BLOCKS - 1)) * SUB + (y >> 4)
    moved = ((cell & (NY * NZ)) + y * NZ + (cell & (NZ - 1))).astype(f32)
    lane = lax.broadcasted_iota(jnp.int32, (8, 128), 1)
    row = lax.broadcasted_iota(jnp.int32, (8, 128), 0)
    seg = segment_v[...].astype(f32)
    extra = jnp.where(row == 0, seg[:, :128], jnp.where(row == 1, seg[:, 128:], 0.0))
    for n in range(measured.shape[1]):
        mine = (row == 2) & (lane == measured.shape[1] * g + n)
        extra = jnp.where(mine, measured_v[0:1, n : n + 1], extra)
    full[D0 : D0 + 8] = moved[:, :128]
    full[D0 + 8 : D0 + 16] = moved[:, 128:]
    full[D0 + 16 : D0 + 24] = extra


def pack_near_kernel(full, near):
    s, z = coordinates()
    z_above, z_below = jnp.where(z < NZ - 1, WZ, 0.0), jnp.where(z > 0, WZ, 0.0)
    z_ends = jnp.where((z == 0) | (z == NZ - 1), WZ, 0.0)

    def at(base, n):
        return full[pl.ds(base + SUB * n, SUB)]

    def turned(last, first):
        return jnp.where(s < SUB - 1, pltpu.roll(first, SUB - 1, 0), 0.0), last

    c = [jnp.exp(at(C0 + NY, n)) for n in range(BLOCKS)]
    u = [at(U0 + NY, n) for n in range(BLOCKS)]
    c_next, c_last = turned(c[-1], c[0])
    u_next, u_last = turned(u[-1], u[0])
    top = WX * (c_last + c_next) * (u_next - u_last)
    left = jnp.where(s > 0, pltpu.roll(top, 1, 0), WX * c[0] * u[0])
    for n in range(BLOCKS):
        right = WX * (c[n] + c[n + 1]) * (u[n + 1] - u[n]) if n < BLOCKS - 1 else top
        below = WX * (c[n] + jnp.exp(at(C0, n))) * (at(U0, n) - u[n])
        kzp = z_above * (c[n] + pltpu.roll(c[n], NZ - 1, 1))
        kzm = z_below * (c[n] + pltpu.roll(c[n], 1, 1))
        side = kzp * pltpu.roll(u[n], NZ - 1, 1) + kzm * pltpu.roll(u[n], 1, 1)
        side -= (kzp + kzm + z_ends * c[n]) * u[n]
        near[pl.ds(SUB * n, SUB)] = u[n]
        near[pl.ds(PARTLY + SUB * n, SUB)] = u[n] + DT * at(Q1, n) + (below + (right - left) + side)
        left = right
    near[NEAR_C0 : NEAR_D0] = full[C0 : C0 + CELLS]
    near[NEAR_D0 : NEAR_PACK] = full[D0 : D0 + 24]


def write_hots(duct, base, flip, j, at_rows, at_lanes, at_segments):
    rows, lanes, segment = duct_lists(duct, base, flip)
    for c in range(8):
        at = pl.ds(256 * c, 256)
        at_rows[j, :, at] = as_bf16(hot(rows[c : c + 1], CELLS))
        at_lanes[j, :, at] = as_bf16(hot(lanes[c : c + 1], NZ))
    if at_segments is not None:
        at_segments[j] = as_bf16(hot(segment, 128))


def place(slab, first, turned, valid, temp0, cond, load):
    for r in range(2):
        i, at = first + r, 1 - r if turned else r
        temp0[i] = slab[pl.ds(U0 + at * NY, NY)]
        conductivity = jnp.exp(slab[pl.ds(C0 + at * NY, NY)])
        cond[i] = conductivity if valid is None else conductivity * valid
        if i < EXT - 1:
            load[i] = DT * slab[pl.ds(Q1 if at else Q0, NY)]


def prepare_own_kernel(own, at_rows, at_lanes, at_segments, temp0, load, cond):
    place(own, 4, False, None, temp0, cond, load)
    write_hots(own, D0, False, 0, at_rows, at_lanes, at_segments)


def prepare_far_kernel(far1, far2, *refs):
    at_rows, at_lanes, at_segments, temp2, temp1, kx, ky, kzp, kzm, keep, temp0, load, cond = refs[3:]
    near, far = validity()
    coefs = (kx, ky, kzp, kzm, keep)
    place(far1, 6, True, None, temp0, cond, load)
    place(far2, 8, False, far, temp0, cond, load)
    coefficients(cond, *coefs, 5, 2)
    advance(temp0, temp1, 5, 8, coefs, load, near, far)
    advance(temp1, temp2, 6, 7, coefs, load, near, far)
    write_hots(far2, D0, False, 0, at_rows, at_lanes, at_segments)


def prepare_near_kernel(near2, far_segments, at_segments):
    _, _, segment = duct_lists(near2, NEAR_D0, False)
    at_segments[0] = as_bf16(hot(segment, 128))


def forward_kernel(near2, near1, own, at_rows, at_lanes, at_segments, *refs):
    temp3, temp4, sums, temp2, temp1, *coefs, temp0, load, cond = refs[FIELDS:]
    near, far = validity()
    temp0[0] = jnp.zeros((NY, NZ), f32)
    load[1] = jnp.zeros((NY, NZ), f32)
    temp0[1] = near2[0:NY]
    for r in range(2):
        cond[r] = jnp.exp(near2[pl.ds(NEAR_C0 + r * NY, NY)]) * near
    place(near1, 2, True, near, temp0, cond, load)
    coefficients(cond, *coefs, 1, 2)
    advance(temp0, temp1, 1, 4, coefs, load, near, far)
    temp1[1] = near * (near2[PARTLY : PARTLY + NY] + coefs[0][1] * (temp0[2] - temp0[1]))
    advance(temp1, temp2, 2, 5, coefs, load, near, far)
    advance(temp2, temp3, 3, 6, coefs, load, near, far)
    advance(temp3, temp4, 4, 5, coefs, load, near, far)

    across = jnp.concatenate([temp4[4].T, temp4[5].T], axis=1)
    stack = jnp.concatenate([part.astype(bf16) for part in parts_of(across, 3)], axis=0)
    picked = jnp.zeros((NZ, 256), f32)
    for c in range(8):
        at = pl.ds(256 * c, 256)
        found = jnp.dot(stack, at_rows[0, :, at], preferred_element_type=f32)
        value = (found[2 * NZ :] + found[NZ : 2 * NZ]) + found[:NZ]
        picked = picked + value * at_lanes[0, :, at].astype(f32)
    partial = 0.5 * jnp.sum(picked, axis=0, keepdims=True)
    by_segment = lax.dot_general(
        stacked_rows(parts_of(partial, 3)),
        at_segments[0],
        (((1,), (1,)), ((), ())),
        preferred_element_type=f32,
    )
    total = jnp.sum(by_segment, axis=0, keepdims=True) - own[pl.ds(D0 + 16, 8)][2:3]
    sums[...] = jnp.broadcast_to(total, sums.shape)


def backward_kernel(
    near2, near1, far1, own_rows, own_lanes, own_segments, far_rows, far_lanes, far_segments, near2_segments,
    sums, temp0, temp1, temp2, temp3, cond, kx, ky, kzp, kzm, keep, grad, seg,
    costate4, costate3, costate2, costate1, acc, weights, near_rows, near_lanes, near_segments,
):
    g, core, _, _ = position()
    near, far = validity()
    temp, costate = (temp0, temp1, temp2, temp3), (costate4, costate3, costate2, costate1)
    resid = jnp.sum(sums[...], axis=0, keepdims=True)
    shift = lax.rem(128 - seg.shape[1] * g, 128)
    seg[...] = pltpu.roll(jnp.broadcast_to(resid, (8, 128)), shift, 1)[0:1, 0 : seg.shape[1]]
    stack = stacked_rows(parts_of(0.5 * resid, 3))
    write_hots(near2, NEAR_D0, False, 0, near_rows, near_lanes, None)
    near_segments[0] = near2_segments[0]
    write_hots(near1, D0, True, 1, near_rows, near_lanes, near_segments)
    write_hots(far1, D0, True, 2, near_rows, near_lanes, near_segments)
    own, fars = (own_rows, own_lanes, own_segments), (far_rows, far_lanes, far_segments)
    nears = (near_rows, near_lanes, near_segments)
    places = ((nears, 0, near), (nears, 1, near), (own, 0, 1.0), (nears, 2, 1.0), (fars, 0, far))
    for j, ((at_rows, at_lanes, at_segments), n, valid) in enumerate(places):
        source = jnp.dot(stack, at_segments[n], preferred_element_type=f32)
        source = jnp.sum(source, axis=0, keepdims=True) * valid
        upper, lower = (part.astype(bf16) for part in parts_of(source, 2))
        for c in range(8):
            at = pl.ds(256 * c, 256)
            weights[j, 0:NZ, at] = at_lanes[n, :, at] * upper
            weights[j, NZ : 2 * NZ, at] = at_lanes[n, :, at] * lower
        out = lax.dot_general(
            weights[j], at_rows[n], (((1,), (1,)), ((), ())), preferred_element_type=f32
        )
        out = (out[:NZ] + out[NZ:]).T
        costate4[2 * j] = out[:NY]
        costate4[2 * j + 1] = out[NY:]

    coefs = (kx, ky, kzp, kzm, keep)
    for k in range(STEPS - 1):
        advance(costate[k], costate[k + 1], k + 1, 8 - k, coefs, None, near, far)
    s, z = coordinates()
    share = grad.shape[2]

    def sensitivity(i, carry):
        at = (i - 4) ^ core

        def products(n):
            across = jnp.zeros((SUB, NZ), f32)
            right, side, own = across, across, across
            for k in range(STEPS):
                u, a = temp[k], costate[STEPS - 1 - k]
                uc, ac = u[i, part(n)], a[i, part(n)]
                across += (uc - u[i + 1, part(n)]) * (ac - a[i + 1, part(n)])
                across += (uc - u[i - 1, part(n)]) * (ac - a[i - 1, part(n)])
                if n < BLOCKS - 1:
                    ur, ar = u[i, part(n + 1)], a[i, part(n + 1)]
                else:
                    ur = jnp.where(s < SUB - 1, pltpu.roll(u[i, part(0)], SUB - 1, 0), 0.0)
                    ar = jnp.where(s < SUB - 1, pltpu.roll(a[i, part(0)], SUB - 1, 0), 0.0)
                right += (ur - uc) * (ar - ac)
                us = jnp.where(z < NZ - 1, pltpu.roll(uc, NZ - 1, 1), 0.0)
                az = jnp.where(z < NZ - 1, pltpu.roll(ac, NZ - 1, 1), 0.0)
                side += (us - uc) * (az - ac)
                own += uc * ac
            side += jnp.where(z > 0, pltpu.roll(side, 1, 1), own)
            return across + 0.5 * side, right, own

        last, last_right, _ = products(BLOCKS - 1)
        left = None
        for n in range(BLOCKS):
            total, right, own = products(n) if n < BLOCKS - 1 else (last, last_right, None)
            if n == 0:
                left = jnp.where(s > 0, pltpu.roll(last_right, 1, 0), own)
            acc[pl.ds(n, SUB, stride=BLOCKS)] = (-WX) * cond[i, part(n)] * (total + (right + left))
            left = right
        for n in range(NY // share):
            grad[n, at] = acc[pl.ds(n * share, share)]
        return carry

    lax.fori_loop(4, 6, sensitivity, 0)


def field(*lead):
    return (*lead, NY, NZ)


def in_hbm(values):
    return pltpu.with_memory_space_constraint(values, pltpu.HBM)


def local(log_cond, opening_increase, heat_load, measured, duct_cells, duct_segment):
    grid = lax.axis_size("grid")
    tests = lax.axis_size("tests")
    vmem = pl.BlockSpec(memory_space=pltpu.VMEM)
    params = pltpu.CompilerParams(vmem_limit_bytes=24 * 1024 * 1024)
    pack = pl.pallas_call(
        pack_kernel,
        out_shape=pltpu.VMEM((PACK, NZ), f32),
        in_specs=[pl.BlockSpec(memory_space=pltpu.HBM)] * 6,
        out_specs=vmem,
        scratch_shapes=[
            pltpu.VMEM(field(6), f32),
            pltpu.VMEM((8, 256), jnp.int32),
            pltpu.VMEM((1, 256), jnp.int32),
            pltpu.VMEM(measured.shape, f32),
            pltpu.SemaphoreType.DMA((9,)),
        ],
        compiler_params=params,
        name="pack",
    )(*map(in_hbm, (log_cond, opening_increase, heat_load, duct_cells.T, duct_segment.T, measured)))
    pack_near = pl.pallas_call(
        pack_near_kernel,
        out_shape=pltpu.VMEM((NEAR_PACK, NZ), f32),
        in_specs=[vmem],
        out_specs=vmem,
        compiler_params=params,
        name="pack_near",
    )(pack)
    to_far = [(s, s - 2) for s in range(2, grid, 2)] + [(s, s + 2) for s in range(1, grid - 2, 2)]
    to_near = [(s, s + 2) for s in range(0, grid - 2, 2)] + [(s, s - 2) for s in range(3, grid, 2)]
    swap = [(s, s ^ 1) for s in range(grid)]
    far2 = lax.ppermute(pack, "grid", to_far)
    far1 = lax.ppermute(pack, "grid", swap)

    def hots(slabs):
        return (
            pltpu.VMEM((slabs, CELLS, 2048), bf16),
            pltpu.VMEM((slabs, NZ, 2048), bf16),
            pltpu.VMEM((slabs, 128, 256), bf16),
        )

    field_shape = pltpu.VMEM(field(EXT), f32)

    def stage(kernel, out_shape, name, *operands, fields=(), cost=COST_ESTIMATE):
        shapes = (*out_shape, *[field_shape] * len(fields))
        return pl.pallas_call(
            kernel,
            out_shape=shapes,
            in_specs=[vmem] * (len(operands) + len(fields)),
            out_specs=(vmem,) * len(shapes),
            input_output_aliases={len(operands) + n: len(out_shape) + n for n in range(len(fields))},
            compiler_params=params,
            cost_estimate=pl.CostEstimate(flops=cost, bytes_accessed=4_000_000, transcendentals=0),
            name=name,
        )(*operands, *fields)

    results = stage(prepare_own_kernel, (*hots(1), *[field_shape] * 3), "prepare_own", pack)
    own_hots, fields = results[:3], results[3:]
    pack_near, own_hots = lax.optimization_barrier((pack_near, own_hots))
    near2 = lax.ppermute(pack_near, "grid", to_near)
    far2, own_hots = lax.optimization_barrier((far2, own_hots))
    near1 = lax.ppermute(far2, "grid", swap)
    results = stage(
        prepare_far_kernel, (*hots(1), *[field_shape] * 7), "prepare_far", far1, far2, fields=fields
    )
    far_hots, fields = results[:3], results[3:]
    near_hots = stage(prepare_near_kernel, hots(1)[2:], "prepare_near", near2, far_hots[2])
    near2, near_hots, far_hots = lax.optimization_barrier((near2, near_hots, far_hots))
    out_shape = (field_shape, field_shape, pltpu.VMEM((grid, 128), f32))
    temp3, _, sums, temp2, temp1, *coefs, temp0, _, cond = stage(
        forward_kernel, out_shape, "forward", near2, near1, pack, *own_hots, fields=fields
    )
    sums = lax.all_to_all(sums, "grid", split_axis=0, concat_axis=0, tiled=True)
    share = NY // tests
    grad, seg = pl.pallas_call(
        backward_kernel,
        out_shape=(
            pltpu.VMEM((tests, 2, share, NZ), f32),
            jax.ShapeDtypeStruct(measured.shape, f32),
        ),
        in_specs=[vmem] * 21,
        out_specs=(vmem, vmem),
        scratch_shapes=[
            *[pltpu.VMEM(field(EXT), f32)] * STEPS,
            pltpu.VMEM((NY, NZ), f32),
            pltpu.VMEM((5, CELLS, 2048), bf16),
            *hots(3),
        ],
        compiler_params=params,
        name="backward",
    )(near2, near1, far1, *own_hots, *far_hots, *near_hots, sums, temp0, temp1, temp2, temp3, cond, *coefs)
    grad = lax.all_to_all(grad, "tests", split_axis=0, concat_axis=0, tiled=True)
    return jnp.sum(grad, axis=0), seg


def solution(mesh):
    in_specs = (
        P("grid", None, None),
        P("tests", "grid", None, None),
        P("tests", "grid", None, None),
        P("tests", "grid"),
        P("grid", None),
        P("grid", None),
    )
    out_specs = (P("grid", "tests", None), P("tests", "grid"))
    return jax.shard_map(local, mesh=mesh, in_specs=in_specs, out_specs=out_specs, check_vma=False)
```
